256 devices in a mesh: ctx: 64 (over y, z, x_lo), head: 4 (over x_hi, core).
Axes of the slice: x: 4 (x_hi: 2, x_lo: 2; x = x_hi * 2 + x_lo), y: 4, z: 8, core: 2. Of those that a mesh axis runs over, the one named last changes fastest.
Arguments:
- queries: bfloat16 [128, 8192], P('ctx', 'head'), may hold values from -32 to 32
- keys: bfloat16 [131072, 1024], P('ctx', 'head'), may hold values from -16 to 16
- values: bfloat16 [131072, 1024], P('ctx', 'head'), may hold values from -20 to 20
- norm_gain: bfloat16 [8192], P('head'), may hold values from 0.099609375 to 1.8984375
- adapter: bfloat16 [1024, 8192], P('ctx', 'head'), may hold values from -0.0625 to 0.0625
- source_row: int32 [128], replicated, may hold values from 0 to 127, each once
- cotangent: bfloat16 [128, 1024], P('ctx'), may hold values from -16 to 16
Outputs:
- student_out: float32 [128, 1024], P('ctx')
- adapter_grad: float32 [1024, 8192], P('ctx', 'head')
The draws below stay inside these ranges and needn't reach their ends.
Inputs may be any that keep to these rules, and one draw needn't show every extreme that they name: `source_row`: each response row is read by exactly one student token.
All inputs are finite; a program needn't handle non-finite values.
Results may differ from the reference program's by a relative error of at most 0.015.
Values may be sent and summed in bfloat16 or wider, within the bound.
A program may use at most 192 MiB of HBM per device.

```python
import jax
import jax.numpy as jnp
from jax import lax

H = 64
KVH = 8
HD = 128
DS = 1024
CTX = 131072
R = 128


def draw_queries(key, part):
    key = jax.random.fold_in(key, 1)
    base = jax.random.truncated_normal(key, -6.0, 6.0, (R, H * HD), jnp.float32)
    return base.astype(jnp.bfloat16)


def draw_keys(key, part):
    key = jax.random.fold_in(key, 2)
    base = 2.5 * jax.random.truncated_normal(key, -6.0, 6.0, (CTX, KVH * HD), jnp.float32)
    return base.astype(jnp.bfloat16)


def draw_values(key, part):
    key = jax.random.fold_in(key, 3)
    head_pos = (jnp.arange(KVH * HD) // HD).astype(jnp.float32) / max(KVH - 1, 1)
    lifted = 3.0 ** head_pos
    base = jax.random.truncated_normal(key, -6.0, 6.0, (CTX, KVH * HD), jnp.float32) * lifted[None, :]
    return base.astype(jnp.bfloat16)


def spiked(result, own_key, source, target, shards_of, factor):
    owner, partner = [(jnp.arange(result.shape[axis_at]) // (result.shape[axis_at] // shards_of)).reshape([-1 if axis == axis_at else 1 for axis in range(result.ndim)]) for axis_at in (source, target)]
    chosen = jax.random.permutation(own_key, shards_of)[partner]
    strong = (owner == chosen) | (owner == (partner + shards_of // 2) % shards_of)
    return jnp.where(strong, factor * result, result)


def steps_of(stream_key, shape, shards, smallest, top_value):
    gain = 1.0
    for axis_at, parts in shards:
        steps = jax.random.uniform(jax.random.fold_in(jax.random.fold_in(stream_key, 6), axis_at), (parts,), jnp.float32, smallest / len(shards), top_value / len(shards))
        gain = gain * jnp.repeat(jnp.exp(steps), shape[axis_at] // parts).reshape((-1,) + (1,) * (len(shape) - 1 - axis_at))
    return gain


def bell_draw(stream_key, extent, width, bound, shards=(), kind=jnp.bfloat16):
    result = width * jax.random.normal(stream_key, extent, jnp.float32)
    if shards:
        result = result * steps_of(stream_key, extent, shards, -0.22, 0.18)
    return jnp.clip(result, -bound, bound).astype(kind)


def gaussian_with(rng, extent, deviation, bound, cuts, heavy, held_as=jnp.bfloat16):
    entries = deviation * jax.random.normal(rng, extent, jnp.float32)
    if cuts:
        entries = entries * steps_of(rng, extent, cuts, -0.22, 0.18)
    return jnp.clip(spiked(entries, jax.random.fold_in(rng, 3), *heavy), -bound, bound).astype(held_as)


def setup_inputs(seed: int = 0) -> dict:
    streams_of = jax.random.split(jax.random.key(seed), 8)
    return {
        "queries": draw_queries(jax.random.fold_in(streams_of[7], 71), 0),
        "keys": draw_keys(jax.random.fold_in(streams_of[7], 71), 0),
        "values": draw_values(jax.random.fold_in(streams_of[7], 71), 0),
        "norm_gain": jnp.clip(1.0 + 0.18 * jax.random.normal(streams_of[3], (H * HD,), jnp.float32), 0.099609375, 1.8984375).astype(jnp.bfloat16),
        "adapter": bell_draw(streams_of[4], (DS, H * HD), (H * HD) ** -0.5, 0.0625, ((0, 64), (1, 4))),
        "source_row": jax.random.permutation(streams_of[5], R).astype(jnp.int32),
        "cotangent": gaussian_with(streams_of[6], (R, DS), 1.0, 16.0, ((0, 64),), (0, 1, 64, 4.0)),
    }


def head_attention(query_rows, key_rows, value_rows):
    key_block = min(4096, CTX)
    row_count = query_rows.shape[0]

    def step(carry, block_id):
        outputs, maxima, totals = carry
        key_part = lax.dynamic_slice_in_dim(key_rows, block_id * key_block, key_block, 0)
        value_part = lax.dynamic_slice_in_dim(value_rows, block_id * key_block, key_block, 0)
        scores = jnp.dot(query_rows, key_part.T, preferred_element_type=jnp.float32) * HD ** (-0.5)
        new_max = jnp.maximum(maxima, lax.optimization_barrier(jnp.max(scores, axis=1)))
        weights = jnp.exp(scores - new_max[:, None])
        shrink = jnp.exp(maxima - new_max)
        totals = totals * shrink + lax.optimization_barrier(jnp.sum(weights, axis=1))
        outputs = outputs * shrink[:, None] + jnp.dot(weights.astype(jnp.bfloat16), value_part, preferred_element_type=jnp.float32)
        return ((outputs, new_max, totals), None)
    start = (jnp.zeros((row_count, HD), jnp.float32), jnp.full((row_count,), -1e+30, jnp.float32), jnp.zeros((row_count,), jnp.float32))
    block_ids = jnp.arange(CTX // key_block, dtype=jnp.int32)
    (outputs, maxima, totals), _ = lax.scan(step, start, block_ids)
    return (outputs / totals[:, None]).astype(jnp.bfloat16)

def reference(queries, keys, values, norm_gain, adapter, source_row, cotangent):
    group = H // KVH
    query_heads = queries.reshape(R, KVH, group, HD).transpose(1, 0, 2, 3).reshape(KVH, R * group, HD)
    key_heads = keys.reshape(CTX, KVH, HD).transpose(1, 0, 2)
    value_heads = values.reshape(CTX, KVH, HD).transpose(1, 0, 2)

    def one_head(inputs):
        return head_attention(inputs[0], inputs[1], inputs[2])
    hidden = lax.map(one_head, (query_heads, key_heads, value_heads))
    hidden = hidden.reshape(KVH, R, group, HD).transpose(1, 0, 2, 3).reshape(R, H * HD)
    rows = jnp.take(hidden, source_row, axis=0)
    widened = rows.astype(jnp.float32)
    power = lax.optimization_barrier(jnp.sum(widened * widened, axis=1))
    scale = lax.rsqrt(power / (H * HD) + 1e-05)
    gained = (widened * norm_gain.astype(jnp.float32)[None, :]).astype(jnp.bfloat16)
    pre = scale[:, None] * jnp.dot(gained, adapter.T, preferred_element_type=jnp.float32)
    student_out = jax.nn.silu(pre)
    sigmoid_val = jax.nn.sigmoid(pre)
    slope = (cotangent.astype(jnp.float32) * sigmoid_val * (1.0 + pre * (1.0 - sigmoid_val)) * scale[:, None]).astype(jnp.bfloat16)
    adapter_grad = jnp.dot(slope.T, gained, preferred_element_type=jnp.float32) * R ** (-0.5)
    return (student_out, adapter_grad)
```

```python
import functools

import jax
import jax.numpy as jnp
from jax import lax
from jax.experimental import pallas as pl
from jax.experimental.pallas import tpu as pltpu
from jax.sharding import PartitionSpec as P

H = 64
HD = 128
GROUP = 8
LANES = 128
LOG2E = 1.4426950408889634
YN, ZN, XN = 4, 8, 2

F32 = jnp.float32
BF16 = jnp.bfloat16
MESH = pl.DeviceIdType.MESH


def iota(shape, axis):
    return lax.broadcasted_iota(jnp.int32, shape, axis)


def nn(left, right):
    return lax.dot_general(left, right, (((1,), (0,)), ((), ())), preferred_element_type=F32)


def div(a, n):
    return a // n if isinstance(a, int) else a >> (n.bit_length() - 1)


def mod(a, n):
    return a % n if isinstance(a, int) else a & (n - 1)


def regroup(outer, zn):
    size = outer * zn * 2
    row, col = iota((size, 1), 0), iota((size, size), 1)
    head, rest = div(row, 2 * zn), mod(row, 2 * zn)
    return (col == div(rest, 2) * (2 * outer) + head * 2 + mod(rest, 2)).astype(F32).astype(BF16)


def row_of(position, sizes):
    yn, zn, xn = sizes
    pair, block = div(position, 2), div(position, 2 * zn)
    ctx = (div(block, xn) * zn + mod(pair, zn)) * xn + mod(block, xn)
    return 2 * ctx + mod(position, 2)


def split3(value):
    high = value.astype(BF16)
    rest = value - high.astype(F32)
    middle = rest.astype(BF16)
    return high, middle, (rest - middle.astype(F32)).astype(BF16)


def kernel(sizes, heads, eps_div, q_hbm, k_hbm, v_hbm, gain_hbm, ad_hbm, src_hbm, cot_hbm,
           stu_ref, grad_ref,
           q_ref, gain_ref, src_ref, cot_ref, kbuf, k_t, vaug, qall, osend, orecv, zsend, zrecv,
           hz, hall, gall, mpre, squares, hx, s_even, s_odd, regroup_h, cz, cg, call, cot_t, mpre_t, st1s, st1r,
           adp, ad_t,
           loc_sem, zq_s, zq_r, q2_s, q2_r, zc_s, zc_r, c2_s, c2_r, o_s, o_r,
           zr_s, zr_r, hz_s, hz_r, h2_s, h2_r, hx_s, hx_r, s1_s, s1_r, za_s, za_r):
    sbuf = (s_even, s_odd)
    yn, zn, xn = sizes
    nb = yn * xn
    tb = 2 * zn
    rows = nb * tb
    kvl = k_hbm.shape[1] // HD
    nh = kvl * GROUP
    kr = GROUP * 2
    cpd = ad_hbm.shape[0]
    per_group = LANES // cpd
    aw = zn * xn * cpd
    groups = cot_hbm.shape[1] // LANES

    ctx = lax.axis_index("ctx")
    hd = lax.axis_index("head")
    y = div(ctx, zn * xn)
    z = mod(div(ctx, xn), zn)
    x = mod(ctx, xn)
    b = y * xn + x

    def at(y_, z_, x_):
        return ((y_ * zn + z_) * xn + x_, hd)

    def z_plus(d):
        return mod(z + d, zn)

    ring = sorted(range(1, zn), key=lambda d: -min(d, zn - d))

    def z_dev(d):
        return at(y, z_plus(d), x)

    def steps(i):
        far, turn = div(i, yn), mod(i, yn)
        if isinstance(i, int):
            near = (0, 1, 3, 2)[turn] if yn == 4 else turn
            return (near if far == 0 else (2, 1, 3, 0)[turn] if yn == 4 else yn - 1 - turn), far
        if yn == 4:
            first = jnp.where(turn == 2, 3, jnp.where(turn == 3, 2, turn))
            second = jnp.where(turn == 0, 2, jnp.where(turn == 1, 1, jnp.where(turn == 2, 3, 0)))
        else:
            first, second = turn, yn - 1 - turn
        return jnp.where(far == 0, first, second), far

    def plus(i):
        dy, dx = steps(i)
        return mod(y + dy, yn), mod(x + dx, xn)

    def minus(i):
        dy, dx = steps(i)
        return mod(y + yn - dy, yn), mod(x + xn - dx, xn)

    def plus_dev(i):
        py, px = plus(i)
        return at(py, z, px)

    def minus_dev(i):
        py, px = minus(i)
        return at(py, z, px)

    def rcopy(src, dst, ssem, rsem, dev):
        return pltpu.make_async_remote_copy(
            src_ref=src, dst_ref=dst, send_sem=ssem, recv_sem=rsem, device_id=dev, device_id_type=MESH
        )

    q_load = pltpu.make_async_copy(q_hbm, q_ref, loc_sem.at[0])
    cot_load = pltpu.make_async_copy(cot_hbm, cot_ref, loc_sem.at[1])
    k_load = pltpu.make_async_copy(k_hbm, kbuf, loc_sem.at[2])
    own_ad = pl.ds(pl.multiple_of((z * xn + x) * cpd, cpd), cpd)
    ad_load = pltpu.make_async_copy(ad_hbm, adp.at[own_ad], loc_sem.at[3])
    late_loads = [
        pltpu.make_async_copy(gain_hbm, gain_ref, loc_sem.at[4]),
        pltpu.make_async_copy(src_hbm, src_ref, loc_sem.at[5]),
    ]
    for k in range(kvl):
        late_loads.append(
            pltpu.make_async_copy(
                v_hbm.at[:, k * HD : (k + 1) * HD], vaug.at[k, :, 0:HD], loc_sem.at[6 + k]
            )
        )
    for load in [q_load, cot_load, k_load, ad_load] + late_loads:
        load.start()

    barrier = pltpu.get_barrier_semaphore()
    partners = (
        [z_dev(d) for d in range(1, zn)]
        + [plus_dev(i) for i in range(1, nb)]
        + [(ctx, mod(hd + e, heads)) for e in range(1, heads)]
    )
    for dev in partners:
        pl.semaphore_signal(barrier, inc=1, device_id=dev, device_id_type=MESH)

    q_load.wait()
    qf = q_ref[...].astype(F32)
    for k in range(kvl):
        qall[k * nb, pl.ds(z, 1)] = jnp.concatenate(
            [qf[:, (k * GROUP + h) * HD : (k * GROUP + h + 1) * HD] for h in range(GROUP)], axis=0
        ).astype(BF16)[None]
    cot_load.wait()
    cf = cot_ref[...].astype(F32)
    cz[pl.ds(z, 1)] = jnp.concatenate(
        [cf[:, g * LANES : (g + 1) * LANES] for g in range(groups)], axis=0
    ).astype(BF16)[None]
    pl.semaphore_wait(barrier, len(partners))

    def z_group(make):
        copies = {d: make(d) for d in ring}
        for copy in copies.values():
            copy.start()
        return copies

    def received(copies):
        for copy in copies.values():
            copy.wait_recv()

    def sent(*groups_of_copies):
        for copies in groups_of_copies:
            for copy in copies.values():
                copy.wait_send()

    zq = [
        z_group(
            lambda d, k=k: rcopy(
                qall.at[k * nb, z], qall.at[k * nb, z], zq_s.at[k * zn + d], zq_r.at[k * zn + d], z_dev(d)
            )
        )
        for k in range(kvl)
    ]
    zc = z_group(lambda d: rcopy(cz.at[z], cz.at[z], zc_s.at[d], zc_r.at[d], z_dev(d)))

    k_load.wait()
    for k in range(kvl):
        k_t[k] = kbuf[:, k * HD : (k + 1) * HD].astype(F32).T.astype(BF16)
    for k in range(kvl):
        vaug[k, :, HD : 2 * HD] = jnp.ones((vaug.shape[1], HD), BF16)

    def q_copy(j, i):
        return rcopy(qall.at[j - i], qall.at[j], q2_s.at[j], q2_r.at[j], plus_dev(i))

    for k in range(kvl):
        received(zq[k])
        for i in range(1, nb):
            q_copy(k * nb + i, i).start()

    for d in range(zn):
        for e in range(1, xn):
            other = pl.multiple_of((d * xn + mod(x + e, xn)) * cpd, cpd)
            adp[pl.ds(other, cpd), :] = jnp.zeros((cpd, nh * HD), BF16)
    st1s[...] = jnp.zeros_like(st1s)
    ad_load.wait()
    za = z_group(lambda d: rcopy(adp.at[own_ad], adp.at[own_ad], za_s.at[d], za_r.at[d], z_dev(d)))
    for load in late_loads:
        load.wait()

    factor = (HD ** -0.5) * LOG2E
    qrows = zn * kr
    eye = iota((qrows, LANES), 0) == iota((qrows, LANES), 1)

    def stat_tile(row):
        high, middle, low = split3(row)
        line = iota((kr, LANES), 0)
        tile = jnp.where(line == 0, high.astype(F32), jnp.where(line == 1, middle.astype(F32), low.astype(F32)))
        return jnp.where(line < 3, tile, 0.0).astype(BF16)

    def stat_row(tile):
        wide = tile.astype(F32)
        return wide[0:1, :] + wide[1:2, :] + wide[2:3, :]

    def score(j, buf):
        buf[...] = nn(qall[j].reshape(qrows, HD), k_t[div(j, nb)])

    def weigh(j, k, buf):
        m = jnp.max(buf[...], axis=1, keepdims=True)
        p = jnp.exp2((buf[...] - m) * factor).astype(BF16)
        oa = nn(p, vaug[k])
        total = oa[:, HD : 2 * HD]
        o = oa[:, 0:HD] / total
        osend[j, 0:zn] = o.astype(BF16).reshape(zn, kr, HD)
        lse = m * factor + jnp.log2(total)
        osend[j, zn] = stat_tile(jnp.sum(jnp.where(eye, lse, 0.0), axis=0, keepdims=True))

    def o_copy(j, i):
        return rcopy(osend.at[j], orecv.at[j], o_s.at[j], o_r.at[j], minus_dev(i))

    def attend(k):
        def body(t, carry):
            first, second, third = 2 * t, 2 * t + 1, jnp.minimum(2 * t + 2, kvl * nb - 1)
            q_copy(second, mod(second, nb)).wait_recv()
            score(second, sbuf[1])
            weigh(first, k, sbuf[0])

            @pl.when(mod(first, nb) > 0)
            def _():
                o_copy(first, mod(first, nb)).start()

            @pl.when(mod(2 * t + 2, nb) > 0)
            def _():
                q_copy(third, mod(third, nb)).wait_recv()

            score(third, sbuf[0])
            weigh(second, k, sbuf[1])
            o_copy(second, mod(second, nb)).start()
            return carry

        return body

    def combine(k):
        for i in range(1, nb):
            o_copy(k * nb + i, i).wait_recv()
        parts = [(osend if i == 0 else orecv).at[k * nb + i] for i in range(nb)]
        stats = [stat_row(part[zn]) for part in parts]
        top = functools.reduce(jnp.maximum, stats)
        weights = [jnp.exp2(st - top) for st in stats]
        weight_sum = functools.reduce(jnp.add, weights)
        inverse = 1.0 / weight_sum
        acc = jnp.zeros((qrows, HD), F32)
        for i in range(nb):
            share = jnp.where(eye, weights[i] * inverse, 0.0)[:, 0:qrows].astype(BF16)
            acc = acc + nn(share, parts[i][0:zn].reshape(qrows, HD))
        zsend[k, :, 0:kr, :] = acc.astype(BF16).reshape(zn, kr, HD)
        tile = stat_tile(top + jnp.log2(weight_sum))
        for d in range(zn):
            zsend[k, d, kr : 2 * kr, :] = tile
        return z_group(
            lambda d: rcopy(
                zsend.at[k, z_plus(d)], zrecv.at[k, d], zr_s.at[k * zn + d], zr_r.at[k * zn + d], z_dev(d)
            )
        )

    mine = iota((kr, LANES), 1) == iota((kr, LANES), 0) + z * kr

    def settle(k, copies):
        received(copies)
        parts = [zsend[k, z]] + [zrecv[k, d] for d in range(1, zn)]
        stats = [stat_row(part[kr : 2 * kr, :]) for part in parts]
        top = functools.reduce(jnp.maximum, stats)
        weights = [jnp.exp2(st - top) for st in stats]
        inverse = 1.0 / functools.reduce(jnp.add, weights)
        acc = jnp.zeros((kr, HD), F32)
        for d in range(zn):
            column = jnp.sum(jnp.where(mine, weights[d] * inverse, 0.0), axis=1, keepdims=True)
            acc = acc + column * parts[d][0:kr, :].astype(F32)
        hz[k, pl.ds(z, 1)] = acc.astype(BF16)[None]
        return z_group(
            lambda d: rcopy(hz.at[k, z], hz.at[k, z], hz_s.at[k * zn + d], hz_r.at[k * zn + d], z_dev(d))
        )

    def spread(k, copies):
        received(copies)
        pieces = nn(regroup_h[...], hz[k].reshape(zn * kr, HD)).astype(BF16)
        for h in range(GROUP):
            hall[k, pl.ds(b, 1), :, h * HD : (h + 1) * HD] = pieces[h * tb : (h + 1) * tb, :][None]
        copies = {
            i: rcopy(hall.at[k, b], hall.at[k, b], h2_s.at[k * nb + i], h2_r.at[k * nb + i], plus_dev(i))
            for i in range(1, nb)
        }
        for copy in copies.values():
            copy.start()
        return copies

    def project(k, copies):
        gain = gain_ref[...].astype(F32)
        for i in range(nb):
            if i > 0:
                copies[i].wait_recv()
            my, mx = minus(i)
            there = my * xn + mx
            hidden = hall[k, there].astype(F32)
            lines = pl.ds(pl.multiple_of(there * tb, tb), tb)
            partial = jnp.zeros((tb, HD), F32)
            for h in range(GROUP):
                piece = hidden[:, h * HD : (h + 1) * HD]
                partial = partial + piece * piece
                head = k * GROUP + h
                gall[lines, head * HD : (head + 1) * HD] = (piece * gain[head : head + 1, :]).astype(BF16)
            squares[lines, :] = partial if k == 0 else squares[lines, :] + partial
        width = GROUP * HD
        part = nn(gall[:, k * width : (k + 1) * width], ad_t[k * width : (k + 1) * width, :])
        mpre[...] = part if k == 0 else mpre[...] + part

    def turn_adapter(k):
        for h in range(k * GROUP, (k + 1) * GROUP):
            for first in range(0, aw, LANES):
                ad_t[h * HD : (h + 1) * HD, first : first + LANES] = (
                    adp[first : first + LANES, h * HD : (h + 1) * HD].astype(F32).T.astype(BF16)
                )

    score(0, sbuf[0])
    half = nb // 2
    pause = 2 * half - half // 4
    lax.fori_loop(0, half, attend(0), 0)
    lax.fori_loop(half, pause, attend(1), 0)
    z0 = combine(0)
    if pause < 2 * half:
        lax.fori_loop(pause, 2 * half, attend(1), 0)

    regroup_h[...] = regroup(GROUP, zn)
    received(zc)
    pieces = nn(regroup(groups, zn), cz[...].reshape(zn * groups * 2, LANES))
    cg[...] = pieces.astype(BF16).reshape(groups, tb, LANES)
    my_group = div(ctx, per_group)
    c2 = {}
    for i in range(1, nb):
        py, px = plus(i)
        there = div((py * zn + z) * xn + px, per_group)
        c2[i] = rcopy(cg.at[there], call.at[b], c2_s.at[i], c2_r.at[i], at(py, z, px))
        c2[i].start()
    call[pl.ds(b, 1)] = cg[pl.ds(my_group, 1)]

    h0 = settle(0, z0)
    sent(*zq, zc)
    z1 = combine(1)
    received(za)
    turn_adapter(0)
    g0 = spread(0, h0)

    sel = iota((rows, rows), 1) == row_of(iota((rows, 1), 0), sizes)
    wanted = jnp.sum(
        jnp.where(sel, jnp.broadcast_to(src_ref[...].astype(F32), (rows, rows)), 0.0),
        axis=1, keepdims=True,
    )
    pick = (wanted == row_of(iota((1, rows), 1), sizes).astype(F32)).astype(F32)
    received(c2)
    cot_rows = nn(pick.T.astype(BF16), call[...].reshape(rows, LANES))
    cot_t[...] = cot_rows.T
    token = iota((nb * 2, 1), 0)
    block = div(token, 2)
    token = 2 * ((div(block, xn) * zn + z) * xn + mod(block, xn)) + mod(token, 2)
    wanted = jnp.sum(
        jnp.where(iota((nb * 2, rows), 1) == token, src_ref[...].astype(F32), 0.0), axis=1, keepdims=True
    )
    pick = (wanted == row_of(iota((1, rows), 1), sizes).astype(F32)).astype(F32)

    h1 = settle(1, z1)
    turn_adapter(1)
    sent(za, z0, z1, c2)
    for j in range(kvl * nb):
        if j % nb:
            q_copy(j, j % nb).wait_send()
            o_copy(j, j % nb).wait_send()
    g1 = spread(1, h1)
    project(0, g0)
    sent(h0, h1, g0)
    project(1, g1)

    for first in range(0, aw, LANES):
        mpre_t[first : first + LANES, :] = mpre[:, first : first + LANES].T
    hx[pl.ds(hd, 1), 0:cpd, 0:rows] = mpre_t[own_ad, :][None]
    power = jnp.sum(squares[...].T, axis=0, keepdims=True)
    hx[pl.ds(hd, 1), cpd : cpd + 8, 0:rows] = jnp.broadcast_to(power, (8, rows))[None]
    one_hot = pick.astype(BF16)
    chosen = functools.reduce(jnp.add, [nn(one_hot, term) for term in split3(mpre[...])])
    base = cpd + 8
    for j in range(aw // LANES):
        hx[pl.ds(hd, 1), base + j * 2 * nb : base + (j + 1) * 2 * nb, :] = chosen[
            :, j * LANES : (j + 1) * LANES
        ][None]
    hxc = {}
    for e in range(1, heads):
        hxc[e] = rcopy(hx.at[hd], hx.at[hd], hx_s.at[e], hx_r.at[e], (ctx, mod(hd + e, heads)))
        hxc[e].start()
    sent(g1)
    received(hxc)
    summed = hx[0]
    for e in range(1, heads):
        summed = summed + hx[e]
    scale = lax.rsqrt(summed[cpd : cpd + 1, 0:rows] / eps_div + 1e-05)

    token_scale = jnp.sum(pick * scale, axis=1, keepdims=True)
    for j in range(aw // LANES):
        pre = token_scale * summed[base + j * 2 * nb : base + (j + 1) * 2 * nb, :]
        out = pre / (1.0 + jnp.exp(-pre))
        for d in range(nb):
            st1s[d, 0:2, j * LANES : (j + 1) * LANES] = out[2 * d : 2 * d + 2, :]
    s1 = {}
    for i in range(1, nb):
        py, px = plus(i)
        s1[i] = rcopy(st1s.at[py * xn + px], st1r.at[b], s1_s.at[i], s1_r.at[i], at(py, z, px))
        s1[i].start()
    st1r[pl.ds(b, 1)] = st1s[pl.ds(b, 1)]
    sent(hxc)

    pre = scale * summed[0:cpd, 0:rows]
    sig = 1.0 / (1.0 + jnp.exp(-pre))
    own = pl.multiple_of(mod(ctx, per_group) * cpd, cpd)
    slope = (cot_t[pl.ds(own, cpd), :] * sig * (1.0 + pre * (1.0 - sig)) * scale).astype(BF16)
    grad_ref[...] = nn(slope, gall[...]) * (rows ** -0.5)

    sent(s1)
    received(s1)
    for py in range(yn):
        tile = st1r[py * xn]
        for px in range(1, xn):
            tile = tile + st1r[py * xn + px]
        stu_ref[:, py * aw : (py + 1) * aw] = tile[0:2, :]


def local(sizes, heads, queries, keys, values, norm_gain, adapter, source_row, cotangent):
    yn, zn, xn = sizes
    nb = yn * xn
    tb = 2 * zn
    rows = nb * tb
    positions, kvw = keys.shape
    kvl = kvw // HD
    nh = kvl * GROUP
    nf = nh * HD
    kr = GROUP * 2
    cpd = adapter.shape[0]
    aw = zn * xn * cpd
    groups = cotangent.shape[1] // LANES
    vm = pltpu.VMEM
    dma = pltpu.SemaphoreType.DMA
    scratch = [
        vm(queries.shape, BF16),
        vm((nh, HD), BF16),
        vm((1, rows), jnp.int32),
        vm(cotangent.shape, BF16),
        vm((positions, kvw), BF16),
        vm((kvl, HD, positions), BF16),
        vm((kvl, positions, 2 * HD), BF16),
        vm((kvl * nb, zn, kr, HD), BF16),
        vm((kvl * nb, zn + 1, kr, HD), BF16),
        vm((kvl * nb, zn + 1, kr, HD), BF16),
        vm((kvl, zn, 2 * kr, HD), BF16),
        vm((kvl, zn, 2 * kr, HD), BF16),
        vm((kvl, zn, kr, HD), BF16),
        vm((kvl, nb, tb, GROUP * HD), BF16),
        vm((rows, nf), BF16),
        vm((rows, aw), F32),
        vm((rows, HD), F32),
        vm((heads, cpd + 8 + 2 * nb * (aw // LANES), max(rows, LANES)), F32),
        vm((zn * kr, positions), F32),
        vm((zn * kr, positions), F32),
        vm((zn * kr, zn * kr), BF16),
        vm((zn, groups * 2, LANES), BF16),
        vm((groups, tb, LANES), BF16),
        vm((nb, tb, LANES), BF16),
        vm((LANES, rows), F32),
        vm((aw, rows), F32),
        vm((nb, 8, aw), F32),
        vm((nb, 8, aw), F32),
        vm((aw, nf), BF16),
        vm((nf, aw), BF16),
        dma((6 + kvl,)),
        dma((kvl * zn,)), dma((kvl * zn,)), dma((kvl * nb,)), dma((kvl * nb,)),
        dma((zn,)), dma((zn,)), dma((nb,)), dma((nb,)),
        dma((kvl * nb,)), dma((kvl * nb,)),
        dma((kvl * zn,)), dma((kvl * zn,)), dma((kvl * zn,)), dma((kvl * zn,)),
        dma((kvl * nb,)), dma((kvl * nb,)),
        dma((heads,)), dma((heads,)),
        dma((nb,)), dma((nb,)), dma((zn,)), dma((zn,)),
    ]
    vmem = pl.BlockSpec(memory_space=pltpu.VMEM)
    hbm = pl.BlockSpec(memory_space=pltpu.HBM)
    return pl.pallas_call(
        functools.partial(kernel, sizes, heads, float(heads * nf)),
        out_shape=(
            jax.ShapeDtypeStruct(cotangent.shape, F32),
            jax.ShapeDtypeStruct(adapter.shape, F32),
        ),
        in_specs=[hbm] * 7,
        out_specs=(vmem, vmem),
        scratch_shapes=scratch,
        compiler_params=pltpu.CompilerParams(
            collective_id=0, has_side_effects=True, vmem_limit_bytes=63 * 1024 * 1024
        ),
        cost_estimate=pl.CostEstimate(
            flops=4 * rows * nh * HD * positions,
            bytes_accessed=4 * positions * kvw,
            transcendentals=rows * nh * positions,
        ),
        name="distill",
    )(queries, keys, values, norm_gain.reshape(nh, HD), adapter, source_row.reshape(1, -1), cotangent)


def solution(mesh, sizes=(YN, ZN, XN)):
    return jax.shard_map(
        functools.partial(local, sizes, mesh.shape["head"]),
        mesh=mesh,
        in_specs=(
            P("ctx", "head"),
            P("ctx", "head"),
            P("ctx", "head"),
            P("head"),
            P("ctx", "head"),
            P(),
            P("ctx", None),
        ),
        out_specs=(P("ctx", None), P("ctx", "head")),
        check_vma=False,
    )
```

```python
import functools

import jax
import jax.numpy as jnp
from jax import lax
from jax.experimental import pallas as pl
from jax.experimental.pallas import tpu as pltpu
from jax.sharding import PartitionSpec as P

H = 64
HD = 128
GROUP = 8
LANES = 128
LOG2E = 1.4426950408889634
YN, ZN, XN = 4, 8, 2

F32 = jnp.float32
BF16 = jnp.bfloat16
MESH = pl.DeviceIdType.MESH


def iota(shape, axis):
    return lax.broadcasted_iota(jnp.int32, shape, axis)


def nn(left, right):
    return lax.dot_general(left, right, (((1,), (0,)), ((), ())), preferred_element_type=F32)


def div(a, n):
    return a // n if isinstance(a, int) else a >> (n.bit_length() - 1)


def mod(a, n):
    return a % n if isinstance(a, int) else a & (n - 1)


def regroup(outer, zn):
    size = outer * zn * 2
    row, col = iota((size, 1), 0), iota((size, size), 1)
    head, rest = div(row, 2 * zn), mod(row, 2 * zn)
    return (col == div(rest, 2) * (2 * outer) + head * 2 + mod(rest, 2)).astype(F32).astype(BF16)


def row_of(position, sizes):
    yn, zn, xn = sizes
    pair, block = div(position, 2), div(position, 2 * zn)
    ctx = (div(block, xn) * zn + mod(pair, zn)) * xn + mod(block, xn)
    return 2 * ctx + mod(position, 2)


def split3(value):
    high = value.astype(BF16)
    rest = value - high.astype(F32)
    middle = rest.astype(BF16)
    return high, middle, (rest - middle.astype(F32)).astype(BF16)


def kernel(sizes, heads, eps_div, q_hbm, k_hbm, v_hbm, gain_hbm, ad_hbm, src_hbm, cot_hbm,
           stu_ref, grad_ref,
           q_ref, gain_ref, src_ref, cot_ref, kbuf, k_t, vaug, qall, osend, orecv, zsend, zrecv,
           hz, hall, gall, mpre, squares, hx, s_even, s_odd, regroup_h, cz, cg, call, cot_t, mpre_t, st1s, st1r,
           adp, ad_t,
           loc_sem, zq_s, zq_r, q2_s, q2_r, zc_s, zc_r, c2_s, c2_r, o_s, o_r,
           zr_s, zr_r, hz_s, hz_r, h2_s, h2_r, hx_s, hx_r, s1_s, s1_r, za_s, za_r):
    sbuf = (s_even, s_odd)
    yn, zn, xn = sizes
    nb = yn * xn
    tb = 2 * zn
    rows = nb * tb
    kvl = k_hbm.shape[1] // HD
    nh = kvl * GROUP
    kr = GROUP * 2
    cpd = ad_hbm.shape[0]
    per_group = LANES // cpd
    aw = zn * xn * cpd
    groups = cot_hbm.shape[1] // LANES

    ctx = lax.axis_index("ctx")
    hd = lax.axis_index("head")
    y = div(ctx, zn * xn)
    z = mod(div(ctx, xn), zn)
    x = mod(ctx, xn)
    b = y * xn + x

    def at(y_, z_, x_):
        return ((y_ * zn + z_) * xn + x_, hd)

    def z_plus(d):
        return mod(z + d, zn)

    ring = sorted(range(1, zn), key=lambda d: -min(d, zn - d))

    def z_dev(d):
        return at(y, z_plus(d), x)

    def steps(i):
        far, turn = div(i, yn), mod(i, yn)
        if isinstance(i, int):
            near = (0, 1, 3, 2)[turn] if yn == 4 else turn
            return (near if far == 0 else (2, 1, 3, 0)[turn] if yn == 4 else yn - 1 - turn), far
        if yn == 4:
            first = jnp.where(turn == 2, 3, jnp.where(turn == 3, 2, turn))
            second = jnp.where(turn == 0, 2, jnp.where(turn == 1, 1, jnp.where(turn == 2, 3, 0)))
        else:
            first, second = turn, yn - 1 - turn
        return jnp.where(far == 0, first, second), far

    def plus(i):
        dy, dx = steps(i)
        return mod(y + dy, yn), mod(x + dx, xn)

    def minus(i):
        dy, dx = steps(i)
        return mod(y + yn - dy, yn), mod(x + xn - dx, xn)

    def plus_dev(i):
        py, px = plus(i)
        return at(py, z, px)

    def minus_dev(i):
        py, px = minus(i)
        return at(py, z, px)

    def rcopy(src, dst, ssem, rsem, dev):
        return pltpu.make_async_remote_copy(
            src_ref=src, dst_ref=dst, send_sem=ssem, recv_sem=rsem, device_id=dev, device_id_type=MESH
        )

    q_load = pltpu.make_async_copy(q_hbm, q_ref, loc_sem.at[0])
    q_load.start()
    barrier = pltpu.get_barrier_semaphore()
    partners = (
        [z_dev(d) for d in range(1, zn)]
        + [plus_dev(i) for i in range(1, nb)]
        + [(ctx, mod(hd + e, heads)) for e in range(1, heads)]
    )
    for dev in partners:
        pl.semaphore_signal(barrier, inc=1, device_id=dev, device_id_type=MESH)

    cot_load = pltpu.make_async_copy(cot_hbm, cot_ref, loc_sem.at[1])
    k_load = pltpu.make_async_copy(k_hbm, kbuf, loc_sem.at[2])
    own_ad = pl.ds(pl.multiple_of((z * xn + x) * cpd, cpd), cpd)
    ad_load = pltpu.make_async_copy(ad_hbm, adp.at[own_ad], loc_sem.at[3])
    late_loads = [
        pltpu.make_async_copy(gain_hbm, gain_ref, loc_sem.at[4]),
        pltpu.make_async_copy(src_hbm, src_ref, loc_sem.at[5]),
    ]
    for k in range(kvl):
        late_loads.append(
            pltpu.make_async_copy(
                v_hbm.at[:, k * HD : (k + 1) * HD], vaug.at[k, :, 0:HD], loc_sem.at[6 + k]
            )
        )
    for load in [cot_load, k_load, ad_load] + late_loads:
        load.start()

    q_load.wait()
    qf = q_ref[...].astype(F32)
    for k in range(kvl):
        qall[k * nb, pl.ds(z, 1)] = jnp.concatenate(
            [qf[:, (k * GROUP + h) * HD : (k * GROUP + h + 1) * HD] for h in range(GROUP)], axis=0
        ).astype(BF16)[None]
    cot_load.wait()
    cf = cot_ref[...].astype(F32)
    cz[pl.ds(z, 1)] = jnp.concatenate(
        [cf[:, g * LANES : (g + 1) * LANES] for g in range(groups)], axis=0
    ).astype(BF16)[None]
    pl.semaphore_wait(barrier, len(partners))

    def z_group(make):
        copies = {d: make(d) for d in ring}
        for copy in copies.values():
            copy.start()
        return copies

    def received(copies):
        for copy in copies.values():
            copy.wait_recv()

    def sent(*groups_of_copies):
        for copies in groups_of_copies:
            for copy in copies.values():
                copy.wait_send()

    zq = [
        z_group(
            lambda d, k=k: rcopy(
                qall.at[k * nb, z], qall.at[k * nb, z], zq_s.at[k * zn + d], zq_r.at[k * zn + d], z_dev(d)
            )
        )
        for k in range(kvl)
    ]
    zc = z_group(lambda d: rcopy(cz.at[z], cz.at[z], zc_s.at[d], zc_r.at[d], z_dev(d)))

    k_load.wait()
    for k in range(kvl):
        k_t[k] = kbuf[:, k * HD : (k + 1) * HD].astype(F32).T.astype(BF16)
    for k in range(kvl):
        vaug[k, :, HD : 2 * HD] = jnp.ones((vaug.shape[1], HD), BF16)

    def q_copy(j, i):
        return rcopy(qall.at[j - i], qall.at[j], q2_s.at[j], q2_r.at[j], plus_dev(i))

    for k in range(kvl):
        received(zq[k])
        for i in range(1, nb):
            q_copy(k * nb + i, i).start()

    for d in range(zn):
        for e in range(1, xn):
            other = pl.multiple_of((d * xn + mod(x + e, xn)) * cpd, cpd)
            adp[pl.ds(other, cpd), :] = jnp.zeros((cpd, nh * HD), BF16)
    st1s[...] = jnp.zeros_like(st1s)
    ad_load.wait()
    za = z_group(lambda d: rcopy(adp.at[own_ad], adp.at[own_ad], za_s.at[d], za_r.at[d], z_dev(d)))
    for load in late_loads:
        load.wait()

    factor = (HD ** -0.5) * LOG2E
    qrows = zn * kr
    eye = iota((qrows, LANES), 0) == iota((qrows, LANES), 1)

    def stat_tile(row):
        high, middle, low = split3(row)
        line = iota((kr, LANES), 0)
        tile = jnp.where(line == 0, high.astype(F32), jnp.where(line == 1, middle.astype(F32), low.astype(F32)))
        return jnp.where(line < 3, tile, 0.0).astype(BF16)

    def stat_row(tile):
        wide = tile.astype(F32)
        return wide[0:1, :] + wide[1:2, :] + wide[2:3, :]

    def score(k, i, count, buf):
        q = qall[pl.ds(k * nb + i, count)].reshape(count * qrows, HD)
        buf[0 : count * qrows, :] = nn(q, k_t[k])

    def weigh(k, i, count, buf):
        s = buf[0 : count * qrows, :]
        m = jnp.max(s, axis=1, keepdims=True)
        p = jnp.exp2((buf[0 : count * qrows, :] - m) * factor).astype(BF16)
        oa = nn(p, vaug[k])
        total = oa[:, HD : 2 * HD]
        o = (oa[:, 0:HD] / total).astype(BF16)
        lse = m * factor + jnp.log2(total)
        for c in range(count):
            part = slice(c * qrows, (c + 1) * qrows)
            osend[k * nb + i + c, 0:zn] = o[part].reshape(zn, kr, HD)
            row = jnp.sum(jnp.where(eye, lse[part], 0.0), axis=0, keepdims=True)
            osend[k * nb + i + c, zn] = stat_tile(row)
            if i + c > 0:
                o_copy(k * nb + i + c, i + c).start()

    def o_copy(j, i):
        return rcopy(osend.at[j], orecv.at[j], o_s.at[j], o_r.at[j], minus_dev(i))

    units = [(1, 1)] + [(i, 2) for i in range(2, nb, 2)]

    def queries_here(k, i, count):
        for c in range(count):
            q_copy(k * nb + i + c, i + c).wait_recv()

    def attend(k, carry):
        for n, (i, count) in enumerate(units):
            here, there = sbuf[n % 2], sbuf[(n + 1) % 2]
            if n + 1 < len(units):
                queries_here(k, *units[n + 1])
                score(k, *units[n + 1], there)
                weigh(k, i, count, here)
            else:

                @pl.when(k == 1)
                def _():
                    combine(0)

                later = jnp.minimum(k + 1, kvl - 1)

                @pl.when(k + 1 < kvl)
                def _():
                    queries_here(later, *units[0])

                score(later, *units[0], there)
                weigh(k, i, count, here)
        return carry

    def z_copies(k):
        return {
            d: rcopy(zsend.at[k, z_plus(d)], zrecv.at[k, d], zr_s.at[k * zn + d], zr_r.at[k * zn + d], z_dev(d))
            for d in ring
        }

    def combine(k):
        for i in range(1, nb):
            o_copy(k * nb + i, i).wait_recv()
        parts = [(osend if i == 0 else orecv).at[k * nb + i] for i in range(nb)]
        stats = [stat_row(part[zn]) for part in parts]
        top = functools.reduce(jnp.maximum, stats)
        weights = [jnp.exp2(st - top) for st in stats]
        weight_sum = functools.reduce(jnp.add, weights)
        inverse = 1.0 / weight_sum
        acc = jnp.zeros((qrows, HD), F32)
        for i in range(nb):
            share = jnp.where(eye, weights[i] * inverse, 0.0)[:, 0:qrows].astype(BF16)
            acc = acc + nn(share, parts[i][0:zn].reshape(qrows, HD))
        zsend[k, :, 0:kr, :] = acc.astype(BF16).reshape(zn, kr, HD)
        tile = stat_tile(top + jnp.log2(weight_sum))
        for d in range(zn):
            zsend[k, d, kr : 2 * kr, :] = tile
        for copy in z_copies(k).values():
            copy.start()

    mine = iota((kr, LANES), 1) == iota((kr, LANES), 0) + z * kr

    def settle(k, copies):
        received(copies)
        parts = [zsend[k, z]] + [zrecv[k, d] for d in range(1, zn)]
        stats = [stat_row(part[kr : 2 * kr, :]) for part in parts]
        top = functools.reduce(jnp.maximum, stats)
        weights = [jnp.exp2(st - top) for st in stats]
        inverse = 1.0 / functools.reduce(jnp.add, weights)
        acc = jnp.zeros((kr, HD), F32)
        for d in range(zn):
            column = jnp.sum(jnp.where(mine, weights[d] * inverse, 0.0), axis=1, keepdims=True)
            acc = acc + column * parts[d][0:kr, :].astype(F32)
        hz[k, pl.ds(z, 1)] = acc.astype(BF16)[None]
        return z_group(
            lambda d: rcopy(hz.at[k, z], hz.at[k, z], hz_s.at[k * zn + d], hz_r.at[k * zn + d], z_dev(d))
        )

    def spread(k, copies):
        received(copies)
        pieces = nn(regroup_h[...], hz[k].reshape(zn * kr, HD)).astype(BF16)
        for h in range(GROUP):
            hall[k, pl.ds(b, 1), :, h * HD : (h + 1) * HD] = pieces[h * tb : (h + 1) * tb, :][None]
        copies = {
            i: rcopy(hall.at[k, b], hall.at[k, b], h2_s.at[k * nb + i], h2_r.at[k * nb + i], plus_dev(i))
            for i in range(1, nb)
        }
        for copy in copies.values():
            copy.start()
        return copies

    def project(k, copies):
        gain = gain_ref[...].astype(F32)
        for i in range(nb):
            if i > 0:
                copies[i].wait_recv()
            my, mx = minus(i)
            there = my * xn + mx
            hidden = hall[k, there].astype(F32)
            lines = pl.ds(pl.multiple_of(there * tb, tb), tb)
            partial = jnp.zeros((tb, HD), F32)
            for h in range(GROUP):
                piece = hidden[:, h * HD : (h + 1) * HD]
                partial = partial + piece * piece
                head = k * GROUP + h
                gall[lines, head * HD : (head + 1) * HD] = (piece * gain[head : head + 1, :]).astype(BF16)
            squares[lines, :] = partial if k == 0 else squares[lines, :] + partial
        width = GROUP * HD
        part = nn(gall[:, k * width : (k + 1) * width], ad_t[k * width : (k + 1) * width, :])
        mpre[...] = part if k == 0 else mpre[...] + part

    def turn_adapter(k):
        for h in range(k * GROUP, (k + 1) * GROUP):
            for first in range(0, aw, LANES):
                ad_t[h * HD : (h + 1) * HD, first : first + LANES] = (
                    adp[first : first + LANES, h * HD : (h + 1) * HD].astype(F32).T.astype(BF16)
                )

    score(0, 0, 1, sbuf[0])
    score(1, 0, 1, sbuf[1])
    weigh(0, 0, 1, sbuf[0])
    queries_here(0, *units[0])
    score(0, *units[0], sbuf[0])
    weigh(1, 0, 1, sbuf[1])
    lax.fori_loop(0, kvl, attend, 0)

    regroup_h[...] = regroup(GROUP, zn)
    received(zc)
    pieces = nn(regroup(groups, zn), cz[...].reshape(zn * groups * 2, LANES))
    cg[...] = pieces.astype(BF16).reshape(groups, tb, LANES)
    my_group = div(ctx, per_group)
    c2 = {}
    for i in range(1, nb):
        py, px = plus(i)
        there = div((py * zn + z) * xn + px, per_group)
        c2[i] = rcopy(cg.at[there], call.at[b], c2_s.at[i], c2_r.at[i], at(py, z, px))
        c2[i].start()
    call[pl.ds(b, 1)] = cg[pl.ds(my_group, 1)]

    h0 = settle(0, z_copies(0))
    sent(*zq, zc)
    combine(1)
    received(za)
    turn_adapter(0)
    g0 = spread(0, h0)

    sel = iota((rows, rows), 1) == row_of(iota((rows, 1), 0), sizes)
    wanted = jnp.sum(
        jnp.where(sel, jnp.broadcast_to(src_ref[...].astype(F32), (rows, rows)), 0.0),
        axis=1, keepdims=True,
    )
    pick = (wanted == row_of(iota((1, rows), 1), sizes).astype(F32)).astype(F32)
    received(c2)
    cot_rows = nn(pick.T.astype(BF16), call[...].reshape(rows, LANES))
    cot_t[...] = cot_rows.T
    token = iota((nb * 2, 1), 0)
    block = div(token, 2)
    token = 2 * ((div(block, xn) * zn + z) * xn + mod(block, xn)) + mod(token, 2)
    wanted = jnp.sum(
        jnp.where(iota((nb * 2, rows), 1) == token, src_ref[...].astype(F32), 0.0), axis=1, keepdims=True
    )
    pick = (wanted == row_of(iota((1, rows), 1), sizes).astype(F32)).astype(F32)

    h1 = settle(1, z_copies(1))
    turn_adapter(1)
    sent(za, z_copies(0), z_copies(1), c2)
    for j in range(kvl * nb):
        if j % nb:
            q_copy(j, j % nb).wait_send()
            o_copy(j, j % nb).wait_send()
    g1 = spread(1, h1)
    project(0, g0)
    sent(h0, h1, g0)
    project(1, g1)

    for first in range(0, aw, LANES):
        mpre_t[first : first + LANES, :] = mpre[:, first : first + LANES].T
    hx[pl.ds(hd, 1), 0:cpd, 0:rows] = mpre_t[own_ad, :][None]
    power = jnp.sum(squares[...].T, axis=0, keepdims=True)
    hx[pl.ds(hd, 1), cpd : cpd + 8, 0:rows] = jnp.broadcast_to(power, (8, rows))[None]
    one_hot = pick.astype(BF16)
    chosen = functools.reduce(jnp.add, [nn(one_hot, term) for term in split3(mpre[...])])
    base = cpd + 8
    for j in range(aw // LANES):
        hx[pl.ds(hd, 1), base + j * 2 * nb : base + (j + 1) * 2 * nb, :] = chosen[
            :, j * LANES : (j + 1) * LANES
        ][None]
    hxc = {}
    for e in range(1, heads):
        hxc[e] = rcopy(hx.at[hd], hx.at[hd], hx_s.at[e], hx_r.at[e], (ctx, mod(hd + e, heads)))
        hxc[e].start()
    sent(g1)
    received(hxc)
    summed = hx[0]
    for e in range(1, heads):
        summed = summed + hx[e]
    scale = lax.rsqrt(summed[cpd : cpd + 1, 0:rows] / eps_div + 1e-05)

    token_scale = jnp.sum(pick * scale, axis=1, keepdims=True)
    for j in range(aw // LANES):
        pre = token_scale * summed[base + j * 2 * nb : base + (j + 1) * 2 * nb, :]
        out = pre / (1.0 + jnp.exp(-pre))
        for d in range(nb):
            st1s[d, 0:2, j * LANES : (j + 1) * LANES] = out[2 * d : 2 * d + 2, :]
    s1 = {}
    for i in range(1, nb):
        py, px = plus(i)
        s1[i] = rcopy(st1s.at[py * xn + px], st1r.at[b], s1_s.at[i], s1_r.at[i], at(py, z, px))
        s1[i].start()
    st1r[pl.ds(b, 1)] = st1s[pl.ds(b, 1)]
    sent(hxc)

    pre = scale * summed[0:cpd, 0:rows]
    sig = 1.0 / (1.0 + jnp.exp(-pre))
    own = pl.multiple_of(mod(ctx, per_group) * cpd, cpd)
    slope = (cot_t[pl.ds(own, cpd), :] * sig * (1.0 + pre * (1.0 - sig)) * scale).astype(BF16)
    grad_ref[...] = nn(slope, gall[...]) * (rows ** -0.5)

    sent(s1)
    received(s1)
    for py in range(yn):
        tile = st1r[py * xn]
        for px in range(1, xn):
            tile = tile + st1r[py * xn + px]
        stu_ref[:, py * aw : (py + 1) * aw] = tile[0:2, :]


def local(sizes, heads, queries, keys, values, norm_gain, adapter, source_row, cotangent):
    yn, zn, xn = sizes
    nb = yn * xn
    tb = 2 * zn
    rows = nb * tb
    positions, kvw = keys.shape
    kvl = kvw // HD
    nh = kvl * GROUP
    nf = nh * HD
    kr = GROUP * 2
    cpd = adapter.shape[0]
    aw = zn * xn * cpd
    groups = cotangent.shape[1] // LANES
    vm = pltpu.VMEM
    dma = pltpu.SemaphoreType.DMA
    scratch = [
        vm(queries.shape, BF16),
        vm((nh, HD), BF16),
        vm((1, rows), jnp.int32),
        vm(cotangent.shape, BF16),
        vm((positions, kvw), BF16),
        vm((kvl, HD, positions), BF16),
        vm((kvl, positions, 2 * HD), BF16),
        vm((kvl * nb, zn, kr, HD), BF16),
        vm((kvl * nb, zn + 1, kr, HD), BF16),
        vm((kvl * nb, zn + 1, kr, HD), BF16),
        vm((kvl, zn, 2 * kr, HD), BF16),
        vm((kvl, zn, 2 * kr, HD), BF16),
        vm((kvl, zn, kr, HD), BF16),
        vm((kvl, nb, tb, GROUP * HD), BF16),
        vm((rows, nf), BF16),
        vm((rows, aw), F32),
        vm((rows, HD), F32),
        vm((heads, cpd + 8 + 2 * nb * (aw // LANES), max(rows, LANES)), F32),
        vm((2 * zn * kr, positions), F32),
        vm((2 * zn * kr, positions), F32),
        vm((zn * kr, zn * kr), BF16),
        vm((zn, groups * 2, LANES), BF16),
        vm((groups, tb, LANES), BF16),
        vm((nb, tb, LANES), BF16),
        vm((LANES, rows), F32),
        vm((aw, rows), F32),
        vm((nb, 8, aw), F32),
        vm((nb, 8, aw), F32),
        vm((aw, nf), BF16),
        vm((nf, aw), BF16),
        dma((6 + kvl,)),
        dma((kvl * zn,)), dma((kvl * zn,)), dma((kvl * nb,)), dma((kvl * nb,)),
        dma((zn,)), dma((zn,)), dma((nb,)), dma((nb,)),
        dma((kvl * nb,)), dma((kvl * nb,)),
        dma((kvl * zn,)), dma((kvl * zn,)), dma((kvl * zn,)), dma((kvl * zn,)),
        dma((kvl * nb,)), dma((kvl * nb,)),
        dma((heads,)), dma((heads,)),
        dma((nb,)), dma((nb,)), dma((zn,)), dma((zn,)),
    ]
    vmem = pl.BlockSpec(memory_space=pltpu.VMEM)
    hbm = pl.BlockSpec(memory_space=pltpu.HBM)
    outs = pl.pallas_call(
        functools.partial(kernel, sizes, heads, float(heads * nf)),
        out_shape=(
            jax.ShapeDtypeStruct(cotangent.shape, F32),
            jax.ShapeDtypeStruct(adapter.shape, F32),
        ),
        in_specs=[hbm] * 7,
        out_specs=(vmem, vmem),
        scratch_shapes=scratch,
        compiler_params=pltpu.CompilerParams(
            collective_id=0, has_side_effects=True, vmem_limit_bytes=63 * 1024 * 1024
        ),
        cost_estimate=pl.CostEstimate(
            flops=4 * rows * nh * HD * positions,
            bytes_accessed=4 * positions * kvw,
            transcendentals=rows * nh * positions,
        ),
        name="distill",
    )(queries, keys, values, norm_gain.reshape(nh, HD), adapter, source_row.reshape(1, -1), cotangent)
    return pl.pallas_call(
        copy_kernel,
        out_shape=tuple(jax.ShapeDtypeStruct(out.shape, F32) for out in outs),
        in_specs=[hbm] * 2,
        out_specs=(hbm, hbm),
        scratch_shapes=[dma((2,))],
        compiler_params=pltpu.CompilerParams(vmem_limit_bytes=63 * 1024 * 1024),
        name="hand_out",
    )(*outs)


def copy_kernel(a_ref, b_ref, a_out, b_out, sem):
    copies = [
        pltpu.make_async_copy(b_ref, b_out, sem.at[0]),
        pltpu.make_async_copy(a_ref, a_out, sem.at[1]),
    ]
    for copy in copies:
        copy.start()
    for copy in copies:
        copy.wait()


def solution(mesh, sizes=(YN, ZN, XN)):
    return jax.shard_map(
        functools.partial(local, sizes, mesh.shape["head"]),
        mesh=mesh,
        in_specs=(
            P("ctx", "head"),
            P("ctx", "head"),
            P("ctx", "head"),
            P("head"),
            P("ctx", "head"),
            P(),
            P("ctx", None),
        ),
        out_specs=(P("ctx", None), P("ctx", "head")),
        check_vma=False,
    )
```

```python
import functools

import jax
import jax.numpy as jnp
from jax import lax
from jax.experimental import pallas as pl
from jax.experimental.pallas import tpu as pltpu
from jax.sharding import PartitionSpec as P

H = 64
HD = 128
GROUP = 8
LANES = 128
LOG2E = 1.4426950408889634
YN, ZN, XN = 4, 8, 2

F32 = jnp.float32
BF16 = jnp.bfloat16
MESH = pl.DeviceIdType.MESH


def iota(shape, axis):
    return lax.broadcasted_iota(jnp.int32, shape, axis)


def nn(left, right):
    return lax.dot_general(left, right, (((1,), (0,)), ((), ())), preferred_element_type=F32)


def div(a, n):
    return a // n if isinstance(a, int) else a >> (n.bit_length() - 1)


def mod(a, n):
    return a % n if isinstance(a, int) else a & (n - 1)


def regroup(outer, zn):
    size = outer * zn * 2
    row, col = iota((size, 1), 0), iota((size, size), 1)
    head, rest = div(row, 2 * zn), mod(row, 2 * zn)
    return (col == div(rest, 2) * (2 * outer) + head * 2 + mod(rest, 2)).astype(F32).astype(BF16)


def row_of(position, sizes):
    yn, zn, xn = sizes
    pair, block = div(position, 2), div(position, 2 * zn)
    ctx = (div(block, xn) * zn + mod(pair, zn)) * xn + mod(block, xn)
    return 2 * ctx + mod(position, 2)


def split3(value):
    high = value.astype(BF16)
    rest = value - high.astype(F32)
    middle = rest.astype(BF16)
    return high, middle, (rest - middle.astype(F32)).astype(BF16)


def kernel(sizes, heads, eps_div, q_hbm, k_hbm, v_hbm, gain_hbm, ad_hbm, src_hbm, cot_hbm,
           stu_ref, grad_ref,
           q_ref, gain_ref, src_ref, cot_ref, kbuf, k_t, vaug, qall, osend, orecv, zsend, zrecv,
           hz, hall, gall, mpre, squares, hx, s_even, s_odd, regroup_h, cz, cg, call, cot_t, mpre_t, st1s, st1r,
           adp, ad_t,
           loc_sem, zq_s, zq_r, q2_s, q2_r, zc_s, zc_r, c2_s, c2_r, o_s, o_r,
           zr_s, zr_r, hz_s, hz_r, h2_s, h2_r, hx_s, hx_r, s1_s, s1_r, za_s, za_r):
    sbuf = (s_even, s_odd)
    yn, zn, xn = sizes
    nb = yn * xn
    tb = 2 * zn
    rows = nb * tb
    kvl = k_hbm.shape[1] // HD
    nh = kvl * GROUP
    kr = GROUP * 2
    cpd = ad_hbm.shape[0]
    per_group = LANES // cpd
    aw = zn * xn * cpd
    groups = cot_hbm.shape[1] // LANES

    ctx = lax.axis_index("ctx")
    hd = lax.axis_index("head")
    y = div(ctx, zn * xn)
    z = mod(div(ctx, xn), zn)
    x = mod(ctx, xn)
    b = y * xn + x

    def at(y_, z_, x_):
        return ((y_ * zn + z_) * xn + x_, hd)

    def z_plus(d):
        return mod(z + d, zn)

    ring = sorted(range(1, zn), key=lambda d: -min(d, zn - d))

    def z_dev(d):
        return at(y, z_plus(d), x)

    def steps(i):
        far, turn = div(i, yn), mod(i, yn)
        if isinstance(i, int):
            near = (0, 1, 3, 2)[turn] if yn == 4 else turn
            return (near if far == 0 else (2, 1, 3, 0)[turn] if yn == 4 else yn - 1 - turn), far
        if yn == 4:
            first = jnp.where(turn == 2, 3, jnp.where(turn == 3, 2, turn))
            second = jnp.where(turn == 0, 2, jnp.where(turn == 1, 1, jnp.where(turn == 2, 3, 0)))
        else:
            first, second = turn, yn - 1 - turn
        return jnp.where(far == 0, first, second), far

    def plus(i):
        dy, dx = steps(i)
        return mod(y + dy, yn), mod(x + dx, xn)

    def minus(i):
        dy, dx = steps(i)
        return mod(y + yn - dy, yn), mod(x + xn - dx, xn)

    def plus_dev(i):
        py, px = plus(i)
        return at(py, z, px)

    def minus_dev(i):
        py, px = minus(i)
        return at(py, z, px)

    def rcopy(src, dst, ssem, rsem, dev):
        return pltpu.make_async_remote_copy(
            src_ref=src, dst_ref=dst, send_sem=ssem, recv_sem=rsem, device_id=dev, device_id_type=MESH
        )

    q_load = pltpu.make_async_copy(q_hbm, q_ref, loc_sem.at[0])
    q_load.start()
    barrier = pltpu.get_barrier_semaphore()
    partners = (
        [z_dev(d) for d in range(1, zn)]
        + [plus_dev(i) for i in range(1, nb)]
        + [(ctx, mod(hd + e, heads)) for e in range(1, heads)]
    )
    for dev in partners:
        pl.semaphore_signal(barrier, inc=1, device_id=dev, device_id_type=MESH)

    cot_load = pltpu.make_async_copy(cot_hbm, cot_ref, loc_sem.at[1])
    k_load = pltpu.make_async_copy(k_hbm, kbuf, loc_sem.at[2])
    own_ad = pl.ds(pl.multiple_of((z * xn + x) * cpd, cpd), cpd)
    ad_load = pltpu.make_async_copy(ad_hbm, adp.at[own_ad], loc_sem.at[3])
    late_loads = [
        pltpu.make_async_copy(gain_hbm, gain_ref, loc_sem.at[4]),
        pltpu.make_async_copy(src_hbm, src_ref, loc_sem.at[5]),
    ]
    for k in range(kvl):
        late_loads.append(
            pltpu.make_async_copy(
                v_hbm.at[:, k * HD : (k + 1) * HD], vaug.at[k, :, 0:HD], loc_sem.at[6 + k]
            )
        )
    for load in [cot_load, k_load, ad_load] + late_loads:
        load.start()

    q_load.wait()
    qf = q_ref[...].astype(F32)
    for k in range(kvl):
        qall[k * nb, pl.ds(z, 1)] = jnp.concatenate(
            [qf[:, (k * GROUP + h) * HD : (k * GROUP + h + 1) * HD] for h in range(GROUP)], axis=0
        ).astype(BF16)[None]
    cot_load.wait()
    cf = cot_ref[...].astype(F32)
    cz[pl.ds(z, 1)] = jnp.concatenate(
        [cf[:, g * LANES : (g + 1) * LANES] for g in range(groups)], axis=0
    ).astype(BF16)[None]
    pl.semaphore_wait(barrier, len(partners))

    def z_group(make):
        copies = {d: make(d) for d in ring}
        for copy in copies.values():
            copy.start()
        return copies

    def received(copies):
        for copy in copies.values():
            copy.wait_recv()

    def sent(*groups_of_copies):
        for copies in groups_of_copies:
            for copy in copies.values():
                copy.wait_send()

    zq = [
        z_group(
            lambda d, k=k: rcopy(
                qall.at[k * nb, z], qall.at[k * nb, z], zq_s.at[k * zn + d], zq_r.at[k * zn + d], z_dev(d)
            )
        )
        for k in range(kvl)
    ]
    zc = z_group(lambda d: rcopy(cz.at[z], cz.at[z], zc_s.at[d], zc_r.at[d], z_dev(d)))

    k_load.wait()
    for k in range(kvl):
        k_t[k] = kbuf[:, k * HD : (k + 1) * HD].astype(F32).T.astype(BF16)
    for k in range(kvl):
        vaug[k, :, HD : 2 * HD] = jnp.ones((vaug.shape[1], HD), BF16)

    def q_copy(j, i):
        return rcopy(qall.at[j - i], qall.at[j], q2_s.at[j], q2_r.at[j], plus_dev(i))

    for k in range(kvl):
        received(zq[k])
        for i in range(1, nb):
            q_copy(k * nb + i, i).start()

    for d in range(zn):
        for e in range(1, xn):
            other = pl.multiple_of((d * xn + mod(x + e, xn)) * cpd, cpd)
            adp[pl.ds(other, cpd), :] = jnp.zeros((cpd, nh * HD), BF16)
    st1s[...] = jnp.zeros_like(st1s)
    ad_load.wait()
    za = z_group(lambda d: rcopy(adp.at[own_ad], adp.at[own_ad], za_s.at[d], za_r.at[d], z_dev(d)))
    for load in late_loads:
        load.wait()

    factor = (HD ** -0.5) * LOG2E
    qrows = zn * kr
    eye = iota((qrows, LANES), 0) == iota((qrows, LANES), 1)

    def stat_tile(row):
        high, middle, low = split3(row)
        line = iota((kr, LANES), 0)
        tile = jnp.where(line == 0, high.astype(F32), jnp.where(line == 1, middle.astype(F32), low.astype(F32)))
        return jnp.where(line < 3, tile, 0.0).astype(BF16)

    def stat_row(tile):
        wide = tile.astype(F32)
        return wide[0:1, :] + wide[1:2, :] + wide[2:3, :]

    def score(k, i, count, buf):
        q = qall[pl.ds(k * nb + i, count)].reshape(count * qrows, HD)
        buf[0 : count * qrows, :] = nn(q, k_t[k])

    def weigh(k, i, count, buf):
        s = buf[0 : count * qrows, :]
        m = jnp.max(s, axis=1, keepdims=True)
        p = jnp.exp2((buf[0 : count * qrows, :] - m) * factor).astype(BF16)
        oa = nn(p, vaug[k])
        total = oa[:, HD : 2 * HD]
        o = (oa[:, 0:HD] / total).astype(BF16)
        lse = m * factor + jnp.log2(total)
        for c in range(count):
            part = slice(c * qrows, (c + 1) * qrows)
            osend[k * nb + i + c, 0:zn] = o[part].reshape(zn, kr, HD)
            row = jnp.sum(jnp.where(eye, lse[part], 0.0), axis=0, keepdims=True)
            osend[k * nb + i + c, zn] = stat_tile(row)
            if i + c > 0:
                o_copy(k * nb + i + c, i + c).start()

    def o_copy(j, i):
        return rcopy(osend.at[j], orecv.at[j], o_s.at[j], o_r.at[j], minus_dev(i))

    units = [(1, 1)] + [(i, 2) for i in range(2, nb, 2)]

    def queries_here(k, i, count):
        for c in range(count):
            q_copy(k * nb + i + c, i + c).wait_recv()

    def attend(k, carry):
        for n, (i, count) in enumerate(units):
            here, there = sbuf[n % 2], sbuf[(n + 1) % 2]
            if n + 1 < len(units):
                queries_here(k, *units[n + 1])
                score(k, *units[n + 1], there)
                weigh(k, i, count, here)
            else:

                @pl.when(k == 1)
                def _():
                    combine(0)

                later = jnp.minimum(k + 1, kvl - 1)

                @pl.when(k + 1 < kvl)
                def _():
                    queries_here(later, *units[0])

                score(later, *units[0], there)
                weigh(k, i, count, here)
        return carry

    def z_copies(k):
        return {
            d: rcopy(zsend.at[k, z_plus(d)], zrecv.at[k, d], zr_s.at[k * zn + d], zr_r.at[k * zn + d], z_dev(d))
            for d in ring
        }

    def combine(k):
        for i in range(1, nb):
            o_copy(k * nb + i, i).wait_recv()
        parts = [(osend if i == 0 else orecv).at[k * nb + i] for i in range(nb)]
        stats = [stat_row(part[zn]) for part in parts]
        top = functools.reduce(jnp.maximum, stats)
        weights = [jnp.exp2(st - top) for st in stats]
        weight_sum = functools.reduce(jnp.add, weights)
        inverse = 1.0 / weight_sum
        acc = jnp.zeros((qrows, HD), F32)
        for i in range(nb):
            share = jnp.where(eye, weights[i] * inverse, 0.0)[:, 0:qrows].astype(BF16)
            acc = acc + nn(share, parts[i][0:zn].reshape(qrows, HD))
        zsend[k, :, 0:kr, :] = acc.astype(BF16).reshape(zn, kr, HD)
        tile = stat_tile(top + jnp.log2(weight_sum))
        for d in range(zn):
            zsend[k, d, kr : 2 * kr, :] = tile
        for copy in z_copies(k).values():
            copy.start()

    mine = iota((kr, LANES), 1) == iota((kr, LANES), 0) + z * kr

    def settle(k, copies):
        received(copies)
        parts = [zsend[k, z]] + [zrecv[k, d] for d in range(1, zn)]
        stats = [stat_row(part[kr : 2 * kr, :]) for part in parts]
        top = functools.reduce(jnp.maximum, stats)
        weights = [jnp.exp2(st - top) for st in stats]
        inverse = 1.0 / functools.reduce(jnp.add, weights)
        acc = jnp.zeros((kr, HD), F32)
        for d in range(zn):
            column = jnp.sum(jnp.where(mine, weights[d] * inverse, 0.0), axis=1, keepdims=True)
            acc = acc + column * parts[d][0:kr, :].astype(F32)
        hz[k, pl.ds(z, 1)] = acc.astype(BF16)[None]
        return z_group(
            lambda d: rcopy(hz.at[k, z], hz.at[k, z], hz_s.at[k * zn + d], hz_r.at[k * zn + d], z_dev(d))
        )

    def spread(k, copies):
        received(copies)
        pieces = nn(regroup_h[...], hz[k].reshape(zn * kr, HD)).astype(BF16)
        for h in range(GROUP):
            hall[k, pl.ds(b, 1), :, h * HD : (h + 1) * HD] = pieces[h * tb : (h + 1) * tb, :][None]
        copies = {
            i: rcopy(hall.at[k, b], hall.at[k, b], h2_s.at[k * nb + i], h2_r.at[k * nb + i], plus_dev(i))
            for i in range(1, nb)
        }
        for copy in copies.values():
            copy.start()
        return copies

    def project(k, copies):
        gain = gain_ref[...].astype(F32)
        for i in range(nb):
            if i > 0:
                copies[i].wait_recv()
            my, mx = minus(i)
            there = my * xn + mx
            hidden = hall[k, there].astype(F32)
            lines = pl.ds(pl.multiple_of(there * tb, tb), tb)
            partial = jnp.zeros((tb, HD), F32)
            for h in range(GROUP):
                piece = hidden[:, h * HD : (h + 1) * HD]
                partial = partial + piece * piece
                head = k * GROUP + h
                gall[lines, head * HD : (head + 1) * HD] = (piece * gain[head : head + 1, :]).astype(BF16)
            squares[lines, :] = partial if k == 0 else squares[lines, :] + partial
        width = GROUP * HD
        part = nn(gall[:, k * width : (k + 1) * width], ad_t[k * width : (k + 1) * width, :])
        mpre[...] = part if k == 0 else mpre[...] + part

    def turn_adapter(k):
        for h in range(k * GROUP, (k + 1) * GROUP):
            for first in range(0, aw, LANES):
                ad_t[h * HD : (h + 1) * HD, first : first + LANES] = (
                    adp[first : first + LANES, h * HD : (h + 1) * HD].astype(F32).T.astype(BF16)
                )

    score(0, 0, 1, sbuf[0])
    score(1, 0, 1, sbuf[1])
    weigh(0, 0, 1, sbuf[0])
    queries_here(0, *units[0])
    score(0, *units[0], sbuf[0])
    weigh(1, 0, 1, sbuf[1])
    lax.fori_loop(0, kvl, attend, 0)

    regroup_h[...] = regroup(GROUP, zn)
    received(zc)
    pieces = nn(regroup(groups, zn), cz[...].reshape(zn * groups * 2, LANES))
    cg[...] = pieces.astype(BF16).reshape(groups, tb, LANES)
    my_group = div(ctx, per_group)
    c2 = {}
    for i in range(1, nb):
        py, px = plus(i)
        there = div((py * zn + z) * xn + px, per_group)
        c2[i] = rcopy(cg.at[there], call.at[b], c2_s.at[i], c2_r.at[i], at(py, z, px))
        c2[i].start()
    call[pl.ds(b, 1)] = cg[pl.ds(my_group, 1)]

    h0 = settle(0, z_copies(0))
    sent(*zq, zc)
    combine(1)
    received(za)
    turn_adapter(0)
    g0 = spread(0, h0)

    sel = iota((rows, rows), 1) == row_of(iota((rows, 1), 0), sizes)
    wanted = jnp.sum(
        jnp.where(sel, jnp.broadcast_to(src_ref[...].astype(F32), (rows, rows)), 0.0),
        axis=1, keepdims=True,
    )
    pick = (wanted == row_of(iota((1, rows), 1), sizes).astype(F32)).astype(F32)
    received(c2)
    cot_rows = nn(pick.T.astype(BF16), call[...].reshape(rows, LANES))
    cot_t[...] = cot_rows.T
    token = iota((nb * 2, 1), 0)
    block = div(token, 2)
    token = 2 * ((div(block, xn) * zn + z) * xn + mod(block, xn)) + mod(token, 2)
    wanted = jnp.sum(
        jnp.where(iota((nb * 2, rows), 1) == token, src_ref[...].astype(F32), 0.0), axis=1, keepdims=True
    )
    pick = (wanted == row_of(iota((1, rows), 1), sizes).astype(F32)).astype(F32)

    h1 = settle(1, z_copies(1))
    turn_adapter(1)
    sent(za, z_copies(0), z_copies(1), c2)
    for j in range(kvl * nb):
        if j % nb:
            q_copy(j, j % nb).wait_send()
            o_copy(j, j % nb).wait_send()
    g1 = spread(1, h1)
    project(0, g0)
    sent(h0, h1, g0)
    project(1, g1)

    for first in range(0, aw, LANES):
        mpre_t[first : first + LANES, :] = mpre[:, first : first + LANES].T
    hx[pl.ds(hd, 1), 0:cpd, 0:rows] = mpre_t[own_ad, :][None]
    power = jnp.sum(squares[...].T, axis=0, keepdims=True)
    hx[pl.ds(hd, 1), cpd : cpd + 8, 0:rows] = jnp.broadcast_to(power, (8, rows))[None]
    one_hot = pick.astype(BF16)
    chosen = functools.reduce(jnp.add, [nn(one_hot, term) for term in split3(mpre[...])])
    base = cpd + 8
    for j in range(aw // LANES):
        hx[pl.ds(hd, 1), base + j * 2 * nb : base + (j + 1) * 2 * nb, :] = chosen[
            :, j * LANES : (j + 1) * LANES
        ][None]
    hxc = {}
    for e in range(1, heads):
        hxc[e] = rcopy(hx.at[hd], hx.at[hd], hx_s.at[e], hx_r.at[e], (ctx, mod(hd + e, heads)))
        hxc[e].start()
    sent(g1)
    received(hxc)
    summed = hx[0]
    for e in range(1, heads):
        summed = summed + hx[e]
    scale = lax.rsqrt(summed[cpd : cpd + 1, 0:rows] / eps_div + 1e-05)

    token_scale = jnp.sum(pick * scale, axis=1, keepdims=True)
    for j in range(aw // LANES):
        pre = token_scale * summed[base + j * 2 * nb : base + (j + 1) * 2 * nb, :]
        out = pre / (1.0 + jnp.exp(-pre))
        for d in range(nb):
            st1s[d, 0:2, j * LANES : (j + 1) * LANES] = out[2 * d : 2 * d + 2, :]
    s1 = {}
    for i in range(1, nb):
        py, px = plus(i)
        s1[i] = rcopy(st1s.at[py * xn + px], st1r.at[b], s1_s.at[i], s1_r.at[i], at(py, z, px))
        s1[i].start()
    st1r[pl.ds(b, 1)] = st1s[pl.ds(b, 1)]
    sent(hxc)

    pre = scale * summed[0:cpd, 0:rows]
    sig = 1.0 / (1.0 + jnp.exp(-pre))
    own = pl.multiple_of(mod(ctx, per_group) * cpd, cpd)
    slope = (cot_t[pl.ds(own, cpd), :] * sig * (1.0 + pre * (1.0 - sig)) * scale).astype(BF16)
    grad_ref[...] = nn(slope, gall[...]) * (rows ** -0.5)

    sent(s1)
    received(s1)
    for py in range(yn):
        tile = st1r[py * xn]
        for px in range(1, xn):
            tile = tile + st1r[py * xn + px]
        stu_ref[:, py * aw : (py + 1) * aw] = tile[0:2, :]


def local(sizes, heads, queries, keys, values, norm_gain, adapter, source_row, cotangent):
    yn, zn, xn = sizes
    nb = yn * xn
    tb = 2 * zn
    rows = nb * tb
    positions, kvw = keys.shape
    kvl = kvw // HD
    nh = kvl * GROUP
    nf = nh * HD
    kr = GROUP * 2
    cpd = adapter.shape[0]
    aw = zn * xn * cpd
    groups = cotangent.shape[1] // LANES
    vm = pltpu.VMEM
    dma = pltpu.SemaphoreType.DMA
    scratch = [
        vm(queries.shape, BF16),
        vm((nh, HD), BF16),
        vm((1, rows), jnp.int32),
        vm(cotangent.shape, BF16),
        vm((positions, kvw), BF16),
        vm((kvl, HD, positions), BF16),
        vm((kvl, positions, 2 * HD), BF16),
        vm((kvl * nb, zn, kr, HD), BF16),
        vm((kvl * nb, zn + 1, kr, HD), BF16),
        vm((kvl * nb, zn + 1, kr, HD), BF16),
        vm((kvl, zn, 2 * kr, HD), BF16),
        vm((kvl, zn, 2 * kr, HD), BF16),
        vm((kvl, zn, kr, HD), BF16),
        vm((kvl, nb, tb, GROUP * HD), BF16),
        vm((rows, nf), BF16),
        vm((rows, aw), F32),
        vm((rows, HD), F32),
        vm((heads, cpd + 8 + 2 * nb * (aw // LANES), max(rows, LANES)), F32),
        vm((2 * zn * kr, positions), F32),
        vm((2 * zn * kr, positions), F32),
        vm((zn * kr, zn * kr), BF16),
        vm((zn, groups * 2, LANES), BF16),
        vm((groups, tb, LANES), BF16),
        vm((nb, tb, LANES), BF16),
        vm((LANES, rows), F32),
        vm((aw, rows), F32),
        vm((nb, 8, aw), F32),
        vm((nb, 8, aw), F32),
        vm((aw, nf), BF16),
        vm((nf, aw), BF16),
        dma((6 + kvl,)),
        dma((kvl * zn,)), dma((kvl * zn,)), dma((kvl * nb,)), dma((kvl * nb,)),
        dma((zn,)), dma((zn,)), dma((nb,)), dma((nb,)),
        dma((kvl * nb,)), dma((kvl * nb,)),
        dma((kvl * zn,)), dma((kvl * zn,)), dma((kvl * zn,)), dma((kvl * zn,)),
        dma((kvl * nb,)), dma((kvl * nb,)),
        dma((heads,)), dma((heads,)),
        dma((nb,)), dma((nb,)), dma((zn,)), dma((zn,)),
    ]
    args = (queries, keys, values, norm_gain.reshape(nh, HD), adapter, source_row.reshape(1, -1), cotangent)
    vmem = pl.BlockSpec(memory_space=pltpu.VMEM)
    hbm = pl.BlockSpec(memory_space=pltpu.HBM)
    return pl.pallas_call(
        functools.partial(kernel, sizes, heads, float(heads * nf)),
        out_shape=(
            pltpu.VMEM(cotangent.shape, F32),
            pltpu.VMEM(adapter.shape, F32),
        ),
        in_specs=[hbm] * 7,
        out_specs=(vmem, vmem),
        scratch_shapes=scratch,
        compiler_params=pltpu.CompilerParams(
            collective_id=0, has_side_effects=True, vmem_limit_bytes=48 * 1024 * 1024
        ),
        cost_estimate=pl.CostEstimate(
            flops=4 * rows * nh * HD * positions,
            bytes_accessed=4 * positions * kvw,
            transcendentals=rows * nh * positions,
        ),
        name="distill",
    )(*(pltpu.with_memory_space_constraint(arg, pltpu.HBM) for arg in args))


def solution(mesh, sizes=(YN, ZN, XN)):
    return jax.shard_map(
        functools.partial(local, sizes, mesh.shape["head"]),
        mesh=mesh,
        in_specs=(
            P("ctx", "head"),
            P("ctx", "head"),
            P("ctx", "head"),
            P("head"),
            P("ctx", "head"),
            P(),
            P("ctx", None),
        ),
        out_specs=(P("ctx", None), P("ctx", "head")),
        check_vma=False,
    )
```

```python
import functools

import jax
import jax.numpy as jnp
from jax import lax
from jax.experimental import pallas as pl
from jax.experimental.pallas import tpu as pltpu
from jax.sharding import PartitionSpec as P

H = 64
HD = 128
GROUP = 8
LANES = 128
LOG2E = 1.4426950408889634
YN, ZN, XN = 4, 8, 2

F32 = jnp.float32
BF16 = jnp.bfloat16
MESH = pl.DeviceIdType.MESH


def iota(shape, axis):
    return lax.broadcasted_iota(jnp.int32, shape, axis)


def nn(left, right):
    return lax.dot_general(left, right, (((1,), (0,)), ((), ())), preferred_element_type=F32)


def div(a, n):
    return a // n if isinstance(a, int) else a >> (n.bit_length() - 1)


def mod(a, n):
    return a % n if isinstance(a, int) else a & (n - 1)


def regroup(outer, zn):
    size = outer * zn * 2
    row, col = iota((size, 1), 0), iota((size, size), 1)
    head, rest = div(row, 2 * zn), mod(row, 2 * zn)
    return (col == div(rest, 2) * (2 * outer) + head * 2 + mod(rest, 2)).astype(F32).astype(BF16)


def row_of(position, sizes):
    yn, zn, xn = sizes
    pair, block = div(position, 2), div(position, 2 * zn)
    ctx = (div(block, xn) * zn + mod(pair, zn)) * xn + mod(block, xn)
    return 2 * ctx + mod(position, 2)


def split3(value):
    high = value.astype(BF16)
    rest = value - high.astype(F32)
    middle = rest.astype(BF16)
    return high, middle, (rest - middle.astype(F32)).astype(BF16)


def kernel(sizes, heads, eps_div, q_hbm, k_hbm, v_hbm, gain_hbm, ad_hbm, src_hbm, cot_hbm,
           stu_ref, grad_ref,
           q_ref, gain_ref, src_ref, cot_ref, kbuf, k_t, vaug, qall, osend, orecv, zsend, zrecv,
           hz, hall, gall, mpre, squares, hx, s_even, s_odd, shares, regroup_h, cz, cg, call, cot_t, mpre_t, st1s, st1r,
           adp, ad_t,
           loc_sem, zq_s, zq_r, q2_s, q2_r, zc_s, zc_r, c2_s, c2_r, o_s, o_r,
           zr_s, zr_r, hz_s, hz_r, h2_s, h2_r, hx_s, hx_r, s1_s, s1_r, za_s, za_r):
    sbuf = (s_even, s_odd)
    yn, zn, xn = sizes
    nb = yn * xn
    tb = 2 * zn
    rows = nb * tb
    kvl = k_hbm.shape[1] // HD
    nh = kvl * GROUP
    kr = GROUP * 2
    cpd = ad_hbm.shape[0]
    per_group = LANES // cpd
    aw = zn * xn * cpd
    groups = cot_hbm.shape[1] // LANES

    ctx = lax.axis_index("ctx")
    hd = lax.axis_index("head")
    y = div(ctx, zn * xn)
    z = mod(div(ctx, xn), zn)
    x = mod(ctx, xn)
    b = y * xn + x

    def at(y_, z_, x_):
        return ((y_ * zn + z_) * xn + x_, hd)

    def z_plus(d):
        return mod(z + d, zn)

    def loop(first, last, body):
        def step(n, carry):
            body(n)
            return carry

        lax.fori_loop(first, last, step, 0)

    def over_ring(body):
        loop(0, zn - 1, lambda n: body(zn // 2 + jnp.where(mod(n, 2) == 1, -div(n + 1, 2), div(n, 2))))

    def z_dev(d):
        return at(y, z_plus(d), x)

    def steps(i):
        far, turn = div(i, yn), mod(i, yn)
        if isinstance(i, int):
            near = (0, 1, 3, 2)[turn] if yn == 4 else turn
            return (near if far == 0 else (2, 1, 3, 0)[turn] if yn == 4 else yn - 1 - turn), far
        if yn == 4:
            first = jnp.where(turn == 2, 3, jnp.where(turn == 3, 2, turn))
            second = jnp.where(turn == 0, 2, jnp.where(turn == 1, 1, jnp.where(turn == 2, 3, 0)))
        else:
            first, second = turn, yn - 1 - turn
        return jnp.where(far == 0, first, second), far

    def plus(i):
        dy, dx = steps(i)
        return mod(y + dy, yn), mod(x + dx, xn)

    def minus(i):
        dy, dx = steps(i)
        return mod(y + yn - dy, yn), mod(x + xn - dx, xn)

    def plus_dev(i):
        py, px = plus(i)
        return at(py, z, px)

    def minus_dev(i):
        py, px = minus(i)
        return at(py, z, px)

    def rcopy(src, dst, ssem, rsem, dev):
        return pltpu.make_async_remote_copy(
            src_ref=src, dst_ref=dst, send_sem=ssem, recv_sem=rsem, device_id=dev, device_id_type=MESH
        )

    q_load = pltpu.make_async_copy(q_hbm, q_ref, loc_sem.at[0])
    q_load.start()
    barrier = pltpu.get_barrier_semaphore()

    def greet(dev):
        pl.semaphore_signal(barrier, inc=1, device_id=dev, device_id_type=MESH)

    over_ring(lambda d: greet(z_dev(d)))
    loop(1, nb, lambda i: greet(plus_dev(i)))
    loop(1, heads, lambda e: greet((ctx, mod(hd + e, heads))))

    cot_load = pltpu.make_async_copy(cot_hbm, cot_ref, loc_sem.at[1])
    k_load = pltpu.make_async_copy(k_hbm, kbuf, loc_sem.at[2])
    own_ad = pl.ds(pl.multiple_of((z * xn + x) * cpd, cpd), cpd)
    ad_load = pltpu.make_async_copy(ad_hbm, adp.at[own_ad], loc_sem.at[3])
    late_loads = [
        pltpu.make_async_copy(gain_hbm, gain_ref, loc_sem.at[4]),
        pltpu.make_async_copy(src_hbm, src_ref, loc_sem.at[5]),
    ]
    for k in range(kvl):
        late_loads.append(
            pltpu.make_async_copy(
                v_hbm.at[:, k * HD : (k + 1) * HD], vaug.at[k, :, 0:HD], loc_sem.at[6 + k]
            )
        )
    for load in [cot_load, k_load, ad_load] + late_loads:
        load.start()

    q_load.wait()
    qf = q_ref[...].astype(F32)
    for k in range(kvl):
        qall[k * nb, pl.ds(z, 1)] = jnp.concatenate(
            [qf[:, (k * GROUP + h) * HD : (k * GROUP + h + 1) * HD] for h in range(GROUP)], axis=0
        ).astype(BF16)[None]
    cot_load.wait()
    cf = cot_ref[...].astype(F32)
    cz[pl.ds(z, 1)] = jnp.concatenate(
        [cf[:, g * LANES : (g + 1) * LANES] for g in range(groups)], axis=0
    ).astype(BF16)[None]
    pl.semaphore_wait(barrier, zn - 1 + nb - 1 + heads - 1)

    class Copies:
        def __init__(self, over, make):
            self.over, self.make = over, make

        def start(self):
            self.over(lambda n: self.make(n).start())
            return self

    def z_group(make):
        return Copies(over_ring, make)

    def plane_group(make):
        return Copies(lambda body: loop(1, nb, body), make)

    def received(copies):
        copies.over(lambda n: copies.make(n).wait_recv())

    def sent(*groups_of_copies):
        for copies in groups_of_copies:
            copies.over(lambda n, copies=copies: copies.make(n).wait_send())

    zq = [
        z_group(
            lambda d, k=k: rcopy(
                qall.at[k * nb, z], qall.at[k * nb, z], zq_s.at[k * zn + d], zq_r.at[k * zn + d], z_dev(d)
            )
        ).start()
        for k in range(kvl)
    ]
    zc = z_group(lambda d: rcopy(cz.at[z], cz.at[z], zc_s.at[d], zc_r.at[d], z_dev(d))).start()

    k_load.wait()

    def turn_keys(c):
        lines = pl.ds(pl.multiple_of(c * LANES, LANES), LANES)
        for k in range(kvl):
            k_t[k, :, lines] = kbuf[lines, k * HD : (k + 1) * HD].astype(F32).T.astype(BF16)

    loop(0, kbuf.shape[0] // LANES, turn_keys)
    for k in range(kvl):
        vaug[k, :, HD : 2 * HD] = jnp.ones((vaug.shape[1], HD), BF16)

    def q_copy(j, i):
        return rcopy(qall.at[j - i], qall.at[j], q2_s.at[j], q2_r.at[j], plus_dev(i))

    for k in range(kvl):
        received(zq[k])
        loop(1, nb, lambda i, k=k: q_copy(k * nb + i, i).start())


    def blank(d):
        for e in range(1, xn):
            other = pl.multiple_of((d * xn + mod(x + e, xn)) * cpd, cpd)
            adp[pl.ds(other, cpd), :] = jnp.zeros((cpd, nh * HD), BF16)

    loop(0, zn, blank)
    st1s[...] = jnp.zeros_like(st1s)
    ad_load.wait()
    za = z_group(lambda d: rcopy(adp.at[own_ad], adp.at[own_ad], za_s.at[d], za_r.at[d], z_dev(d))).start()
    for load in late_loads:
        load.wait()

    factor = (HD ** -0.5) * LOG2E
    qrows = zn * kr
    eye = iota((qrows, LANES), 0) == iota((qrows, LANES), 1)

    def stat_tile(row):
        high, middle, low = split3(row)
        line = iota((kr, LANES), 0)
        tile = jnp.where(line == 0, high.astype(F32), jnp.where(line == 1, middle.astype(F32), low.astype(F32)))
        return jnp.where(line < 3, tile, 0.0).astype(BF16)

    def stat_row(tile):
        wide = tile.astype(F32)
        return wide[0:1, :] + wide[1:2, :] + wide[2:3, :]

    def unit(n):
        k = jnp.where(n < kvl, n, jnp.where(n < kvl + nb - 1, 0, 1))
        i = jnp.where(n < kvl, 0, jnp.where(n < kvl + nb - 1, n - kvl + 1, n - kvl - nb + 2))
        return k, i

    def score(n, buf):
        k, i = unit(n)
        buf[...] = nn(qall[k * nb + i].reshape(qrows, HD), k_t[k])

    def weigh(n, buf):
        k, i = unit(n)
        j = k * nb + i
        m = jnp.max(buf[...], axis=1, keepdims=True)
        p = jnp.exp2((buf[...] - m) * factor).astype(BF16)
        oa = nn(p, vaug[k])
        total = oa[:, HD : 2 * HD]
        o = oa[:, 0:HD] / total
        osend[j, 0:zn] = o.astype(BF16).reshape(zn, kr, HD)
        lse = m * factor + jnp.log2(total)
        osend[j, zn] = stat_tile(jnp.sum(jnp.where(eye, lse, 0.0), axis=0, keepdims=True))

        @pl.when(i > 0)
        def _():
            o_copy(j, i).start()

    def o_copy(j, i):
        return rcopy(osend.at[j], orecv.at[j], o_s.at[j], o_r.at[j], minus_dev(i))

    last = kvl * nb - 1

    def queries_here(n):
        k, i = unit(jnp.minimum(n, last))

        @pl.when((i > 0) & (n <= last))
        def _():
            q_copy(k * nb + i, i).wait_recv()

    def attend(t):
        queries_here(2 * t + 1)
        score(2 * t + 1, sbuf[1])
        weigh(2 * t, sbuf[0])

        @pl.when(2 * t + 2 == last - 1)
        def _():
            combine(0)

        queries_here(2 * t + 2)
        score(jnp.minimum(2 * t + 2, last), sbuf[0])
        weigh(2 * t + 1, sbuf[1])

    def z_copies(k):
        return z_group(
            lambda d: rcopy(
                zsend.at[k, z_plus(d)], zrecv.at[k, d], zr_s.at[k * zn + d], zr_r.at[k * zn + d], z_dev(d)
            )
        )

    def combine(k):
        loop(1, nb, lambda i: o_copy(k * nb + i, i).wait_recv())
        orecv[k * nb] = osend[k * nb]
        stats = [stat_row(orecv[k * nb + i, zn]) for i in range(nb)]
        top = functools.reduce(jnp.maximum, stats)
        weights = [jnp.exp2(st - top) for st in stats]
        weight_sum = functools.reduce(jnp.add, weights)
        inverse = 1.0 / weight_sum
        for i in range(nb):
            shares[i : i + 1, :] = weights[i] * inverse

        def add(i, acc):
            share = jnp.where(eye, shares[pl.ds(i, 1), :], 0.0)[:, 0:qrows].astype(BF16)
            return acc + nn(share, orecv[k * nb + i, 0:zn].reshape(qrows, HD))

        acc = lax.fori_loop(0, nb, add, jnp.zeros((qrows, HD), F32))
        zsend[k, :, 0:kr, :] = acc.astype(BF16).reshape(zn, kr, HD)
        tile = stat_tile(top + jnp.log2(weight_sum))
        for d in range(zn):
            zsend[k, d, kr : 2 * kr, :] = tile
        z_copies(k).start()

    mine = iota((kr, LANES), 1) == iota((kr, LANES), 0) + z * kr

    def settle(k, copies):
        received(copies)
        parts = [zsend[k, z]] + [zrecv[k, d] for d in range(1, zn)]
        stats = [stat_row(part[kr : 2 * kr, :]) for part in parts]
        top = functools.reduce(jnp.maximum, stats)
        weights = [jnp.exp2(st - top) for st in stats]
        inverse = 1.0 / functools.reduce(jnp.add, weights)
        acc = jnp.zeros((kr, HD), F32)
        for d in range(zn):
            column = jnp.sum(jnp.where(mine, weights[d] * inverse, 0.0), axis=1, keepdims=True)
            acc = acc + column * parts[d][0:kr, :].astype(F32)
        hz[k, pl.ds(z, 1)] = acc.astype(BF16)[None]
        return z_group(
            lambda d: rcopy(hz.at[k, z], hz.at[k, z], hz_s.at[k * zn + d], hz_r.at[k * zn + d], z_dev(d))
        ).start()

    def spread(k, copies):
        received(copies)
        pieces = nn(regroup_h[...], hz[k].reshape(zn * kr, HD)).astype(BF16)
        for h in range(GROUP):
            hall[k, pl.ds(b, 1), :, h * HD : (h + 1) * HD] = pieces[h * tb : (h + 1) * tb, :][None]
        return plane_group(
            lambda i: rcopy(hall.at[k, b], hall.at[k, b], h2_s.at[k * nb + i], h2_r.at[k * nb + i], plus_dev(i))
        ).start()

    def project(k, copies):
        gain = gain_ref[...].astype(F32)
        def gather(i):
            @pl.when(i > 0)
            def _():
                copies.make(i).wait_recv()

            my, mx = minus(i)
            there = my * xn + mx
            lines = pl.ds(pl.multiple_of(there * tb, tb), tb)
            partial = jnp.zeros((tb, HD), F32)
            for h in range(GROUP):
                piece = hall[k, there, :, h * HD : (h + 1) * HD].astype(F32)
                partial = partial + piece * piece
                head = k * GROUP + h
                gall[lines, head * HD : (head + 1) * HD] = (piece * gain[head : head + 1, :]).astype(BF16)
            squares[lines, :] = partial if k == 0 else squares[lines, :] + partial

        loop(0, nb, gather)
        width = GROUP * HD
        part = nn(gall[:, k * width : (k + 1) * width], ad_t[k * width : (k + 1) * width, :])
        mpre[...] = part if k == 0 else mpre[...] + part

    def turn_adapter(k):
        def turn(h):
            lanes = pl.ds(pl.multiple_of(h * HD, HD), HD)
            for first in range(0, aw, LANES):
                ad_t[lanes, first : first + LANES] = adp[first : first + LANES, lanes].astype(F32).T.astype(BF16)

        loop(k * GROUP, (k + 1) * GROUP, turn)

    score(0, sbuf[0])
    loop(0, kvl * nb // 2, attend)

    regroup_h[...] = regroup(GROUP, zn)
    received(zc)
    pieces = nn(regroup(groups, zn), cz[...].reshape(zn * groups * 2, LANES))
    cg[...] = pieces.astype(BF16).reshape(groups, tb, LANES)
    my_group = div(ctx, per_group)

    def c2_copy(i):
        py, px = plus(i)
        there = div((py * zn + z) * xn + px, per_group)
        return rcopy(cg.at[there], call.at[b], c2_s.at[i], c2_r.at[i], at(py, z, px))

    c2 = plane_group(c2_copy).start()
    call[pl.ds(b, 1)] = cg[pl.ds(my_group, 1)]

    h0 = settle(0, z_copies(0))
    sent(*zq, zc)
    combine(1)
    received(za)
    turn_adapter(0)
    g0 = spread(0, h0)

    sel = iota((rows, rows), 1) == row_of(iota((rows, 1), 0), sizes)
    wanted = jnp.sum(
        jnp.where(sel, jnp.broadcast_to(src_ref[...].astype(F32), (rows, rows)), 0.0),
        axis=1, keepdims=True,
    )
    pick = (wanted == row_of(iota((1, rows), 1), sizes).astype(F32)).astype(F32)
    received(c2)
    cot_rows = nn(pick.T.astype(BF16), call[...].reshape(rows, LANES))
    cot_t[...] = cot_rows.T
    token = iota((nb * 2, 1), 0)
    block = div(token, 2)
    token = 2 * ((div(block, xn) * zn + z) * xn + mod(block, xn)) + mod(token, 2)
    wanted = jnp.sum(
        jnp.where(iota((nb * 2, rows), 1) == token, src_ref[...].astype(F32), 0.0), axis=1, keepdims=True
    )
    pick = (wanted == row_of(iota((1, rows), 1), sizes).astype(F32)).astype(F32)

    h1 = settle(1, z_copies(1))
    turn_adapter(1)
    sent(za, z_copies(0), z_copies(1), c2)
    for k in range(kvl):
        sent(plane_group(lambda i, k=k: q_copy(k * nb + i, i)), plane_group(lambda i, k=k: o_copy(k * nb + i, i)))
    g1 = spread(1, h1)
    project(0, g0)
    sent(h0, h1, g0)
    project(1, g1)

    for first in range(0, aw, LANES):
        mpre_t[first : first + LANES, :] = mpre[:, first : first + LANES].T
    hx[pl.ds(hd, 1), 0:cpd, 0:rows] = mpre_t[own_ad, :][None]
    power = jnp.sum(squares[...].T, axis=0, keepdims=True)
    hx[pl.ds(hd, 1), cpd : cpd + 8, 0:rows] = jnp.broadcast_to(power, (8, rows))[None]
    one_hot = pick.astype(BF16)
    chosen = functools.reduce(jnp.add, [nn(one_hot, term) for term in split3(mpre[...])])
    base = cpd + 8
    for j in range(aw // LANES):
        hx[pl.ds(hd, 1), base + j * 2 * nb : base + (j + 1) * 2 * nb, :] = chosen[
            :, j * LANES : (j + 1) * LANES
        ][None]
    hxc = Copies(
        lambda body: loop(1, heads, body),
        lambda e: rcopy(hx.at[hd], hx.at[hd], hx_s.at[e], hx_r.at[e], (ctx, mod(hd + e, heads))),
    ).start()
    sent(g1)
    received(hxc)
    summed = hx[0]
    for e in range(1, heads):
        summed = summed + hx[e]
    scale = lax.rsqrt(summed[cpd : cpd + 1, 0:rows] / eps_div + 1e-05)

    token_scale = jnp.sum(pick * scale, axis=1, keepdims=True)
    for j in range(aw // LANES):
        pre = token_scale * summed[base + j * 2 * nb : base + (j + 1) * 2 * nb, :]
        out = pre / (1.0 + jnp.exp(-pre))
        for d in range(nb):
            st1s[d, 0:2, j * LANES : (j + 1) * LANES] = out[2 * d : 2 * d + 2, :]

    def s1_copy(i):
        py, px = plus(i)
        return rcopy(st1s.at[py * xn + px], st1r.at[b], s1_s.at[i], s1_r.at[i], at(py, z, px))

    s1 = plane_group(s1_copy).start()
    st1r[pl.ds(b, 1)] = st1s[pl.ds(b, 1)]
    sent(hxc)

    pre = scale * summed[0:cpd, 0:rows]
    sig = 1.0 / (1.0 + jnp.exp(-pre))
    own = pl.multiple_of(mod(ctx, per_group) * cpd, cpd)
    slope = (cot_t[pl.ds(own, cpd), :] * sig * (1.0 + pre * (1.0 - sig)) * scale).astype(BF16)
    grad_ref[...] = nn(slope, gall[...]) * (rows ** -0.5)

    sent(s1)
    received(s1)
    for py in range(yn):
        tile = st1r[py * xn]
        for px in range(1, xn):
            tile = tile + st1r[py * xn + px]
        stu_ref[:, py * aw : (py + 1) * aw] = tile[0:2, :]


def local(sizes, heads, queries, keys, values, norm_gain, adapter, source_row, cotangent):
    yn, zn, xn = sizes
    nb = yn * xn
    tb = 2 * zn
    rows = nb * tb
    positions, kvw = keys.shape
    kvl = kvw // HD
    nh = kvl * GROUP
    nf = nh * HD
    kr = GROUP * 2
    cpd = adapter.shape[0]
    aw = zn * xn * cpd
    groups = cotangent.shape[1] // LANES
    vm = pltpu.VMEM
    dma = pltpu.SemaphoreType.DMA
    scratch = [
        vm(queries.shape, BF16),
        vm((nh, HD), BF16),
        vm((1, rows), jnp.int32),
        vm(cotangent.shape, BF16),
        vm((positions, kvw), BF16),
        vm((kvl, HD, positions), BF16),
        vm((kvl, positions, 2 * HD), BF16),
        vm((kvl * nb, zn, kr, HD), BF16),
        vm((kvl * nb, zn + 1, kr, HD), BF16),
        vm((kvl * nb, zn + 1, kr, HD), BF16),
        vm((kvl, zn, 2 * kr, HD), BF16),
        vm((kvl, zn, 2 * kr, HD), BF16),
        vm((kvl, zn, kr, HD), BF16),
        vm((kvl, nb, tb, GROUP * HD), BF16),
        vm((rows, nf), BF16),
        vm((rows, aw), F32),
        vm((rows, HD), F32),
        vm((heads, cpd + 8 + 2 * nb * (aw // LANES), max(rows, LANES)), F32),
        vm((zn * kr, positions), F32),
        vm((zn * kr, positions), F32),
        vm((nb, LANES), F32),
        vm((zn * kr, zn * kr), BF16),
        vm((zn, groups * 2, LANES), BF16),
        vm((groups, tb, LANES), BF16),
        vm((nb, tb, LANES), BF16),
        vm((LANES, rows), F32),
        vm((aw, rows), F32),
        vm((nb, 8, aw), F32),
        vm((nb, 8, aw), F32),
        vm((aw, nf), BF16),
        vm((nf, aw), BF16),
        dma((6 + kvl,)),
        dma((kvl * zn,)), dma((kvl * zn,)), dma((kvl * nb,)), dma((kvl * nb,)),
        dma((zn,)), dma((zn,)), dma((nb,)), dma((nb,)),
        dma((kvl * nb,)), dma((kvl * nb,)),
        dma((kvl * zn,)), dma((kvl * zn,)), dma((kvl * zn,)), dma((kvl * zn,)),
        dma((kvl * nb,)), dma((kvl * nb,)),
        dma((heads,)), dma((heads,)),
        dma((nb,)), dma((nb,)), dma((zn,)), dma((zn,)),
    ]
    args = (queries, keys, values, norm_gain.reshape(nh, HD), adapter, source_row.reshape(1, -1), cotangent)
    vmem = pl.BlockSpec(memory_space=pltpu.VMEM)
    hbm = pl.BlockSpec(memory_space=pltpu.HBM)
    return pl.pallas_call(
        functools.partial(kernel, sizes, heads, float(heads * nf)),
        out_shape=(
            pltpu.VMEM(cotangent.shape, F32),
            pltpu.VMEM(adapter.shape, F32),
        ),
        in_specs=[hbm] * 7,
        out_specs=(vmem, vmem),
        scratch_shapes=scratch,
        compiler_params=pltpu.CompilerParams(
            collective_id=0, has_side_effects=True, vmem_limit_bytes=48 * 1024 * 1024
        ),
        cost_estimate=pl.CostEstimate(
            flops=4 * rows * nh * HD * positions,
            bytes_accessed=4 * positions * kvw,
            transcendentals=rows * nh * positions,
        ),
        name="distill",
    )(*(pltpu.with_memory_space_constraint(arg, pltpu.HBM) for arg in args))


def solution(mesh, sizes=(YN, ZN, XN)):
    return jax.shard_map(
        functools.partial(local, sizes, mesh.shape["head"]),
        mesh=mesh,
        in_specs=(
            P("ctx", "head"),
            P("ctx", "head"),
            P("ctx", "head"),
            P("head"),
            P("ctx", "head"),
            P(),
            P("ctx", None),
        ),
        out_specs=(P("ctx", None), P("ctx", "head")),
        check_vma=False,
    )
```

```python
import functools

import jax
import jax.numpy as jnp
from jax import lax
from jax.experimental import pallas as pl
from jax.experimental.pallas import tpu as pltpu
from jax.sharding import PartitionSpec as P

H = 64
HD = 128
GROUP = 8
LANES = 128
LOG2E = 1.4426950408889634
YN, ZN, XN = 4, 8, 2

F32 = jnp.float32
BF16 = jnp.bfloat16
MESH = pl.DeviceIdType.MESH


def iota(shape, axis):
    return lax.broadcasted_iota(jnp.int32, shape, axis)


def nn(left, right):
    return lax.dot_general(left, right, (((1,), (0,)), ((), ())), preferred_element_type=F32)


def div(a, n):
    return a // n if isinstance(a, int) else a >> (n.bit_length() - 1)


def mod(a, n):
    return a % n if isinstance(a, int) else a & (n - 1)


def regroup(outer, zn):
    size = outer * zn * 2
    row, col = iota((size, 1), 0), iota((size, size), 1)
    head, rest = div(row, 2 * zn), mod(row, 2 * zn)
    return (col == div(rest, 2) * (2 * outer) + head * 2 + mod(rest, 2)).astype(F32).astype(BF16)


def row_of(position, sizes):
    yn, zn, xn = sizes
    pair, block = div(position, 2), div(position, 2 * zn)
    ctx = (div(block, xn) * zn + mod(pair, zn)) * xn + mod(block, xn)
    return 2 * ctx + mod(position, 2)


def split3(value):
    high = value.astype(BF16)
    rest = value - high.astype(F32)
    middle = rest.astype(BF16)
    return high, middle, (rest - middle.astype(F32)).astype(BF16)


def kernel(sizes, heads, eps_div, q_hbm, k_hbm, v_hbm, gain_hbm, ad_hbm, src_hbm, cot_hbm,
           stu_ref, grad_ref,
           q_ref, gain_ref, src_ref, cot_ref, kbuf, k_t, vaug, qall, osend, orecv, zsend, zrecv,
           hz, hall, gall, mpre, squares, hx, s_even, s_odd, regroup_h, cz, cg, call, cot_t, mpre_t, st1s, st1r,
           adp, ad_t,
           loc_sem, zq_s, zq_r, q2_s, q2_r, zc_s, zc_r, c2_s, c2_r, o_s, o_r,
           zr_s, zr_r, hz_s, hz_r, h2_s, h2_r, hx_s, hx_r, s1_s, s1_r, za_s, za_r):
    sbuf = (s_even, s_odd)
    yn, zn, xn = sizes
    nb = yn * xn
    tb = 2 * zn
    rows = nb * tb
    kvl = k_hbm.shape[1] // HD
    nh = kvl * GROUP
    kr = GROUP * 2
    cpd = ad_hbm.shape[0]
    per_group = LANES // cpd
    aw = zn * xn * cpd
    groups = cot_hbm.shape[1] // LANES

    ctx = lax.axis_index("ctx")
    hd = lax.axis_index("head")
    y = div(ctx, zn * xn)
    z = mod(div(ctx, xn), zn)
    x = mod(ctx, xn)
    b = y * xn + x

    def at(y_, z_, x_):
        return ((y_ * zn + z_) * xn + x_, hd)

    def z_plus(d):
        return mod(z + d, zn)

    ring = sorted(range(1, zn), key=lambda d: -min(d, zn - d))

    def z_dev(d):
        return at(y, z_plus(d), x)

    def steps(i):
        far, turn = div(i, yn), mod(i, yn)
        if isinstance(i, int):
            near = (0, 1, 3, 2)[turn] if yn == 4 else turn
            return (near if far == 0 else (2, 1, 3, 0)[turn] if yn == 4 else yn - 1 - turn), far
        if yn == 4:
            first = jnp.where(turn == 2, 3, jnp.where(turn == 3, 2, turn))
            second = jnp.where(turn == 0, 2, jnp.where(turn == 1, 1, jnp.where(turn == 2, 3, 0)))
        else:
            first, second = turn, yn - 1 - turn
        return jnp.where(far == 0, first, second), far

    def plus(i):
        dy, dx = steps(i)
        return mod(y + dy, yn), mod(x + dx, xn)

    def minus(i):
        dy, dx = steps(i)
        return mod(y + yn - dy, yn), mod(x + xn - dx, xn)

    def plus_dev(i):
        py, px = plus(i)
        return at(py, z, px)

    def minus_dev(i):
        py, px = minus(i)
        return at(py, z, px)

    def rcopy(src, dst, ssem, rsem, dev):
        return pltpu.make_async_remote_copy(
            src_ref=src, dst_ref=dst, send_sem=ssem, recv_sem=rsem, device_id=dev, device_id_type=MESH
        )

    q_load = pltpu.make_async_copy(q_hbm, q_ref, loc_sem.at[0])
    q_load.start()
    barrier = pltpu.get_barrier_semaphore()
    partners = (
        [z_dev(d) for d in range(1, zn)]
        + [plus_dev(i) for i in range(1, nb)]
        + [(ctx, mod(hd + e, heads)) for e in range(1, heads)]
    )
    for dev in partners:
        pl.semaphore_signal(barrier, inc=1, device_id=dev, device_id_type=MESH)

    cot_load = pltpu.make_async_copy(cot_hbm, cot_ref, loc_sem.at[1])
    k_load = pltpu.make_async_copy(k_hbm, kbuf, loc_sem.at[2])
    own_ad = pl.ds(pl.multiple_of((z * xn + x) * cpd, cpd), cpd)
    ad_load = pltpu.make_async_copy(ad_hbm, adp.at[own_ad], loc_sem.at[3])
    late_loads = [
        pltpu.make_async_copy(gain_hbm, gain_ref, loc_sem.at[4]),
        pltpu.make_async_copy(src_hbm, src_ref, loc_sem.at[5]),
    ]
    for k in range(kvl):
        late_loads.append(
            pltpu.make_async_copy(
                v_hbm.at[:, k * HD : (k + 1) * HD], vaug.at[k, :, 0:HD], loc_sem.at[6 + k]
            )
        )
    for load in [cot_load, k_load, ad_load] + late_loads:
        load.start()

    q_load.wait()
    qf = q_ref[...].astype(F32)
    for k in range(kvl):
        qall[k * nb, pl.ds(z, 1)] = jnp.concatenate(
            [qf[:, (k * GROUP + h) * HD : (k * GROUP + h + 1) * HD] for h in range(GROUP)], axis=0
        ).astype(BF16)[None]
    cot_load.wait()
    cf = cot_ref[...].astype(F32)
    cz[pl.ds(z, 1)] = jnp.concatenate(
        [cf[:, g * LANES : (g + 1) * LANES] for g in range(groups)], axis=0
    ).astype(BF16)[None]
    pl.semaphore_wait(barrier, len(partners))

    def z_group(make):
        copies = {d: make(d) for d in ring}
        for copy in copies.values():
            copy.start()
        return copies

    def received(copies):
        for copy in copies.values():
            copy.wait_recv()

    def sent(*groups_of_copies):
        for copies in groups_of_copies:
            for copy in copies.values():
                copy.wait_send()

    zq = [
        z_group(
            lambda d, k=k: rcopy(
                qall.at[k * nb, z], qall.at[k * nb, z], zq_s.at[k * zn + d], zq_r.at[k * zn + d], z_dev(d)
            )
        )
        for k in range(kvl)
    ]
    zc = z_group(lambda d: rcopy(cz.at[z], cz.at[z], zc_s.at[d], zc_r.at[d], z_dev(d)))

    k_load.wait()
    for k in range(kvl):
        k_t[k] = kbuf[:, k * HD : (k + 1) * HD].astype(F32).T.astype(BF16)
    for k in range(kvl):
        vaug[k, :, HD : 2 * HD] = jnp.ones((vaug.shape[1], HD), BF16)

    def q_copy(j, i):
        return rcopy(qall.at[j - i], qall.at[j], q2_s.at[j], q2_r.at[j], plus_dev(i))

    for k in range(kvl):
        received(zq[k])
        for i in range(1, nb):
            q_copy(k * nb + i, i).start()

    for d in range(zn):
        for e in range(1, xn):
            other = pl.multiple_of((d * xn + mod(x + e, xn)) * cpd, cpd)
            adp[pl.ds(other, cpd), :] = jnp.zeros((cpd, nh * HD), BF16)
    st1s[...] = jnp.zeros_like(st1s)
    ad_load.wait()
    za = z_group(lambda d: rcopy(adp.at[own_ad], adp.at[own_ad], za_s.at[d], za_r.at[d], z_dev(d)))
    for load in late_loads:
        load.wait()

    factor = (HD ** -0.5) * LOG2E
    qrows = zn * kr
    eye = iota((qrows, LANES), 0) == iota((qrows, LANES), 1)

    def stat_tile(row):
        high, middle, low = split3(row)
        line = iota((kr, LANES), 0)
        tile = jnp.where(line == 0, high.astype(F32), jnp.where(line == 1, middle.astype(F32), low.astype(F32)))
        return jnp.where(line < 3, tile, 0.0).astype(BF16)

    def stat_row(tile):
        wide = tile.astype(F32)
        return wide[0:1, :] + wide[1:2, :] + wide[2:3, :]

    def score(k, i, count, buf):
        q = qall[pl.ds(k * nb + i, count)].reshape(count * qrows, HD)
        buf[0 : count * qrows, :] = nn(q, k_t[k])

    def weigh(k, i, count, buf):
        s = buf[0 : count * qrows, :]
        m = jnp.max(s, axis=1, keepdims=True)
        p = jnp.exp2((buf[0 : count * qrows, :] - m) * factor).astype(BF16)
        oa = nn(p, vaug[k])
        total = oa[:, HD : 2 * HD]
        o = (oa[:, 0:HD] / total).astype(BF16)
        lse = m * factor + jnp.log2(total)
        for c in range(count):
            part = slice(c * qrows, (c + 1) * qrows)
            osend[k * nb + i + c, 0:zn] = o[part].reshape(zn, kr, HD)
            row = jnp.sum(jnp.where(eye, lse[part], 0.0), axis=0, keepdims=True)
            osend[k * nb + i + c, zn] = stat_tile(row)
            if i + c > 0:
                o_copy(k * nb + i + c, i + c).start()

    def o_copy(j, i):
        return rcopy(osend.at[j], orecv.at[j], o_s.at[j], o_r.at[j], minus_dev(i))

    units = [(1, 1)] + [(i, 2) for i in range(2, nb, 2)]

    def queries_here(k, i, count):
        for c in range(count):
            q_copy(k * nb + i + c, i + c).wait_recv()

    def attend(k, carry):
        for n, (i, count) in enumerate(units):
            here, there = sbuf[n % 2], sbuf[(n + 1) % 2]
            if n + 1 < len(units):
                queries_here(k, *units[n + 1])
                score(k, *units[n + 1], there)
                weigh(k, i, count, here)
            else:

                @pl.when(k == 1)
                def _():
                    combine(0)

                later = jnp.minimum(k + 1, kvl - 1)

                @pl.when(k + 1 < kvl)
                def _():
                    queries_here(later, *units[0])

                score(later, *units[0], there)
                weigh(k, i, count, here)
        return carry

    def z_copies(k):
        return {
            d: rcopy(zsend.at[k, z_plus(d)], zrecv.at[k, d], zr_s.at[k * zn + d], zr_r.at[k * zn + d], z_dev(d))
            for d in ring
        }

    def combine(k):
        for i in range(1, nb):
            o_copy(k * nb + i, i).wait_recv()
        parts = [(osend if i == 0 else orecv).at[k * nb + i] for i in range(nb)]
        stats = [stat_row(part[zn]) for part in parts]
        top = functools.reduce(jnp.maximum, stats)
        weights = [jnp.exp2(st - top) for st in stats]
        weight_sum = functools.reduce(jnp.add, weights)
        inverse = 1.0 / weight_sum
        acc = jnp.zeros((qrows, HD), F32)
        for i in range(nb):
            share = jnp.where(eye, weights[i] * inverse, 0.0)[:, 0:qrows].astype(BF16)
            acc = acc + nn(share, parts[i][0:zn].reshape(qrows, HD))
        zsend[k, :, 0:kr, :] = acc.astype(BF16).reshape(zn, kr, HD)
        tile = stat_tile(top + jnp.log2(weight_sum))
        for d in range(zn):
            zsend[k, d, kr : 2 * kr, :] = tile
        for copy in z_copies(k).values():
            copy.start()

    mine = iota((kr, LANES), 1) == iota((kr, LANES), 0) + z * kr

    def settle(k, copies):
        received(copies)
        parts = [zsend[k, z]] + [zrecv[k, d] for d in range(1, zn)]
        stats = [stat_row(part[kr : 2 * kr, :]) for part in parts]
        top = functools.reduce(jnp.maximum, stats)
        weights = [jnp.exp2(st - top) for st in stats]
        inverse = 1.0 / functools.reduce(jnp.add, weights)
        acc = jnp.zeros((kr, HD), F32)
        for d in range(zn):
            column = jnp.sum(jnp.where(mine, weights[d] * inverse, 0.0), axis=1, keepdims=True)
            acc = acc + column * parts[d][0:kr, :].astype(F32)
        hz[k, pl.ds(z, 1)] = acc.astype(BF16)[None]
        return z_group(
            lambda d: rcopy(hz.at[k, z], hz.at[k, z], hz_s.at[k * zn + d], hz_r.at[k * zn + d], z_dev(d))
        )

    def spread(k, copies):
        received(copies)
        pieces = nn(regroup_h[...], hz[k].reshape(zn * kr, HD)).astype(BF16)
        for h in range(GROUP):
            hall[k, pl.ds(b, 1), :, h * HD : (h + 1) * HD] = pieces[h * tb : (h + 1) * tb, :][None]
        copies = {
            i: rcopy(hall.at[k, b], hall.at[k, b], h2_s.at[k * nb + i], h2_r.at[k * nb + i], plus_dev(i))
            for i in range(1, nb)
        }
        for copy in copies.values():
            copy.start()
        return copies

    def project(k, copies):
        gain = gain_ref[...].astype(F32)
        for i in range(nb):
            if i > 0:
                copies[i].wait_recv()
            my, mx = minus(i)
            there = my * xn + mx
            hidden = hall[k, there].astype(F32)
            lines = pl.ds(pl.multiple_of(there * tb, tb), tb)
            partial = jnp.zeros((tb, HD), F32)
            for h in range(GROUP):
                piece = hidden[:, h * HD : (h + 1) * HD]
                partial = partial + piece * piece
                head = k * GROUP + h
                gall[lines, head * HD : (head + 1) * HD] = (piece * gain[head : head + 1, :]).astype(BF16)
            squares[lines, :] = partial if k == 0 else squares[lines, :] + partial
        width = GROUP * HD
        part = nn(gall[:, k * width : (k + 1) * width], ad_t[k * width : (k + 1) * width, :])
        mpre[...] = part if k == 0 else mpre[...] + part

    def turn_adapter(k):
        for h in range(k * GROUP, (k + 1) * GROUP):
            for first in range(0, aw, LANES):
                ad_t[h * HD : (h + 1) * HD, first : first + LANES] = (
                    adp[first : first + LANES, h * HD : (h + 1) * HD].astype(F32).T.astype(BF16)
                )

    score(0, 0, 1, sbuf[0])
    score(1, 0, 1, sbuf[1])
    weigh(0, 0, 1, sbuf[0])
    queries_here(0, *units[0])
    score(0, *units[0], sbuf[0])
    weigh(1, 0, 1, sbuf[1])
    lax.fori_loop(0, kvl, attend, 0)

    regroup_h[...] = regroup(GROUP, zn)
    received(zc)
    pieces = nn(regroup(groups, zn), cz[...].reshape(zn * groups * 2, LANES))
    cg[...] = pieces.astype(BF16).reshape(groups, tb, LANES)
    my_group = div(ctx, per_group)
    c2 = {}
    for i in range(1, nb):
        py, px = plus(i)
        there = div((py * zn + z) * xn + px, per_group)
        c2[i] = rcopy(cg.at[there], call.at[b], c2_s.at[i], c2_r.at[i], at(py, z, px))
        c2[i].start()
    call[pl.ds(b, 1)] = cg[pl.ds(my_group, 1)]

    combine(1)
    sent(*zq, zc)
    h0 = settle(0, z_copies(0))
    received(za)
    turn_adapter(0)

    sel = iota((rows, rows), 1) == row_of(iota((rows, 1), 0), sizes)
    wanted = jnp.sum(
        jnp.where(sel, jnp.broadcast_to(src_ref[...].astype(F32), (rows, rows)), 0.0),
        axis=1, keepdims=True,
    )
    pick = (wanted == row_of(iota((1, rows), 1), sizes).astype(F32)).astype(F32)
    received(c2)
    cot_rows = nn(pick.T.astype(BF16), call[...].reshape(rows, LANES))
    cot_t[...] = cot_rows.T
    token = iota((nb * 2, 1), 0)
    block = div(token, 2)
    token = 2 * ((div(block, xn) * zn + z) * xn + mod(block, xn)) + mod(token, 2)
    wanted = jnp.sum(
        jnp.where(iota((nb * 2, rows), 1) == token, src_ref[...].astype(F32), 0.0), axis=1, keepdims=True
    )
    pick = (wanted == row_of(iota((1, rows), 1), sizes).astype(F32)).astype(F32)

    h1 = settle(1, z_copies(1))
    g0 = spread(0, h0)
    turn_adapter(1)
    sent(za, z_copies(0), z_copies(1), c2)
    for j in range(kvl * nb):
        if j % nb:
            q_copy(j, j % nb).wait_send()
            o_copy(j, j % nb).wait_send()
    g1 = spread(1, h1)
    project(0, g0)
    sent(h0, h1, g0)
    project(1, g1)

    for first in range(0, aw, LANES):
        mpre_t[first : first + LANES, :] = mpre[:, first : first + LANES].T
    hx[pl.ds(hd, 1), 0:cpd, 0:rows] = mpre_t[own_ad, :][None]
    power = jnp.sum(squares[...].T, axis=0, keepdims=True)
    hx[pl.ds(hd, 1), cpd : cpd + 8, 0:rows] = jnp.broadcast_to(power, (8, rows))[None]
    one_hot = pick.astype(BF16)
    chosen = functools.reduce(jnp.add, [nn(one_hot, term) for term in split3(mpre[...])])
    base = cpd + 8
    for j in range(aw // LANES):
        hx[pl.ds(hd, 1), base + j * 2 * nb : base + (j + 1) * 2 * nb, :] = chosen[
            :, j * LANES : (j + 1) * LANES
        ][None]
    hxc = {}
    for e in range(1, heads):
        hxc[e] = rcopy(hx.at[hd], hx.at[hd], hx_s.at[e], hx_r.at[e], (ctx, mod(hd + e, heads)))
        hxc[e].start()
    sent(g1)
    received(hxc)
    summed = hx[0]
    for e in range(1, heads):
        summed = summed + hx[e]
    scale = lax.rsqrt(summed[cpd : cpd + 1, 0:rows] / eps_div + 1e-05)

    token_scale = jnp.sum(pick * scale, axis=1, keepdims=True)
    for j in range(aw // LANES):
        pre = token_scale * summed[base + j * 2 * nb : base + (j + 1) * 2 * nb, :]
        out = pre / (1.0 + jnp.exp(-pre))
        for d in range(nb):
            st1s[d, 0:2, j * LANES : (j + 1) * LANES] = out[2 * d : 2 * d + 2, :]
    s1 = {}
    for i in range(1, nb):
        py, px = plus(i)
        s1[i] = rcopy(st1s.at[py * xn + px], st1r.at[b], s1_s.at[i], s1_r.at[i], at(py, z, px))
        s1[i].start()
    st1r[pl.ds(b, 1)] = st1s[pl.ds(b, 1)]
    sent(hxc)

    pre = scale * summed[0:cpd, 0:rows]
    sig = 1.0 / (1.0 + jnp.exp(-pre))
    own = pl.multiple_of(mod(ctx, per_group) * cpd, cpd)
    slope = (cot_t[pl.ds(own, cpd), :] * sig * (1.0 + pre * (1.0 - sig)) * scale).astype(BF16)
    grad_ref[...] = nn(slope, gall[...]) * (rows ** -0.5)

    sent(s1)
    received(s1)
    for py in range(yn):
        tile = st1r[py * xn]
        for px in range(1, xn):
            tile = tile + st1r[py * xn + px]
        stu_ref[:, py * aw : (py + 1) * aw] = tile[0:2, :]


def local(sizes, heads, queries, keys, values, norm_gain, adapter, source_row, cotangent):
    yn, zn, xn = sizes
    nb = yn * xn
    tb = 2 * zn
    rows = nb * tb
    positions, kvw = keys.shape
    kvl = kvw // HD
    nh = kvl * GROUP
    nf = nh * HD
    kr = GROUP * 2
    cpd = adapter.shape[0]
    aw = zn * xn * cpd
    groups = cotangent.shape[1] // LANES
    vm = pltpu.VMEM
    dma = pltpu.SemaphoreType.DMA
    scratch = [
        vm(queries.shape, BF16),
        vm((nh, HD), BF16),
        vm((1, rows), jnp.int32),
        vm(cotangent.shape, BF16),
        vm((positions, kvw), BF16),
        vm((kvl, HD, positions), BF16),
        vm((kvl, positions, 2 * HD), BF16),
        vm((kvl * nb, zn, kr, HD), BF16),
        vm((kvl * nb, zn + 1, kr, HD), BF16),
        vm((kvl * nb, zn + 1, kr, HD), BF16),
        vm((kvl, zn, 2 * kr, HD), BF16),
        vm((kvl, zn, 2 * kr, HD), BF16),
        vm((kvl, zn, kr, HD), BF16),
        vm((kvl, nb, tb, GROUP * HD), BF16),
        vm((rows, nf), BF16),
        vm((rows, aw), F32),
        vm((rows, HD), F32),
        vm((heads, cpd + 8 + 2 * nb * (aw // LANES), max(rows, LANES)), F32),
        vm((2 * zn * kr, positions), F32),
        vm((2 * zn * kr, positions), F32),
        vm((zn * kr, zn * kr), BF16),
        vm((zn, groups * 2, LANES), BF16),
        vm((groups, tb, LANES), BF16),
        vm((nb, tb, LANES), BF16),
        vm((LANES, rows), F32),
        vm((aw, rows), F32),
        vm((nb, 8, aw), F32),
        vm((nb, 8, aw), F32),
        vm((aw, nf), BF16),
        vm((nf, aw), BF16),
        dma((6 + kvl,)),
        dma((kvl * zn,)), dma((kvl * zn,)), dma((kvl * nb,)), dma((kvl * nb,)),
        dma((zn,)), dma((zn,)), dma((nb,)), dma((nb,)),
        dma((kvl * nb,)), dma((kvl * nb,)),
        dma((kvl * zn,)), dma((kvl * zn,)), dma((kvl * zn,)), dma((kvl * zn,)),
        dma((kvl * nb,)), dma((kvl * nb,)),
        dma((heads,)), dma((heads,)),
        dma((nb,)), dma((nb,)), dma((zn,)), dma((zn,)),
    ]
    args = (queries, keys, values, norm_gain.reshape(nh, HD), adapter, source_row.reshape(1, -1), cotangent)
    vmem = pl.BlockSpec(memory_space=pltpu.VMEM)
    hbm = pl.BlockSpec(memory_space=pltpu.HBM)
    return pl.pallas_call(
        functools.partial(kernel, sizes, heads, float(heads * nf)),
        out_shape=(
            pltpu.VMEM(cotangent.shape, F32),
            pltpu.VMEM(adapter.shape, F32),
        ),
        in_specs=[hbm] * 7,
        out_specs=(vmem, vmem),
        scratch_shapes=scratch,
        compiler_params=pltpu.CompilerParams(
            collective_id=0, has_side_effects=True, vmem_limit_bytes=48 * 1024 * 1024
        ),
        cost_estimate=pl.CostEstimate(
            flops=4 * rows * nh * HD * positions,
            bytes_accessed=4 * positions * kvw,
            transcendentals=rows * nh * positions,
        ),
        name="distill",
    )(*(pltpu.with_memory_space_constraint(arg, pltpu.HBM) for arg in args))


def solution(mesh, sizes=(YN, ZN, XN)):
    return jax.shard_map(
        functools.partial(local, sizes, mesh.shape["head"]),
        mesh=mesh,
        in_specs=(
            P("ctx", "head"),
            P("ctx", "head"),
            P("ctx", "head"),
            P("head"),
            P("ctx", "head"),
            P(),
            P("ctx", None),
        ),
        out_specs=(P("ctx", None), P("ctx", "head")),
        check_vma=False,
    )
```

```python
import functools

import jax
import jax.numpy as jnp
from jax import lax
from jax.experimental import pallas as pl
from jax.experimental.pallas import tpu as pltpu
from jax.sharding import PartitionSpec as P

H = 64
HD = 128
GROUP = 8
LANES = 128
LOG2E = 1.4426950408889634
YN, ZN, XN = 4, 8, 2

F32 = jnp.float32
BF16 = jnp.bfloat16
MESH = pl.DeviceIdType.MESH


def iota(shape, axis):
    return lax.broadcasted_iota(jnp.int32, shape, axis)


def nn(left, right):
    return lax.dot_general(left, right, (((1,), (0,)), ((), ())), preferred_element_type=F32)


def div(a, n):
    return a // n if isinstance(a, int) else a >> (n.bit_length() - 1)


def mod(a, n):
    return a % n if isinstance(a, int) else a & (n - 1)


def regroup(outer, zn):
    size = outer * zn * 2
    row, col = iota((size, 1), 0), iota((size, size), 1)
    head, rest = div(row, 2 * zn), mod(row, 2 * zn)
    return (col == div(rest, 2) * (2 * outer) + head * 2 + mod(rest, 2)).astype(F32).astype(BF16)


def row_of(position, sizes):
    yn, zn, xn = sizes
    pair, block = div(position, 2), div(position, 2 * zn)
    ctx = (div(block, xn) * zn + mod(pair, zn)) * xn + mod(block, xn)
    return 2 * ctx + mod(position, 2)


def split3(value):
    high = value.astype(BF16)
    rest = value - high.astype(F32)
    middle = rest.astype(BF16)
    return high, middle, (rest - middle.astype(F32)).astype(BF16)


def kernel(sizes, heads, eps_div, q_hbm, k_hbm, v_hbm, gain_hbm, ad_hbm, src_hbm, cot_hbm,
           stu_ref, grad_ref,
           q_ref, gain_ref, src_ref, cot_ref, kbuf, k_t, vaug, qall, osend, orecv, zsend, zrecv,
           hz, hall, gall, mpre, squares, hx, s_even, s_odd, rowbuf, regroup_h, cz, cg, call, cot_t, mpre_t, st1s, st1r,
           adp, ad_t,
           loc_sem, zq_s, zq_r, q2_s, q2_r, zc_s, zc_r, c2_s, c2_r, o_s, o_r,
           zr_s, zr_r, hz_s, hz_r, h2_s, h2_r, hx_s, hx_r, s1_s, s1_r, za_s, za_r):
    sbuf = (s_even, s_odd)
    yn, zn, xn = sizes
    nb = yn * xn
    tb = 2 * zn
    rows = nb * tb
    kvl = k_hbm.shape[1] // HD
    nh = kvl * GROUP
    kr = GROUP * 2
    cpd = ad_hbm.shape[0]
    per_group = LANES // cpd
    aw = zn * xn * cpd
    groups = cot_hbm.shape[1] // LANES

    ctx = lax.axis_index("ctx")
    hd = lax.axis_index("head")
    y = div(ctx, zn * xn)
    z = mod(div(ctx, xn), zn)
    x = mod(ctx, xn)
    b = y * xn + x

    def at(y_, z_, x_):
        return ((y_ * zn + z_) * xn + x_, hd)

    def z_plus(d):
        return mod(z + d, zn)

    ring = sorted(range(1, zn), key=lambda d: -min(d, zn - d))

    def z_dev(d):
        return at(y, z_plus(d), x)

    steps = sorted(
        ((dy, dx) for dy in range(yn) for dx in range(xn)), key=lambda st: (min(st[0], yn - st[0]) + st[1], st[1], st[0])
    )
    far_first = range(nb - 1, 0, -1)
    planes = sorted(range(zn), key=lambda d: (min(d, zn - d), d))
    near = 1 + 2 * (zn // 4)
    parts_of = ((0, near), (near, zn))

    def plus(i):
        dy, dx = steps[i]
        return mod(y + dy, yn), mod(x + dx, xn)

    def minus(i):
        dy, dx = steps[i]
        return mod(y + yn - dy, yn), mod(x + xn - dx, xn)

    def plus_dev(i):
        py, px = plus(i)
        return at(py, z, px)

    def minus_dev(i):
        py, px = minus(i)
        return at(py, z, px)

    def rcopy(src, dst, ssem, rsem, dev):
        return pltpu.make_async_remote_copy(
            src_ref=src, dst_ref=dst, send_sem=ssem, recv_sem=rsem, device_id=dev, device_id_type=MESH
        )

    q_load = pltpu.make_async_copy(q_hbm, q_ref, loc_sem.at[0])
    q_load.start()
    barrier = pltpu.get_barrier_semaphore()
    partners = (
        [z_dev(d) for d in range(1, zn)]
        + [plus_dev(i) for i in range(1, nb)]
        + [(ctx, mod(hd + e, heads)) for e in range(1, heads)]
    )
    for dev in partners:
        pl.semaphore_signal(barrier, inc=1, device_id=dev, device_id_type=MESH)

    cot_load = pltpu.make_async_copy(cot_hbm, cot_ref, loc_sem.at[1])
    k_load = pltpu.make_async_copy(k_hbm, kbuf, loc_sem.at[2])
    own_ad = pl.ds(pl.multiple_of((z * xn + x) * cpd, cpd), cpd)
    ad_load = pltpu.make_async_copy(ad_hbm, adp.at[own_ad], loc_sem.at[3])
    late_loads = [
        pltpu.make_async_copy(gain_hbm, gain_ref, loc_sem.at[4]),
        pltpu.make_async_copy(src_hbm, src_ref, loc_sem.at[5]),
    ]
    for k in range(kvl):
        late_loads.append(
            pltpu.make_async_copy(
                v_hbm.at[:, k * HD : (k + 1) * HD], vaug.at[k, :, 0:HD], loc_sem.at[6 + k]
            )
        )
    for load in [cot_load, k_load, ad_load] + late_loads:
        load.start()

    q_load.wait()
    qf = q_ref[...].astype(F32)
    for k in range(kvl):
        qall[k * nb, 0] = jnp.concatenate(
            [qf[:, (k * GROUP + h) * HD : (k * GROUP + h + 1) * HD] for h in range(GROUP)], axis=0
        ).astype(BF16)
    cot_load.wait()
    cf = cot_ref[...].astype(F32)
    cz[pl.ds(z, 1)] = jnp.concatenate(
        [cf[:, g * LANES : (g + 1) * LANES] for g in range(groups)], axis=0
    ).astype(BF16)[None]
    pl.semaphore_wait(barrier, len(partners))

    def z_group(make):
        copies = {d: make(d) for d in ring}
        for copy in copies.values():
            copy.start()
        return copies

    def received(copies):
        for copy in copies.values():
            copy.wait_recv()

    def sent(*groups_of_copies):
        for copies in groups_of_copies:
            for copy in copies.values():
                copy.wait_send()

    def zq_copy(k, d):
        slot = planes.index((zn - d) % zn)
        return rcopy(
            qall.at[k * nb, 0], qall.at[k * nb, slot], zq_s.at[k * zn + d], zq_r.at[k * zn + d], z_dev(d)
        )

    zq = [z_group(lambda d, k=k: zq_copy(k, d)) for k in range(kvl)]
    zc = z_group(lambda d: rcopy(cz.at[z], cz.at[z], zc_s.at[d], zc_r.at[d], z_dev(d)))

    k_load.wait()
    for k in range(kvl):
        k_t[k] = kbuf[:, k * HD : (k + 1) * HD].astype(F32).T.astype(BF16)
    for k in range(kvl):
        vaug[k, :, HD : 2 * HD] = jnp.ones((vaug.shape[1], HD), BF16)

    def q_copy(part, j, i):
        lines = slice(*parts_of[part])
        n = part * kvl * nb + j
        return rcopy(qall.at[j - i, lines], qall.at[j, lines], q2_s.at[n], q2_r.at[n], plus_dev(i))

    def pass_on(part):
        for k in range(kvl):
            for d in planes[slice(*parts_of[part])]:
                if d:
                    zq[k][zn - d].wait_recv()
            for i in range(1, nb):
                q_copy(part, k * nb + i, i).start()

    pass_on(0)
    for d in range(zn):
        for e in range(1, xn):
            other = pl.multiple_of((d * xn + mod(x + e, xn)) * cpd, cpd)
            adp[pl.ds(other, cpd), :] = jnp.zeros((cpd, nh * HD), BF16)
    st1s[...] = jnp.zeros_like(st1s)
    ad_load.wait()
    za = z_group(lambda d: rcopy(adp.at[own_ad], adp.at[own_ad], za_s.at[d], za_r.at[d], z_dev(d)))
    for load in late_loads:
        load.wait()

    factor = (HD ** -0.5) * LOG2E
    qrows = zn * kr
    eye = iota((qrows, LANES), 0) == iota((qrows, LANES), 1)
    group_rows = [(last - first) * kr for first, last in parts_of]
    eyes = [
        iota((size, LANES), 0) + first * kr == iota((size, LANES), 1)
        for size, (first, last) in zip(group_rows, parts_of)
    ]

    def stat_tile(row):
        high, middle, low = split3(row)
        line = iota((kr, LANES), 0)
        tile = jnp.where(line == 0, high.astype(F32), jnp.where(line == 1, middle.astype(F32), low.astype(F32)))
        return jnp.where(line < 3, tile, 0.0).astype(BF16)

    def stat_row(tile):
        wide = tile.astype(F32)
        return wide[0:1, :] + wide[1:2, :] + wide[2:3, :]

    def score(part, k, i, count, buf):
        size = count * group_rows[part]
        q = qall[k * nb + i : k * nb + i + count, slice(*parts_of[part])].reshape(size, HD)
        buf[0:size, :] = nn(q, k_t[k])

    def weigh(part, k, i, count, buf):
        size = group_rows[part]
        first, last = parts_of[part]
        m = jnp.max(buf[0 : count * size, :], axis=1, keepdims=True)
        p = jnp.exp2((buf[0 : count * size, :] - m) * factor).astype(BF16)
        oa = nn(p, vaug[k])
        total = oa[:, HD : 2 * HD]
        o = (oa[:, 0:HD] / total).astype(BF16)
        lse = m * factor + jnp.log2(total)
        for c in range(count):
            j = k * nb + i + c
            lines = slice(c * size, (c + 1) * size)
            osend[j, first:last] = o[lines].reshape(last - first, kr, HD)
            row = jnp.sum(jnp.where(eyes[part], lse[lines], 0.0), axis=0, keepdims=True)
            if part == 0:
                rowbuf[j : j + 1, :] = row
            else:
                osend[j, zn] = stat_tile(rowbuf[j : j + 1, :] + row)
                if i + c > 0:
                    o_copy(j, i + c).start()

    def o_copy(j, i):
        return rcopy(osend.at[j], orecv.at[j], o_s.at[j], o_r.at[j], minus_dev(i))

    def attend(units, pause=None):
        def begin(n):
            part, k, i, count = units[n]
            for c in range(count):
                if i + c > 0:
                    q_copy(part, k * nb + i + c, i + c).wait_recv()
            score(*units[n], sbuf[n % 2])

        begin(0)
        for n, unit in enumerate(units):
            if n + 1 == pause:
                combine(0)
            if n + 1 < len(units):
                begin(n + 1)
            weigh(*unit, sbuf[n % 2])

    def z_copies(k):
        return {
            d: rcopy(zsend.at[k, planes.index(d)], zrecv.at[k, d], zr_s.at[k * zn + d], zr_r.at[k * zn + d], z_dev(d))
            for d in ring
        }

    def combine(k):
        for i in range(1, nb):
            o_copy(k * nb + i, i).wait_recv()
        parts = [(osend if i == 0 else orecv).at[k * nb + i] for i in range(nb)]
        stats = [stat_row(part[zn]) for part in parts]
        top = functools.reduce(jnp.maximum, stats)
        weights = [jnp.exp2(st - top) for st in stats]
        weight_sum = functools.reduce(jnp.add, weights)
        inverse = 1.0 / weight_sum
        acc = jnp.zeros((qrows, HD), F32)
        for i in range(nb):
            share = jnp.where(eye, weights[i] * inverse, 0.0)[:, 0:qrows].astype(BF16)
            acc = acc + nn(share, parts[i][0:zn].reshape(qrows, HD))
        zsend[k, :, 0:kr, :] = acc.astype(BF16).reshape(zn, kr, HD)
        tile = stat_tile(top + jnp.log2(weight_sum))
        for d in range(zn):
            zsend[k, d, kr : 2 * kr, :] = tile
        for copy in z_copies(k).values():
            copy.start()

    def settle(k, copies):
        received(copies)
        parts = [zsend[k, 0]] + [zrecv[k, d] for d in range(1, zn)]
        columns = []
        for d in range(zn):
            mine = iota((kr, LANES), 1) == iota((kr, LANES), 0) + planes.index(d) * kr
            columns.append(
                jnp.sum(jnp.where(mine, stat_row(parts[d][kr : 2 * kr, :]), 0.0), axis=1, keepdims=True)
            )
        top = functools.reduce(jnp.maximum, columns)
        weights = [jnp.exp2(column - top) for column in columns]
        inverse = 1.0 / functools.reduce(jnp.add, weights)
        acc = jnp.zeros((kr, HD), F32)
        for d in range(zn):
            acc = acc + (weights[d] * inverse) * parts[d][0:kr, :].astype(F32)
        hz[k, pl.ds(z, 1)] = acc.astype(BF16)[None]
        return z_group(
            lambda d: rcopy(hz.at[k, z], hz.at[k, z], hz_s.at[k * zn + d], hz_r.at[k * zn + d], z_dev(d))
        )

    def spread(k, copies):
        received(copies)
        pieces = nn(regroup_h[...], hz[k].reshape(zn * kr, HD)).astype(BF16)
        for h in range(GROUP):
            hall[k, pl.ds(b, 1), :, h * HD : (h + 1) * HD] = pieces[h * tb : (h + 1) * tb, :][None]
        copies = {
            i: rcopy(hall.at[k, b], hall.at[k, b], h2_s.at[k * nb + i], h2_r.at[k * nb + i], plus_dev(i))
            for i in far_first
        }
        for copy in copies.values():
            copy.start()
        return copies

    def project(k, copies):
        gain = gain_ref[...].astype(F32)
        for i in range(nb):
            if i > 0:
                copies[i].wait_recv()
            my, mx = minus(i)
            there = my * xn + mx
            hidden = hall[k, there].astype(F32)
            lines = pl.ds(pl.multiple_of(there * tb, tb), tb)
            partial = jnp.zeros((tb, HD), F32)
            for h in range(GROUP):
                piece = hidden[:, h * HD : (h + 1) * HD]
                partial = partial + piece * piece
                head = k * GROUP + h
                gall[lines, head * HD : (head + 1) * HD] = (piece * gain[head : head + 1, :]).astype(BF16)
            squares[lines, :] = partial if k == 0 else squares[lines, :] + partial
        width = GROUP * HD
        part = nn(gall[:, k * width : (k + 1) * width], ad_t[k * width : (k + 1) * width, :])
        mpre[...] = part if k == 0 else mpre[...] + part

    def turn_adapter(k):
        for h in range(k * GROUP, (k + 1) * GROUP):
            for first in range(0, aw, LANES):
                ad_t[h * HD : (h + 1) * HD, first : first + LANES] = (
                    adp[first : first + LANES, h * HD : (h + 1) * HD].astype(F32).T.astype(BF16)
                )

    attend([(0, k, 0, 1) for k in range(kvl)])
    pass_on(1)
    pairs = [(1, 1)] + [(i, 2) for i in range(2, nb, 2)]
    attend([(0, k, i, count) for k in range(kvl) for i, count in pairs])
    quads = [(nb // 2, nb // 2), (0, nb // 2)]
    attend([(1, k, i, count) for k in range(kvl) for i, count in quads], 2 * kvl - 1)

    regroup_h[...] = regroup(GROUP, zn)
    received(zc)
    pieces = nn(regroup(groups, zn), cz[...].reshape(zn * groups * 2, LANES))
    cg[...] = pieces.astype(BF16).reshape(groups, tb, LANES)
    my_group = div(ctx, per_group)
    c2 = {}
    for i in range(1, nb):
        py, px = plus(i)
        there = div((py * zn + z) * xn + px, per_group)
        c2[i] = rcopy(cg.at[there], call.at[b], c2_s.at[i], c2_r.at[i], at(py, z, px))
        c2[i].start()
    call[pl.ds(b, 1)] = cg[pl.ds(my_group, 1)]

    combine(1)
    sent(*zq, zc)
    h0 = settle(0, z_copies(0))
    received(za)
    turn_adapter(0)

    sel = iota((rows, rows), 1) == row_of(iota((rows, 1), 0), sizes)
    wanted = jnp.sum(
        jnp.where(sel, jnp.broadcast_to(src_ref[...].astype(F32), (rows, rows)), 0.0),
        axis=1, keepdims=True,
    )
    pick = (wanted == row_of(iota((1, rows), 1), sizes).astype(F32)).astype(F32)
    received(c2)
    cot_rows = nn(pick.T.astype(BF16), call[...].reshape(rows, LANES))
    cot_t[...] = cot_rows.T
    token = iota((nb * 2, 1), 0)
    block = div(token, 2)
    token = 2 * ((div(block, xn) * zn + z) * xn + mod(block, xn)) + mod(token, 2)
    wanted = jnp.sum(
        jnp.where(iota((nb * 2, rows), 1) == token, src_ref[...].astype(F32), 0.0), axis=1, keepdims=True
    )
    pick = (wanted == row_of(iota((1, rows), 1), sizes).astype(F32)).astype(F32)

    h1 = settle(1, z_copies(1))
    g0 = spread(0, h0)
    turn_adapter(1)
    sent(za, z_copies(0), z_copies(1), c2)
    for j in range(kvl * nb):
        if j % nb:
            q_copy(0, j, j % nb).wait_send()
            q_copy(1, j, j % nb).wait_send()
            o_copy(j, j % nb).wait_send()
    g1 = spread(1, h1)
    project(0, g0)
    sent(h0, h1, g0)
    project(1, g1)

    for first in range(0, aw, LANES):
        mpre_t[first : first + LANES, :] = mpre[:, first : first + LANES].T
    hx[pl.ds(hd, 1), 0:cpd, 0:rows] = mpre_t[own_ad, :][None]
    power = jnp.sum(squares[...].T, axis=0, keepdims=True)
    hx[pl.ds(hd, 1), cpd : cpd + 8, 0:rows] = jnp.broadcast_to(power, (8, rows))[None]
    one_hot = pick.astype(BF16)
    chosen = functools.reduce(jnp.add, [nn(one_hot, term) for term in split3(mpre[...])])
    base = cpd + 8
    for j in range(aw // LANES):
        hx[pl.ds(hd, 1), base + j * 2 * nb : base + (j + 1) * 2 * nb, :] = chosen[
            :, j * LANES : (j + 1) * LANES
        ][None]
    hxc = {}
    for e in range(1, heads):
        hxc[e] = rcopy(hx.at[hd], hx.at[hd], hx_s.at[e], hx_r.at[e], (ctx, mod(hd + e, heads)))
        hxc[e].start()
    sent(g1)
    received(hxc)
    summed = hx[0]
    for e in range(1, heads):
        summed = summed + hx[e]
    scale = lax.rsqrt(summed[cpd : cpd + 1, 0:rows] / eps_div + 1e-05)

    token_scale = jnp.sum(pick * scale, axis=1, keepdims=True)
    for j in range(aw // LANES):
        pre = token_scale * summed[base + j * 2 * nb : base + (j + 1) * 2 * nb, :]
        out = pre / (1.0 + jnp.exp(-pre))
        for d in range(nb):
            st1s[d, 0:2, j * LANES : (j + 1) * LANES] = out[2 * d : 2 * d + 2, :]
    s1 = {}
    for i in far_first:
        py, px = plus(i)
        s1[i] = rcopy(st1s.at[py * xn + px], st1r.at[b], s1_s.at[i], s1_r.at[i], at(py, z, px))
        s1[i].start()
    st1r[pl.ds(b, 1)] = st1s[pl.ds(b, 1)]
    sent(hxc)

    pre = scale * summed[0:cpd, 0:rows]
    sig = 1.0 / (1.0 + jnp.exp(-pre))
    own = pl.multiple_of(mod(ctx, per_group) * cpd, cpd)
    slope = (cot_t[pl.ds(own, cpd), :] * sig * (1.0 + pre * (1.0 - sig)) * scale).astype(BF16)
    grad_ref[...] = nn(slope, gall[...]) * (rows ** -0.5)

    sent(s1)
    received(s1)
    for py in range(yn):
        tile = st1r[py * xn]
        for px in range(1, xn):
            tile = tile + st1r[py * xn + px]
        stu_ref[:, py * aw : (py + 1) * aw] = tile[0:2, :]


def local(sizes, heads, queries, keys, values, norm_gain, adapter, source_row, cotangent):
    yn, zn, xn = sizes
    nb = yn * xn
    tb = 2 * zn
    rows = nb * tb
    positions, kvw = keys.shape
    kvl = kvw // HD
    nh = kvl * GROUP
    nf = nh * HD
    kr = GROUP * 2
    cpd = adapter.shape[0]
    aw = zn * xn * cpd
    groups = cotangent.shape[1] // LANES
    near = 1 + 2 * (zn // 4)
    buf_rows = kr * max(2 * near, nb // 2 * (zn - near))
    vm = pltpu.VMEM
    dma = pltpu.SemaphoreType.DMA
    scratch = [
        vm(queries.shape, BF16),
        vm((nh, HD), BF16),
        vm((1, rows), jnp.int32),
        vm(cotangent.shape, BF16),
        vm((positions, kvw), BF16),
        vm((kvl, HD, positions), BF16),
        vm((kvl, positions, 2 * HD), BF16),
        vm((kvl * nb, zn, kr, HD), BF16),
        vm((kvl * nb, zn + 1, kr, HD), BF16),
        vm((kvl * nb, zn + 1, kr, HD), BF16),
        vm((kvl, zn, 2 * kr, HD), BF16),
        vm((kvl, zn, 2 * kr, HD), BF16),
        vm((kvl, zn, kr, HD), BF16),
        vm((kvl, nb, tb, GROUP * HD), BF16),
        vm((rows, nf), BF16),
        vm((rows, aw), F32),
        vm((rows, HD), F32),
        vm((heads, cpd + 8 + 2 * nb * (aw // LANES), max(rows, LANES)), F32),
        vm((buf_rows, positions), F32),
        vm((buf_rows, positions), F32),
        vm((kvl * nb, LANES), F32),
        vm((zn * kr, zn * kr), BF16),
        vm((zn, groups * 2, LANES), BF16),
        vm((groups, tb, LANES), BF16),
        vm((nb, tb, LANES), BF16),
        vm((LANES, rows), F32),
        vm((aw, rows), F32),
        vm((nb, 8, aw), F32),
        vm((nb, 8, aw), F32),
        vm((aw, nf), BF16),
        vm((nf, aw), BF16),
        dma((6 + kvl,)),
        dma((kvl * zn,)), dma((kvl * zn,)), dma((2 * kvl * nb,)), dma((2 * kvl * nb,)),
        dma((zn,)), dma((zn,)), dma((nb,)), dma((nb,)),
        dma((kvl * nb,)), dma((kvl * nb,)),
        dma((kvl * zn,)), dma((kvl * zn,)), dma((kvl * zn,)), dma((kvl * zn,)),
        dma((kvl * nb,)), dma((kvl * nb,)),
        dma((heads,)), dma((heads,)),
        dma((nb,)), dma((nb,)), dma((zn,)), dma((zn,)),
    ]
    args = (queries, keys, values, norm_gain.reshape(nh, HD), adapter, source_row.reshape(1, -1), cotangent)
    vmem = pl.BlockSpec(memory_space=pltpu.VMEM)
    hbm = pl.BlockSpec(memory_space=pltpu.HBM)
    return pl.pallas_call(
        functools.partial(kernel, sizes, heads, float(heads * nf)),
        out_shape=(
            pltpu.VMEM(cotangent.shape, F32),
            pltpu.VMEM(adapter.shape, F32),
        ),
        in_specs=[hbm] * 7,
        out_specs=(vmem, vmem),
        scratch_shapes=scratch,
        compiler_params=pltpu.CompilerParams(
            collective_id=0, has_side_effects=True, vmem_limit_bytes=48 * 1024 * 1024
        ),
        cost_estimate=pl.CostEstimate(
            flops=4 * rows * nh * HD * positions,
            bytes_accessed=4 * positions * kvw,
            transcendentals=rows * nh * positions,
        ),
        name="distill",
    )(*(pltpu.with_memory_space_constraint(arg, pltpu.HBM) for arg in args))


def solution(mesh, sizes=(YN, ZN, XN)):
    return jax.shard_map(
        functools.partial(local, sizes, mesh.shape["head"]),
        mesh=mesh,
        in_specs=(
            P("ctx", "head"),
            P("ctx", "head"),
            P("ctx", "head"),
            P("head"),
            P("ctx", "head"),
            P(),
            P("ctx", None),
        ),
        out_specs=(P("ctx", None), P("ctx", "head")),
        check_vma=False,
    )
```

```python
import functools

import jax
import jax.numpy as jnp
from jax import lax
from jax.experimental import pallas as pl
from jax.experimental.pallas import tpu as pltpu
from jax.sharding import PartitionSpec as P

H = 64
HD = 128
GROUP = 8
LANES = 128
LOG2E = 1.4426950408889634
YN, ZN, XN = 4, 8, 2

F32 = jnp.float32
BF16 = jnp.bfloat16
MESH = pl.DeviceIdType.MESH


def iota(shape, axis):
    return lax.broadcasted_iota(jnp.int32, shape, axis)


def nn(left, right):
    return lax.dot_general(left, right, (((1,), (0,)), ((), ())), preferred_element_type=F32)


def div(a, n):
    return a // n if isinstance(a, int) else a >> (n.bit_length() - 1)


def mod(a, n):
    return a % n if isinstance(a, int) else a & (n - 1)


def regroup(outer, zn):
    size = outer * zn * 2
    row, col = iota((size, 1), 0), iota((size, size), 1)
    head, rest = div(row, 2 * zn), mod(row, 2 * zn)
    return (col == div(rest, 2) * (2 * outer) + head * 2 + mod(rest, 2)).astype(F32).astype(BF16)


def row_of(position, sizes):
    yn, zn, xn = sizes
    pair, block = div(position, 2), div(position, 2 * zn)
    ctx = (div(block, xn) * zn + mod(pair, zn)) * xn + mod(block, xn)
    return 2 * ctx + mod(position, 2)


def split3(value):
    high = value.astype(BF16)
    rest = value - high.astype(F32)
    middle = rest.astype(BF16)
    return high, middle, (rest - middle.astype(F32)).astype(BF16)


def kernel(sizes, heads, eps_div, q_hbm, k_hbm, v_hbm, gain_hbm, ad_hbm, src_hbm, cot_hbm,
           stu_ref, grad_ref,
           q_ref, gain_ref, src_ref, cot_ref, kbuf, k_t, vaug, qall, osend, orecv, zsend, zrecv,
           hz, hall, gall, mpre, squares, hx, s_even, s_odd, regroup_h, cz, cg, call, cot_t, mpre_t, st1s, st1r,
           adp, ad_t,
           loc_sem, zq_s, zq_r, q2_s, q2_r, zc_s, zc_r, c2_s, c2_r, o_s, o_r,
           zr_s, zr_r, hz_s, hz_r, h2_s, h2_r, hx_s, hx_r, s1_s, s1_r, za_s, za_r):
    sbuf = (s_even, s_odd)
    yn, zn, xn = sizes
    nb = yn * xn
    tb = 2 * zn
    rows = nb * tb
    kvl = k_hbm.shape[1] // HD
    nh = kvl * GROUP
    kr = GROUP * 2
    cpd = ad_hbm.shape[0]
    per_group = LANES // cpd
    aw = zn * xn * cpd
    groups = cot_hbm.shape[1] // LANES

    ctx = lax.axis_index("ctx")
    hd = lax.axis_index("head")
    y = div(ctx, zn * xn)
    z = mod(div(ctx, xn), zn)
    x = mod(ctx, xn)
    b = y * xn + x

    def at(y_, z_, x_):
        return ((y_ * zn + z_) * xn + x_, hd)

    def z_plus(d):
        return mod(z + d, zn)

    ring = sorted(range(1, zn), key=lambda d: -min(d, zn - d))

    def z_dev(d):
        return at(y, z_plus(d), x)

    others = [(dy, dx) for dy in range(yn) for dx in range(xn) if dy or dx]
    steps = [(0, 0)] + sorted(others, key=lambda st: (-min(st[0], yn - st[0]) - st[1], -st[1], st[0]))

    def plus(i):
        dy, dx = steps[i]
        return mod(y + dy, yn), mod(x + dx, xn)

    def minus(i):
        dy, dx = steps[i]
        return mod(y + yn - dy, yn), mod(x + xn - dx, xn)

    def plus_dev(i):
        py, px = plus(i)
        return at(py, z, px)

    def minus_dev(i):
        py, px = minus(i)
        return at(py, z, px)

    def rcopy(src, dst, ssem, rsem, dev):
        return pltpu.make_async_remote_copy(
            src_ref=src, dst_ref=dst, send_sem=ssem, recv_sem=rsem, device_id=dev, device_id_type=MESH
        )

    q_load = pltpu.make_async_copy(q_hbm, q_ref, loc_sem.at[0])
    q_load.start()
    barrier = pltpu.get_barrier_semaphore()
    partners = (
        [z_dev(d) for d in range(1, zn)]
        + [plus_dev(i) for i in range(1, nb)]
        + [(ctx, mod(hd + e, heads)) for e in range(1, heads)]
    )
    for dev in partners:
        pl.semaphore_signal(barrier, inc=1, device_id=dev, device_id_type=MESH)

    cot_load = pltpu.make_async_copy(cot_hbm, cot_ref, loc_sem.at[1])
    k_load = pltpu.make_async_copy(k_hbm, kbuf, loc_sem.at[2])
    own_ad = pl.ds(pl.multiple_of((z * xn + x) * cpd, cpd), cpd)
    ad_load = pltpu.make_async_copy(ad_hbm, adp.at[own_ad], loc_sem.at[3])
    late_loads = [
        pltpu.make_async_copy(gain_hbm, gain_ref, loc_sem.at[4]),
        pltpu.make_async_copy(src_hbm, src_ref, loc_sem.at[5]),
    ]
    for k in range(kvl):
        late_loads.append(
            pltpu.make_async_copy(
                v_hbm.at[:, k * HD : (k + 1) * HD], vaug.at[k, :, 0:HD], loc_sem.at[6 + k]
            )
        )
    for load in [cot_load, k_load, ad_load] + late_loads:
        load.start()

    q_load.wait()
    qf = q_ref[...].astype(F32)
    for k in range(kvl):
        qall[k * nb, pl.ds(z, 1)] = jnp.concatenate(
            [qf[:, (k * GROUP + h) * HD : (k * GROUP + h + 1) * HD] for h in range(GROUP)], axis=0
        ).astype(BF16)[None]
    cot_load.wait()
    cf = cot_ref[...].astype(F32)
    cz[pl.ds(z, 1)] = jnp.concatenate(
        [cf[:, g * LANES : (g + 1) * LANES] for g in range(groups)], axis=0
    ).astype(BF16)[None]
    pl.semaphore_wait(barrier, len(partners))

    def z_group(make):
        copies = {d: make(d) for d in ring}
        for copy in copies.values():
            copy.start()
        return copies

    def received(copies):
        for copy in copies.values():
            copy.wait_recv()

    def sent(*groups_of_copies):
        for copies in groups_of_copies:
            for copy in copies.values():
                copy.wait_send()

    zq = [
        z_group(
            lambda d, k=k: rcopy(
                qall.at[k * nb, z], qall.at[k * nb, z], zq_s.at[k * zn + d], zq_r.at[k * zn + d], z_dev(d)
            )
        )
        for k in range(kvl)
    ]
    zc = z_group(lambda d: rcopy(cz.at[z], cz.at[z], zc_s.at[d], zc_r.at[d], z_dev(d)))

    k_load.wait()
    for k in range(kvl):
        k_t[k] = kbuf[:, k * HD : (k + 1) * HD].astype(F32).T.astype(BF16)
    for k in range(kvl):
        vaug[k, :, HD : 2 * HD] = jnp.ones((vaug.shape[1], HD), BF16)

    def q_copy(j, i):
        return rcopy(qall.at[j - i], qall.at[j], q2_s.at[j], q2_r.at[j], plus_dev(i))

    for k in range(kvl):
        received(zq[k])
        for i in range(1, nb):
            q_copy(k * nb + i, i).start()

    for d in range(zn):
        for e in range(1, xn):
            other = pl.multiple_of((d * xn + mod(x + e, xn)) * cpd, cpd)
            adp[pl.ds(other, cpd), :] = jnp.zeros((cpd, nh * HD), BF16)
    st1s[...] = jnp.zeros_like(st1s)
    ad_load.wait()
    za = z_group(lambda d: rcopy(adp.at[own_ad], adp.at[own_ad], za_s.at[d], za_r.at[d], z_dev(d)))
    for load in late_loads:
        load.wait()

    factor = (HD ** -0.5) * LOG2E
    qrows = zn * kr
    eye = iota((qrows, LANES), 0) == iota((qrows, LANES), 1)

    def stat_tile(row):
        high, middle, low = split3(row)
        line = iota((kr, LANES), 0)
        tile = jnp.where(line == 0, high.astype(F32), jnp.where(line == 1, middle.astype(F32), low.astype(F32)))
        return jnp.where(line < 3, tile, 0.0).astype(BF16)

    def stat_row(tile):
        wide = tile.astype(F32)
        return wide[0:1, :] + wide[1:2, :] + wide[2:3, :]

    def score(k, i, count, buf):
        q = qall[pl.ds(k * nb + i, count)].reshape(count * qrows, HD)
        buf[0 : count * qrows, :] = nn(q, k_t[k])

    def weigh(k, i, count, buf):
        s = buf[0 : count * qrows, :]
        m = jnp.max(s, axis=1, keepdims=True)
        p = jnp.exp2((buf[0 : count * qrows, :] - m) * factor).astype(BF16)
        oa = nn(p, vaug[k])
        total = oa[:, HD : 2 * HD]
        o = (oa[:, 0:HD] / total).astype(BF16)
        lse = m * factor + jnp.log2(total)
        for c in range(count):
            part = slice(c * qrows, (c + 1) * qrows)
            osend[k * nb + i + c, 0:zn] = o[part].reshape(zn, kr, HD)
            row = jnp.sum(jnp.where(eye, lse[part], 0.0), axis=0, keepdims=True)
            osend[k * nb + i + c, zn] = stat_tile(row)
            if i + c > 0:
                o_copy(k * nb + i + c, i + c).start()

    def o_copy(j, i):
        return rcopy(osend.at[j], orecv.at[j], o_s.at[j], o_r.at[j], minus_dev(i))

    units = [(1, nb // 2 - 1), (nb // 2, nb // 2)]

    def queries_here(k, i, count):
        for c in range(count):
            q_copy(k * nb + i + c, i + c).wait_recv()

    def attend(k, carry):
        for n, (i, count) in enumerate(units):
            here, there = sbuf[n % 2], sbuf[(n + 1) % 2]
            if n + 1 < len(units):
                queries_here(k, *units[n + 1])
                score(k, *units[n + 1], there)
                weigh(k, i, count, here)
            else:

                later = jnp.minimum(k + 1, kvl - 1)

                @pl.when(k + 1 < kvl)
                def _():
                    queries_here(later, *units[0])

                score(later, *units[0], there)
                weigh(k, i, count, here)
        return carry

    def z_copies(k):
        return {
            d: rcopy(zsend.at[k, z_plus(d)], zrecv.at[k, d], zr_s.at[k * zn + d], zr_r.at[k * zn + d], z_dev(d))
            for d in ring
        }

    def combine(k):
        for i in range(1, nb):
            o_copy(k * nb + i, i).wait_recv()
        parts = [(osend if i == 0 else orecv).at[k * nb + i] for i in range(nb)]
        stats = [stat_row(part[zn]) for part in parts]
        top = functools.reduce(jnp.maximum, stats)
        weights = [jnp.exp2(st - top) for st in stats]
        weight_sum = functools.reduce(jnp.add, weights)
        inverse = 1.0 / weight_sum
        acc = jnp.zeros((qrows, HD), F32)
        for i in range(nb):
            share = jnp.where(eye, weights[i] * inverse, 0.0)[:, 0:qrows].astype(BF16)
            acc = acc + nn(share, parts[i][0:zn].reshape(qrows, HD))
        zsend[k, :, 0:kr, :] = acc.astype(BF16).reshape(zn, kr, HD)
        tile = stat_tile(top + jnp.log2(weight_sum))
        for d in range(zn):
            zsend[k, d, kr : 2 * kr, :] = tile
        for copy in z_copies(k).values():
            copy.start()

    mine = iota((kr, LANES), 1) == iota((kr, LANES), 0) + z * kr

    def settle(k, copies):
        received(copies)
        parts = [zsend[k, z]] + [zrecv[k, d] for d in range(1, zn)]
        stats = [stat_row(part[kr : 2 * kr, :]) for part in parts]
        top = functools.reduce(jnp.maximum, stats)
        weights = [jnp.exp2(st - top) for st in stats]
        inverse = 1.0 / functools.reduce(jnp.add, weights)
        acc = jnp.zeros((kr, HD), F32)
        for d in range(zn):
            column = jnp.sum(jnp.where(mine, weights[d] * inverse, 0.0), axis=1, keepdims=True)
            acc = acc + column * parts[d][0:kr, :].astype(F32)
        hz[k, pl.ds(z, 1)] = acc.astype(BF16)[None]
        return z_group(
            lambda d: rcopy(hz.at[k, z], hz.at[k, z], hz_s.at[k * zn + d], hz_r.at[k * zn + d], z_dev(d))
        )

    def spread(k, copies):
        received(copies)
        pieces = nn(regroup_h[...], hz[k].reshape(zn * kr, HD)).astype(BF16)
        for h in range(GROUP):
            hall[k, pl.ds(b, 1), :, h * HD : (h + 1) * HD] = pieces[h * tb : (h + 1) * tb, :][None]
        copies = {
            i: rcopy(hall.at[k, b], hall.at[k, b], h2_s.at[k * nb + i], h2_r.at[k * nb + i], plus_dev(i))
            for i in range(1, nb)
        }
        for copy in copies.values():
            copy.start()
        return copies

    def project(k, copies):
        gain = gain_ref[...].astype(F32)
        for i in (0, *range(nb - 1, 0, -1)):
            if i > 0:
                copies[i].wait_recv()
            my, mx = minus(i)
            there = my * xn + mx
            hidden = hall[k, there].astype(F32)
            lines = pl.ds(pl.multiple_of(there * tb, tb), tb)
            partial = jnp.zeros((tb, HD), F32)
            for h in range(GROUP):
                piece = hidden[:, h * HD : (h + 1) * HD]
                partial = partial + piece * piece
                head = k * GROUP + h
                gall[lines, head * HD : (head + 1) * HD] = (piece * gain[head : head + 1, :]).astype(BF16)
            squares[lines, :] = partial if k == 0 else squares[lines, :] + partial
        width = GROUP * HD
        part = nn(gall[:, k * width : (k + 1) * width], ad_t[k * width : (k + 1) * width, :])
        mpre[...] = part if k == 0 else mpre[...] + part

    def turn_adapter(k):
        for h in range(k * GROUP, (k + 1) * GROUP):
            for first in range(0, aw, LANES):
                ad_t[h * HD : (h + 1) * HD, first : first + LANES] = (
                    adp[first : first + LANES, h * HD : (h + 1) * HD].astype(F32).T.astype(BF16)
                )

    score(0, 0, 1, sbuf[0])
    score(1, 0, 1, sbuf[1])
    weigh(0, 0, 1, sbuf[0])
    queries_here(0, *units[0])
    score(0, *units[0], sbuf[0])
    weigh(1, 0, 1, sbuf[1])
    lax.fori_loop(0, kvl, attend, 0)

    regroup_h[...] = regroup(GROUP, zn)
    received(zc)
    pieces = nn(regroup(groups, zn), cz[...].reshape(zn * groups * 2, LANES))
    cg[...] = pieces.astype(BF16).reshape(groups, tb, LANES)
    my_group = div(ctx, per_group)
    c2 = {}
    for i in range(1, nb):
        py, px = plus(i)
        there = div((py * zn + z) * xn + px, per_group)
        c2[i] = rcopy(cg.at[there], call.at[b], c2_s.at[i], c2_r.at[i], at(py, z, px))
        c2[i].start()
    call[pl.ds(b, 1)] = cg[pl.ds(my_group, 1)]

    combine(0)
    combine(1)
    sent(*zq, zc)
    h0 = settle(0, z_copies(0))
    received(za)
    turn_adapter(0)

    sel = iota((rows, rows), 1) == row_of(iota((rows, 1), 0), sizes)
    wanted = jnp.sum(
        jnp.where(sel, jnp.broadcast_to(src_ref[...].astype(F32), (rows, rows)), 0.0),
        axis=1, keepdims=True,
    )
    pick = (wanted == row_of(iota((1, rows), 1), sizes).astype(F32)).astype(F32)
    received(c2)
    cot_rows = nn(pick.T.astype(BF16), call[...].reshape(rows, LANES))
    cot_t[...] = cot_rows.T
    token = iota((nb * 2, 1), 0)
    block = div(token, 2)
    token = 2 * ((div(block, xn) * zn + z) * xn + mod(block, xn)) + mod(token, 2)
    wanted = jnp.sum(
        jnp.where(iota((nb * 2, rows), 1) == token, src_ref[...].astype(F32), 0.0), axis=1, keepdims=True
    )
    pick = (wanted == row_of(iota((1, rows), 1), sizes).astype(F32)).astype(F32)

    h1 = settle(1, z_copies(1))
    g0 = spread(0, h0)
    turn_adapter(1)
    sent(za, z_copies(0), z_copies(1), c2)
    for j in range(kvl * nb):
        if j % nb:
            q_copy(j, j % nb).wait_send()
            o_copy(j, j % nb).wait_send()
    g1 = spread(1, h1)
    project(0, g0)
    sent(h0, h1, g0)
    project(1, g1)

    for first in range(0, aw, LANES):
        mpre_t[first : first + LANES, :] = mpre[:, first : first + LANES].T
    hx[pl.ds(hd, 1), 0:cpd, 0:rows] = mpre_t[own_ad, :][None]
    power = jnp.sum(squares[...].T, axis=0, keepdims=True)
    hx[pl.ds(hd, 1), cpd : cpd + 8, 0:rows] = jnp.broadcast_to(power, (8, rows))[None]
    one_hot = pick.astype(BF16)
    chosen = functools.reduce(jnp.add, [nn(one_hot, term) for term in split3(mpre[...])])
    base = cpd + 8
    for j in range(aw // LANES):
        hx[pl.ds(hd, 1), base + j * 2 * nb : base + (j + 1) * 2 * nb, :] = chosen[
            :, j * LANES : (j + 1) * LANES
        ][None]
    hxc = {}
    for e in range(1, heads):
        hxc[e] = rcopy(hx.at[hd], hx.at[hd], hx_s.at[e], hx_r.at[e], (ctx, mod(hd + e, heads)))
        hxc[e].start()
    sent(g1)
    received(hxc)
    summed = hx[0]
    for e in range(1, heads):
        summed = summed + hx[e]
    scale = lax.rsqrt(summed[cpd : cpd + 1, 0:rows] / eps_div + 1e-05)

    token_scale = jnp.sum(pick * scale, axis=1, keepdims=True)
    for j in range(aw // LANES):
        pre = token_scale * summed[base + j * 2 * nb : base + (j + 1) * 2 * nb, :]
        out = pre / (1.0 + jnp.exp(-pre))
        for d in range(nb):
            st1s[d, 0:2, j * LANES : (j + 1) * LANES] = out[2 * d : 2 * d + 2, :]
    s1 = {}
    for i in range(1, nb):
        py, px = plus(i)
        s1[i] = rcopy(st1s.at[py * xn + px], st1r.at[b], s1_s.at[i], s1_r.at[i], at(py, z, px))
        s1[i].start()
    st1r[pl.ds(b, 1)] = st1s[pl.ds(b, 1)]
    sent(hxc)

    pre = scale * summed[0:cpd, 0:rows]
    sig = 1.0 / (1.0 + jnp.exp(-pre))
    own = pl.multiple_of(mod(ctx, per_group) * cpd, cpd)
    slope = (cot_t[pl.ds(own, cpd), :] * sig * (1.0 + pre * (1.0 - sig)) * scale).astype(BF16)
    grad_ref[...] = nn(slope, gall[...]) * (rows ** -0.5)

    sent(s1)
    received(s1)
    for py in range(yn):
        tile = st1r[py * xn]
        for px in range(1, xn):
            tile = tile + st1r[py * xn + px]
        stu_ref[:, py * aw : (py + 1) * aw] = tile[0:2, :]


def local(sizes, heads, queries, keys, values, norm_gain, adapter, source_row, cotangent):
    yn, zn, xn = sizes
    nb = yn * xn
    tb = 2 * zn
    rows = nb * tb
    positions, kvw = keys.shape
    kvl = kvw // HD
    nh = kvl * GROUP
    nf = nh * HD
    kr = GROUP * 2
    cpd = adapter.shape[0]
    aw = zn * xn * cpd
    groups = cotangent.shape[1] // LANES
    vm = pltpu.VMEM
    dma = pltpu.SemaphoreType.DMA
    scratch = [
        vm(queries.shape, BF16),
        vm((nh, HD), BF16),
        vm((1, rows), jnp.int32),
        vm(cotangent.shape, BF16),
        vm((positions, kvw), BF16),
        vm((kvl, HD, positions), BF16),
        vm((kvl, positions, 2 * HD), BF16),
        vm((kvl * nb, zn, kr, HD), BF16),
        vm((kvl * nb, zn + 1, kr, HD), BF16),
        vm((kvl * nb, zn + 1, kr, HD), BF16),
        vm((kvl, zn, 2 * kr, HD), BF16),
        vm((kvl, zn, 2 * kr, HD), BF16),
        vm((kvl, zn, kr, HD), BF16),
        vm((kvl, nb, tb, GROUP * HD), BF16),
        vm((rows, nf), BF16),
        vm((rows, aw), F32),
        vm((rows, HD), F32),
        vm((heads, cpd + 8 + 2 * nb * (aw // LANES), max(rows, LANES)), F32),
        vm((nb // 2 * zn * kr, positions), F32),
        vm((nb // 2 * zn * kr, positions), F32),
        vm((zn * kr, zn * kr), BF16),
        vm((zn, groups * 2, LANES), BF16),
        vm((groups, tb, LANES), BF16),
        vm((nb, tb, LANES), BF16),
        vm((LANES, rows), F32),
        vm((aw, rows), F32),
        vm((nb, 8, aw), F32),
        vm((nb, 8, aw), F32),
        vm((aw, nf), BF16),
        vm((nf, aw), BF16),
        dma((6 + kvl,)),
        dma((kvl * zn,)), dma((kvl * zn,)), dma((kvl * nb,)), dma((kvl * nb,)),
        dma((zn,)), dma((zn,)), dma((nb,)), dma((nb,)),
        dma((kvl * nb,)), dma((kvl * nb,)),
        dma((kvl * zn,)), dma((kvl * zn,)), dma((kvl * zn,)), dma((kvl * zn,)),
        dma((kvl * nb,)), dma((kvl * nb,)),
        dma((heads,)), dma((heads,)),
        dma((nb,)), dma((nb,)), dma((zn,)), dma((zn,)),
    ]
    args = (queries, keys, values, norm_gain.reshape(nh, HD), adapter, source_row.reshape(1, -1), cotangent)
    vmem = pl.BlockSpec(memory_space=pltpu.VMEM)
    hbm = pl.BlockSpec(memory_space=pltpu.HBM)
    return pl.pallas_call(
        functools.partial(kernel, sizes, heads, float(heads * nf)),
        out_shape=(
            pltpu.VMEM(cotangent.shape, F32),
            pltpu.VMEM(adapter.shape, F32),
        ),
        in_specs=[hbm] * 7,
        out_specs=(vmem, vmem),
        scratch_shapes=scratch,
        compiler_params=pltpu.CompilerParams(
            collective_id=0, has_side_effects=True, vmem_limit_bytes=48 * 1024 * 1024
        ),
        cost_estimate=pl.CostEstimate(
            flops=4 * rows * nh * HD * positions,
            bytes_accessed=4 * positions * kvw,
            transcendentals=rows * nh * positions,
        ),
        name="distill",
    )(*(pltpu.with_memory_space_constraint(arg, pltpu.HBM) for arg in args))


def solution(mesh, sizes=(YN, ZN, XN)):
    return jax.shard_map(
        functools.partial(local, sizes, mesh.shape["head"]),
        mesh=mesh,
        in_specs=(
            P("ctx", "head"),
            P("ctx", "head"),
            P("ctx", "head"),
            P("head"),
            P("ctx", "head"),
            P(),
            P("ctx", None),
        ),
        out_specs=(P("ctx", None), P("ctx", "head")),
        check_vma=False,
    )
```

```python
import functools

import jax
import jax.numpy as jnp
from jax import lax
from jax.experimental import pallas as pl
from jax.experimental.pallas import tpu as pltpu
from jax.sharding import PartitionSpec as P

H = 64
HD = 128
GROUP = 8
LANES = 128
LOG2E = 1.4426950408889634
YN, ZN, XN = 4, 8, 2

F32 = jnp.float32
BF16 = jnp.bfloat16
MESH = pl.DeviceIdType.MESH


def iota(shape, axis):
    return lax.broadcasted_iota(jnp.int32, shape, axis)


def nn(left, right):
    return lax.dot_general(left, right, (((1,), (0,)), ((), ())), preferred_element_type=F32)


def div(a, n):
    return a // n if isinstance(a, int) else a >> (n.bit_length() - 1)


def mod(a, n):
    return a % n if isinstance(a, int) else a & (n - 1)


def regroup(outer, zn):
    size = outer * zn * 2
    row, col = iota((size, 1), 0), iota((size, size), 1)
    head, rest = div(row, 2 * zn), mod(row, 2 * zn)
    return (col == div(rest, 2) * (2 * outer) + head * 2 + mod(rest, 2)).astype(F32).astype(BF16)


def row_of(position, sizes):
    yn, zn, xn = sizes
    pair, block = div(position, 2), div(position, 2 * zn)
    ctx = (div(block, xn) * zn + mod(pair, zn)) * xn + mod(block, xn)
    return 2 * ctx + mod(position, 2)


def split3(value):
    high = value.astype(BF16)
    rest = value - high.astype(F32)
    middle = rest.astype(BF16)
    return high, middle, (rest - middle.astype(F32)).astype(BF16)


def kernel(sizes, heads, eps_div, q_hbm, k_hbm, v_hbm, gain_hbm, ad_hbm, src_hbm, cot_hbm,
           stu_ref, grad_ref,
           q_ref, gain_ref, src_ref, cot_ref, kbuf, k_t, vaug, qall, osend, orecv, zsend, zrecv,
           hz, hall, gall, mpre, squares, hx, s_even, s_odd, regroup_h, cz, cg, call, cot_t, mpre_t, st1s, st1r,
           adp, ad_t,
           loc_sem, zq_s, zq_r, q2_s, q2_r, zc_s, zc_r, c2_s, c2_r, o_s, o_r,
           zr_s, zr_r, hz_s, hz_r, h2_s, h2_r, hx_s, hx_r, s1_s, s1_r, za_s, za_r):
    sbuf = (s_even, s_odd)
    yn, zn, xn = sizes
    nb = yn * xn
    tb = 2 * zn
    rows = nb * tb
    kvl = k_hbm.shape[1] // HD
    nh = kvl * GROUP
    kr = GROUP * 2
    cpd = ad_hbm.shape[0]
    per_group = LANES // cpd
    aw = zn * xn * cpd
    groups = cot_hbm.shape[1] // LANES

    ctx = lax.axis_index("ctx")
    hd = lax.axis_index("head")
    y = div(ctx, zn * xn)
    z = mod(div(ctx, xn), zn)
    x = mod(ctx, xn)
    b = y * xn + x

    def at(y_, z_, x_):
        return ((y_ * zn + z_) * xn + x_, hd)

    def z_plus(d):
        return mod(z + d, zn)

    ring = sorted(range(1, zn), key=lambda d: -min(d, zn - d))

    def z_dev(d):
        return at(y, z_plus(d), x)

    others = [(dy, dx) for dy in range(yn) for dx in range(xn) if dy or dx]
    steps = [(0, 0)] + sorted(others, key=lambda st: (-min(st[0], yn - st[0]) - st[1], -st[1], st[0]))

    def plus(i):
        dy, dx = steps[i]
        return mod(y + dy, yn), mod(x + dx, xn)

    def minus(i):
        dy, dx = steps[i]
        return mod(y + yn - dy, yn), mod(x + xn - dx, xn)

    def plus_dev(i):
        py, px = plus(i)
        return at(py, z, px)

    def minus_dev(i):
        py, px = minus(i)
        return at(py, z, px)

    def rcopy(src, dst, ssem, rsem, dev):
        return pltpu.make_async_remote_copy(
            src_ref=src, dst_ref=dst, send_sem=ssem, recv_sem=rsem, device_id=dev, device_id_type=MESH
        )

    q_load = pltpu.make_async_copy(q_hbm, q_ref, loc_sem.at[0])
    q_load.start()
    barrier = pltpu.get_barrier_semaphore()
    partners = (
        [z_dev(d) for d in range(1, zn)]
        + [plus_dev(i) for i in range(1, nb)]
        + [(ctx, mod(hd + e, heads)) for e in range(1, heads)]
    )
    for dev in partners:
        pl.semaphore_signal(barrier, inc=1, device_id=dev, device_id_type=MESH)

    cot_load = pltpu.make_async_copy(cot_hbm, cot_ref, loc_sem.at[1])
    k_load = pltpu.make_async_copy(k_hbm, kbuf, loc_sem.at[2])
    own_ad = pl.ds(pl.multiple_of((z * xn + x) * cpd, cpd), cpd)
    ad_load = pltpu.make_async_copy(ad_hbm, adp.at[own_ad], loc_sem.at[3])
    late_loads = [
        pltpu.make_async_copy(gain_hbm, gain_ref, loc_sem.at[4]),
        pltpu.make_async_copy(src_hbm, src_ref, loc_sem.at[5]),
    ]
    for k in range(kvl):
        late_loads.append(
            pltpu.make_async_copy(
                v_hbm.at[:, k * HD : (k + 1) * HD], vaug.at[k, :, 0:HD], loc_sem.at[6 + k]
            )
        )
    for load in [cot_load, k_load, ad_load] + late_loads:
        load.start()

    q_load.wait()
    qf = q_ref[...].astype(F32)
    for k in range(kvl):
        qall[k, 0, pl.ds(z, 1)] = jnp.concatenate(
            [qf[:, (k * GROUP + h) * HD : (k * GROUP + h + 1) * HD] for h in range(GROUP)], axis=0
        ).astype(BF16)[None]
    cot_load.wait()
    cf = cot_ref[...].astype(F32)
    cz[pl.ds(z, 1)] = jnp.concatenate(
        [cf[:, g * LANES : (g + 1) * LANES] for g in range(groups)], axis=0
    ).astype(BF16)[None]
    pl.semaphore_wait(barrier, len(partners))

    def z_group(make):
        copies = {d: make(d) for d in ring}
        for copy in copies.values():
            copy.start()
        return copies

    def received(copies):
        for copy in copies.values():
            copy.wait_recv()

    def sent(*groups_of_copies):
        for copies in groups_of_copies:
            for copy in copies.values():
                copy.wait_send()

    zq = z_group(lambda d: rcopy(qall.at[:, 0, z], qall.at[:, 0, z], zq_s.at[d], zq_r.at[d], z_dev(d)))
    zc = z_group(lambda d: rcopy(cz.at[z], cz.at[z], zc_s.at[d], zc_r.at[d], z_dev(d)))

    k_load.wait()
    for k in range(kvl):
        k_t[k] = kbuf[:, k * HD : (k + 1) * HD].astype(F32).T.astype(BF16)
    for k in range(kvl):
        vaug[k, :, HD : 2 * HD] = jnp.ones((vaug.shape[1], HD), BF16)

    def q_copy(k, i):
        return rcopy(qall.at[k, 0], qall.at[k, i], q2_s.at[k * nb + i], q2_r.at[k * nb + i], plus_dev(i))

    received(zq)
    for k in range(kvl):
        for i in range(1, nb):
            q_copy(k, i).start()

    for d in range(zn):
        for e in range(1, xn):
            other = pl.multiple_of((d * xn + mod(x + e, xn)) * cpd, cpd)
            adp[pl.ds(other, cpd), :] = jnp.zeros((cpd, nh * HD), BF16)
    st1s[...] = jnp.zeros_like(st1s)
    ad_load.wait()
    za = z_group(lambda d: rcopy(adp.at[own_ad], adp.at[own_ad], za_s.at[d], za_r.at[d], z_dev(d)))
    for load in late_loads:
        load.wait()

    factor = (HD ** -0.5) * LOG2E
    qrows = zn * kr
    eye = iota((qrows, LANES), 0) == iota((qrows, LANES), 1)

    def stat_tile(row):
        high, middle, low = split3(row)
        line = iota((kr, LANES), 0)
        tile = jnp.where(line == 0, high.astype(F32), jnp.where(line == 1, middle.astype(F32), low.astype(F32)))
        return jnp.where(line < 3, tile, 0.0).astype(BF16)

    def stat_row(tile):
        wide = tile.astype(F32)
        return wide[0:1, :] + wide[1:2, :] + wide[2:3, :]

    def score(k, i, count, buf):
        q = qall[k, i : i + count].reshape(count * qrows, HD)
        buf[0 : count * qrows, :] = nn(q, k_t[k])

    def weigh(k, i, count, buf):
        s = buf[0 : count * qrows, :]
        m = jnp.max(s, axis=1, keepdims=True)
        p = jnp.exp2((buf[0 : count * qrows, :] - m) * factor).astype(BF16)
        oa = nn(p, vaug[k])
        total = oa[:, HD : 2 * HD]
        o = (oa[:, 0:HD] / total).astype(BF16)
        lse = m * factor + jnp.log2(total)
        for c in range(count):
            part = slice(c * qrows, (c + 1) * qrows)
            osend[k * nb + i + c, 0:zn] = o[part].reshape(zn, kr, HD)
            row = jnp.sum(jnp.where(eye, lse[part], 0.0), axis=0, keepdims=True)
            osend[k * nb + i + c, zn] = stat_tile(row)
            if i + c > 0:
                o_copy(k * nb + i + c, i + c).start()

    def o_copy(j, i):
        return rcopy(osend.at[j], orecv.at[j], o_s.at[j], o_r.at[j], minus_dev(i))

    units = [(1, nb // 2 - 1), (nb // 2, nb // 2)]

    def queries_here(k, i, count):
        for c in range(count):
            q_copy(k, i + c).wait_recv()

    def attend(k, carry):
        for n, (i, count) in enumerate(units):
            here, there = sbuf[n % 2], sbuf[(n + 1) % 2]
            if n + 1 < len(units):
                queries_here(k, *units[n + 1])
                score(k, *units[n + 1], there)
                weigh(k, i, count, here)
            else:

                later = jnp.minimum(k + 1, kvl - 1)

                @pl.when(k + 1 < kvl)
                def _():
                    queries_here(later, *units[0])

                score(later, *units[0], there)
                weigh(k, i, count, here)
        return carry

    def z_copies(k):
        return {
            d: rcopy(zsend.at[k, z_plus(d)], zrecv.at[k, d], zr_s.at[k * zn + d], zr_r.at[k * zn + d], z_dev(d))
            for d in ring
        }

    def combine(k):
        for i in range(1, nb):
            o_copy(k * nb + i, i).wait_recv()
        parts = [(osend if i == 0 else orecv).at[k * nb + i] for i in range(nb)]
        stats = [stat_row(part[zn]) for part in parts]
        top = functools.reduce(jnp.maximum, stats)
        weights = [jnp.exp2(st - top) for st in stats]
        weight_sum = functools.reduce(jnp.add, weights)
        inverse = 1.0 / weight_sum
        acc = jnp.zeros((qrows, HD), F32)
        for i in range(nb):
            share = jnp.where(eye, weights[i] * inverse, 0.0)[:, 0:qrows].astype(BF16)
            acc = acc + nn(share, parts[i][0:zn].reshape(qrows, HD))
        zsend[k, :, 0:kr, :] = acc.astype(BF16).reshape(zn, kr, HD)
        tile = stat_tile(top + jnp.log2(weight_sum))
        for d in range(zn):
            zsend[k, d, kr : 2 * kr, :] = tile
        for copy in z_copies(k).values():
            copy.start()

    mine = iota((kr, LANES), 1) == iota((kr, LANES), 0) + z * kr

    def settle(k, copies):
        received(copies)
        parts = [zsend[k, z]] + [zrecv[k, d] for d in range(1, zn)]
        stats = [stat_row(part[kr : 2 * kr, :]) for part in parts]
        top = functools.reduce(jnp.maximum, stats)
        weights = [jnp.exp2(st - top) for st in stats]
        inverse = 1.0 / functools.reduce(jnp.add, weights)
        acc = jnp.zeros((kr, HD), F32)
        for d in range(zn):
            column = jnp.sum(jnp.where(mine, weights[d] * inverse, 0.0), axis=1, keepdims=True)
            acc = acc + column * parts[d][0:kr, :].astype(F32)
        hz[k, pl.ds(z, 1)] = acc.astype(BF16)[None]
        return z_group(
            lambda d: rcopy(hz.at[k, z], hz.at[k, z], hz_s.at[k * zn + d], hz_r.at[k * zn + d], z_dev(d))
        )

    def spread(k, copies):
        received(copies)
        pieces = nn(regroup_h[...], hz[k].reshape(zn * kr, HD)).astype(BF16)
        for h in range(GROUP):
            hall[k, pl.ds(b, 1), :, h * HD : (h + 1) * HD] = pieces[h * tb : (h + 1) * tb, :][None]
        copies = {
            i: rcopy(hall.at[k, b], hall.at[k, b], h2_s.at[k * nb + i], h2_r.at[k * nb + i], plus_dev(i))
            for i in range(1, nb)
        }
        for copy in copies.values():
            copy.start()
        return copies

    def project(k, copies):
        gain = gain_ref[...].astype(F32)
        for i in (0, *range(nb - 1, 0, -1)):
            if i > 0:
                copies[i].wait_recv()
            my, mx = minus(i)
            there = my * xn + mx
            hidden = hall[k, there].astype(F32)
            lines = pl.ds(pl.multiple_of(there * tb, tb), tb)
            partial = jnp.zeros((tb, HD), F32)
            for h in range(GROUP):
                piece = hidden[:, h * HD : (h + 1) * HD]
                partial = partial + piece * piece
                head = k * GROUP + h
                gall[lines, head * HD : (head + 1) * HD] = (piece * gain[head : head + 1, :]).astype(BF16)
            squares[lines, :] = partial if k == 0 else squares[lines, :] + partial
        width = GROUP * HD
        part = nn(gall[:, k * width : (k + 1) * width], ad_t[k * width : (k + 1) * width, :])
        mpre[...] = part if k == 0 else mpre[...] + part

    def turn_adapter(k):
        for h in range(k * GROUP, (k + 1) * GROUP):
            for first in range(0, aw, LANES):
                ad_t[h * HD : (h + 1) * HD, first : first + LANES] = (
                    adp[first : first + LANES, h * HD : (h + 1) * HD].astype(F32).T.astype(BF16)
                )

    score(0, 0, 1, sbuf[0])
    score(1, 0, 1, sbuf[1])
    weigh(0, 0, 1, sbuf[0])
    weigh(1, 0, 1, sbuf[1])
    queries_here(0, *units[0])
    score(0, *units[0], sbuf[0])
    lax.fori_loop(0, kvl, attend, 0)

    regroup_h[...] = regroup(GROUP, zn)
    received(zc)
    pieces = nn(regroup(groups, zn), cz[...].reshape(zn * groups * 2, LANES))
    cg[...] = pieces.astype(BF16).reshape(groups, tb, LANES)
    my_group = div(ctx, per_group)
    c2 = {}
    for i in range(1, nb):
        py, px = plus(i)
        there = div((py * zn + z) * xn + px, per_group)
        c2[i] = rcopy(cg.at[there], call.at[b], c2_s.at[i], c2_r.at[i], at(py, z, px))
        c2[i].start()
    call[pl.ds(b, 1)] = cg[pl.ds(my_group, 1)]

    combine(0)
    combine(1)
    sent(zq, zc)
    h0 = settle(0, z_copies(0))
    received(za)
    turn_adapter(0)

    sel = iota((rows, rows), 1) == row_of(iota((rows, 1), 0), sizes)
    wanted = jnp.sum(
        jnp.where(sel, jnp.broadcast_to(src_ref[...].astype(F32), (rows, rows)), 0.0),
        axis=1, keepdims=True,
    )
    pick = (wanted == row_of(iota((1, rows), 1), sizes).astype(F32)).astype(F32)
    received(c2)
    cot_rows = nn(pick.T.astype(BF16), call[...].reshape(rows, LANES))
    cot_t[...] = cot_rows.T
    token = iota((nb * 2, 1), 0)
    block = div(token, 2)
    token = 2 * ((div(block, xn) * zn + z) * xn + mod(block, xn)) + mod(token, 2)
    wanted = jnp.sum(
        jnp.where(iota((nb * 2, rows), 1) == token, src_ref[...].astype(F32), 0.0), axis=1, keepdims=True
    )
    pick = (wanted == row_of(iota((1, rows), 1), sizes).astype(F32)).astype(F32)

    h1 = settle(1, z_copies(1))
    g0 = spread(0, h0)
    turn_adapter(1)
    sent(za, z_copies(0), z_copies(1), c2)
    for j in range(kvl * nb):
        if j % nb:
            q_copy(j // nb, j % nb).wait_send()
            o_copy(j, j % nb).wait_send()
    g1 = spread(1, h1)
    project(0, g0)
    sent(h0, h1, g0)
    project(1, g1)

    for first in range(0, aw, LANES):
        mpre_t[first : first + LANES, :] = mpre[:, first : first + LANES].T
    hx[pl.ds(hd, 1), 0:cpd, 0:rows] = mpre_t[own_ad, :][None]
    power = jnp.sum(squares[...].T, axis=0, keepdims=True)
    hx[pl.ds(hd, 1), cpd : cpd + 8, 0:rows] = jnp.broadcast_to(power, (8, rows))[None]
    one_hot = pick.astype(BF16)
    chosen = functools.reduce(jnp.add, [nn(one_hot, term) for term in split3(mpre[...])])
    base = cpd + 8
    for j in range(aw // LANES):
        hx[pl.ds(hd, 1), base + j * 2 * nb : base + (j + 1) * 2 * nb, :] = chosen[
            :, j * LANES : (j + 1) * LANES
        ][None]
    hxc = {}
    for e in range(1, heads):
        hxc[e] = rcopy(hx.at[hd], hx.at[hd], hx_s.at[e], hx_r.at[e], (ctx, mod(hd + e, heads)))
        hxc[e].start()
    sent(g1)
    received(hxc)
    summed = hx[0]
    for e in range(1, heads):
        summed = summed + hx[e]
    scale = lax.rsqrt(summed[cpd : cpd + 1, 0:rows] / eps_div + 1e-05)

    token_scale = jnp.sum(pick * scale, axis=1, keepdims=True)
    for j in range(aw // LANES):
        pre = token_scale * summed[base + j * 2 * nb : base + (j + 1) * 2 * nb, :]
        out = pre / (1.0 + jnp.exp(-pre))
        for d in range(nb):
            st1s[d, 0:2, j * LANES : (j + 1) * LANES] = out[2 * d : 2 * d + 2, :]
    s1 = {}
    for i in range(1, nb):
        py, px = plus(i)
        s1[i] = rcopy(st1s.at[py * xn + px], st1r.at[b], s1_s.at[i], s1_r.at[i], at(py, z, px))
        s1[i].start()
    st1r[pl.ds(b, 1)] = st1s[pl.ds(b, 1)]
    sent(hxc)

    pre = scale * summed[0:cpd, 0:rows]
    sig = 1.0 / (1.0 + jnp.exp(-pre))
    own = pl.multiple_of(mod(ctx, per_group) * cpd, cpd)
    slope = (cot_t[pl.ds(own, cpd), :] * sig * (1.0 + pre * (1.0 - sig)) * scale).astype(BF16)
    grad_ref[...] = nn(slope, gall[...]) * (rows ** -0.5)

    sent(s1)
    received(s1)
    for py in range(yn):
        tile = st1r[py * xn]
        for px in range(1, xn):
            tile = tile + st1r[py * xn + px]
        stu_ref[:, py * aw : (py + 1) * aw] = tile[0:2, :]


def local(sizes, heads, queries, keys, values, norm_gain, adapter, source_row, cotangent):
    yn, zn, xn = sizes
    nb = yn * xn
    tb = 2 * zn
    rows = nb * tb
    positions, kvw = keys.shape
    kvl = kvw // HD
    nh = kvl * GROUP
    nf = nh * HD
    kr = GROUP * 2
    cpd = adapter.shape[0]
    aw = zn * xn * cpd
    groups = cotangent.shape[1] // LANES
    vm = pltpu.VMEM
    dma = pltpu.SemaphoreType.DMA
    scratch = [
        vm(queries.shape, BF16),
        vm((nh, HD), BF16),
        vm((1, rows), jnp.int32),
        vm(cotangent.shape, BF16),
        vm((positions, kvw), BF16),
        vm((kvl, HD, positions), BF16),
        vm((kvl, positions, 2 * HD), BF16),
        vm((kvl, nb, zn, kr, HD), BF16),
        vm((kvl * nb, zn + 1, kr, HD), BF16),
        vm((kvl * nb, zn + 1, kr, HD), BF16),
        vm((kvl, zn, 2 * kr, HD), BF16),
        vm((kvl, zn, 2 * kr, HD), BF16),
        vm((kvl, zn, kr, HD), BF16),
        vm((kvl, nb, tb, GROUP * HD), BF16),
        vm((rows, nf), BF16),
        vm((rows, aw), F32),
        vm((rows, HD), F32),
        vm((heads, cpd + 8 + 2 * nb * (aw // LANES), max(rows, LANES)), F32),
        vm((nb // 2 * zn * kr, positions), F32),
        vm((nb // 2 * zn * kr, positions), F32),
        vm((zn * kr, zn * kr), BF16),
        vm((zn, groups * 2, LANES), BF16),
        vm((groups, tb, LANES), BF16),
        vm((nb, tb, LANES), BF16),
        vm((LANES, rows), F32),
        vm((aw, rows), F32),
        vm((nb, 8, aw), F32),
        vm((nb, 8, aw), F32),
        vm((aw, nf), BF16),
        vm((nf, aw), BF16),
        dma((6 + kvl,)),
        dma((zn,)), dma((zn,)), dma((kvl * nb,)), dma((kvl * nb,)),
        dma((zn,)), dma((zn,)), dma((nb,)), dma((nb,)),
        dma((kvl * nb,)), dma((kvl * nb,)),
        dma((kvl * zn,)), dma((kvl * zn,)), dma((kvl * zn,)), dma((kvl * zn,)),
        dma((kvl * nb,)), dma((kvl * nb,)),
        dma((heads,)), dma((heads,)),
        dma((nb,)), dma((nb,)), dma((zn,)), dma((zn,)),
    ]
    args = (queries, keys, values, norm_gain.reshape(nh, HD), adapter, source_row.reshape(1, -1), cotangent)
    vmem = pl.BlockSpec(memory_space=pltpu.VMEM)
    hbm = pl.BlockSpec(memory_space=pltpu.HBM)
    return pl.pallas_call(
        functools.partial(kernel, sizes, heads, float(heads * nf)),
        out_shape=(
            pltpu.VMEM(cotangent.shape, F32),
            pltpu.VMEM(adapter.shape, F32),
        ),
        in_specs=[hbm] * 7,
        out_specs=(vmem, vmem),
        scratch_shapes=scratch,
        compiler_params=pltpu.CompilerParams(
            collective_id=0, has_side_effects=True, vmem_limit_bytes=48 * 1024 * 1024
        ),
        cost_estimate=pl.CostEstimate(
            flops=4 * rows * nh * HD * positions,
            bytes_accessed=4 * positions * kvw,
            transcendentals=rows * nh * positions,
        ),
        name="distill",
    )(*(pltpu.with_memory_space_constraint(arg, pltpu.HBM) for arg in args))


def solution(mesh, sizes=(YN, ZN, XN)):
    return jax.shard_map(
        functools.partial(local, sizes, mesh.shape["head"]),
        mesh=mesh,
        in_specs=(
            P("ctx", "head"),
            P("ctx", "head"),
            P("ctx", "head"),
            P("head"),
            P("ctx", "head"),
            P(),
            P("ctx", None),
        ),
        out_specs=(P("ctx", None), P("ctx", "head")),
        check_vma=False,
    )
```

```python
import functools

import jax
import jax.numpy as jnp
from jax import lax
from jax.experimental import pallas as pl
from jax.experimental.pallas import tpu as pltpu
from jax.sharding import PartitionSpec as P

H = 64
HD = 128
GROUP = 8
LANES = 128
LOG2E = 1.4426950408889634
YN, ZN, XN = 4, 8, 2

F32 = jnp.float32
BF16 = jnp.bfloat16
MESH = pl.DeviceIdType.MESH


def iota(shape, axis):
    return lax.broadcasted_iota(jnp.int32, shape, axis)


def nn(left, right):
    return lax.dot_general(left, right, (((1,), (0,)), ((), ())), preferred_element_type=F32)


def div(a, n):
    return a // n if isinstance(a, int) else a >> (n.bit_length() - 1)


def mod(a, n):
    return a % n if isinstance(a, int) else a & (n - 1)


def regroup(outer, zn):
    size = outer * zn * 2
    row, col = iota((size, 1), 0), iota((size, size), 1)
    head, rest = div(row, 2 * zn), mod(row, 2 * zn)
    return (col == div(rest, 2) * (2 * outer) + head * 2 + mod(rest, 2)).astype(F32).astype(BF16)


def row_of(position, sizes):
    yn, zn, xn = sizes
    pair, block = div(position, 2), div(position, 2 * zn)
    ctx = (div(block, xn) * zn + mod(pair, zn)) * xn + mod(block, xn)
    return 2 * ctx + mod(position, 2)


def split3(value):
    high = value.astype(BF16)
    rest = value - high.astype(F32)
    middle = rest.astype(BF16)
    return high, middle, (rest - middle.astype(F32)).astype(BF16)


def kernel(sizes, heads, eps_div, q_hbm, k_hbm, v_hbm, gain_hbm, ad_hbm, src_hbm, cot_hbm,
           stu_ref, grad_ref,
           q_ref, gain_ref, src_ref, cot_ref, kbuf, k_t, vaug, qall, osend, orecv, zsend, zrecv,
           hz, hall, gall, mpre, squares, hx, s_even, s_odd, regroup_h, cz, cg, call, cot_t, mpre_t, st1s, st1r,
           adp, ad_t,
           loc_sem, zq_s, zq_r, q2_s, q2_r, zc_s, zc_r, c2_s, c2_r, o_s, o_r,
           zr_s, zr_r, hz_s, hz_r, h2_s, h2_r, hx_s, hx_r, s1_s, s1_r, za_s, za_r):
    sbuf = (s_even, s_odd)
    yn, zn, xn = sizes
    nb = yn * xn
    tb = 2 * zn
    rows = nb * tb
    kvl = k_hbm.shape[1] // HD
    nh = kvl * GROUP
    kr = GROUP * 2
    cpd = ad_hbm.shape[0]
    per_group = LANES // cpd
    aw = zn * xn * cpd
    groups = cot_hbm.shape[1] // LANES

    ctx = lax.axis_index("ctx")
    hd = lax.axis_index("head")
    y = div(ctx, zn * xn)
    z = mod(div(ctx, xn), zn)
    x = mod(ctx, xn)
    b = y * xn + x

    def at(y_, z_, x_):
        return ((y_ * zn + z_) * xn + x_, hd)

    def z_plus(d):
        return mod(z + d, zn)

    ring = sorted(range(1, zn), key=lambda d: -min(d, zn - d))

    def z_dev(d):
        return at(y, z_plus(d), x)

    others = [(dy, dx) for dy in range(yn) for dx in range(xn) if dy or dx]
    steps = [(0, 0)] + sorted(others, key=lambda st: (-min(st[0], yn - st[0]) - st[1], -st[1], st[0]))

    def plus(i):
        dy, dx = steps[i]
        return mod(y + dy, yn), mod(x + dx, xn)

    def minus(i):
        dy, dx = steps[i]
        return mod(y + yn - dy, yn), mod(x + xn - dx, xn)

    def plus_dev(i):
        py, px = plus(i)
        return at(py, z, px)

    def minus_dev(i):
        py, px = minus(i)
        return at(py, z, px)

    def rcopy(src, dst, ssem, rsem, dev):
        return pltpu.make_async_remote_copy(
            src_ref=src, dst_ref=dst, send_sem=ssem, recv_sem=rsem, device_id=dev, device_id_type=MESH
        )

    q_load = pltpu.make_async_copy(q_hbm, q_ref, loc_sem.at[0])
    q_load.start()
    barrier = pltpu.get_barrier_semaphore()
    partners = (
        [z_dev(d) for d in range(1, zn)]
        + [plus_dev(i) for i in range(1, nb)]
        + [(ctx, mod(hd + e, heads)) for e in range(1, heads)]
    )
    for dev in partners:
        pl.semaphore_signal(barrier, inc=1, device_id=dev, device_id_type=MESH)

    cot_load = pltpu.make_async_copy(cot_hbm, cot_ref, loc_sem.at[1])
    k_load = pltpu.make_async_copy(k_hbm, kbuf, loc_sem.at[2])
    own_ad = pl.ds(pl.multiple_of((z * xn + x) * cpd, cpd), cpd)
    ad_load = pltpu.make_async_copy(ad_hbm, adp.at[own_ad], loc_sem.at[3])
    late_loads = [
        pltpu.make_async_copy(gain_hbm, gain_ref, loc_sem.at[4]),
        pltpu.make_async_copy(src_hbm, src_ref, loc_sem.at[5]),
    ]
    for k in range(kvl):
        late_loads.append(
            pltpu.make_async_copy(
                v_hbm.at[:, k * HD : (k + 1) * HD], vaug.at[k, :, 0:HD], loc_sem.at[6 + k]
            )
        )
    for load in [cot_load, k_load, ad_load] + late_loads:
        load.start()

    q_load.wait()
    qf = q_ref[...].astype(F32)
    for k in range(kvl):
        qall[k, 0, pl.ds(z, 1)] = jnp.concatenate(
            [qf[:, (k * GROUP + h) * HD : (k * GROUP + h + 1) * HD] for h in range(GROUP)], axis=0
        ).astype(BF16)[None]
    cot_load.wait()
    cf = cot_ref[...].astype(F32)
    cz[pl.ds(z, 1)] = jnp.concatenate(
        [cf[:, g * LANES : (g + 1) * LANES] for g in range(groups)], axis=0
    ).astype(BF16)[None]
    pl.semaphore_wait(barrier, len(partners))

    def z_group(make):
        copies = {d: make(d) for d in ring}
        for copy in copies.values():
            copy.start()
        return copies

    def received(copies):
        for copy in copies.values():
            copy.wait_recv()

    def sent(*groups_of_copies):
        for copies in groups_of_copies:
            for copy in copies.values():
                copy.wait_send()

    zq = z_group(lambda d: rcopy(qall.at[:, 0, z], qall.at[:, 0, z], zq_s.at[d], zq_r.at[d], z_dev(d)))
    zc = z_group(lambda d: rcopy(cz.at[z], cz.at[z], zc_s.at[d], zc_r.at[d], z_dev(d)))

    k_load.wait()
    for k in range(kvl):
        k_t[k] = kbuf[:, k * HD : (k + 1) * HD].astype(F32).T.astype(BF16)
    for k in range(kvl):
        vaug[k, :, HD : 2 * HD] = jnp.ones((vaug.shape[1], HD), BF16)

    def q_copy(k, i):
        return rcopy(qall.at[k, 0], qall.at[k, i], q2_s.at[k * nb + i], q2_r.at[k * nb + i], plus_dev(i))

    received(zq)
    for k in range(kvl):
        for i in range(1, nb):
            q_copy(k, i).start()

    for d in range(zn):
        for e in range(1, xn):
            other = pl.multiple_of((d * xn + mod(x + e, xn)) * cpd, cpd)
            adp[pl.ds(other, cpd), :] = jnp.zeros((cpd, nh * HD), BF16)
    st1s[...] = jnp.zeros_like(st1s)
    ad_load.wait()
    za = z_group(lambda d: rcopy(adp.at[own_ad], adp.at[own_ad], za_s.at[d], za_r.at[d], z_dev(d)))
    for load in late_loads:
        load.wait()

    factor = (HD ** -0.5) * LOG2E
    qrows = zn * kr
    eye = iota((qrows, LANES), 0) == iota((qrows, LANES), 1)

    def stat_tile(row):
        high, middle, low = split3(row)
        line = iota((kr, LANES), 0)
        tile = jnp.where(line == 0, high.astype(F32), jnp.where(line == 1, middle.astype(F32), low.astype(F32)))
        return jnp.where(line < 3, tile, 0.0).astype(BF16)

    def stat_row(tile):
        wide = tile.astype(F32)
        return wide[0:1, :] + wide[1:2, :] + wide[2:3, :]

    def score(k, i, count, buf):
        q = qall[k, i : i + count].reshape(count * qrows, HD)
        buf[0 : count * qrows, :] = nn(q, k_t[k])

    def weigh(k, i, count, buf):
        s = buf[0 : count * qrows, :]
        m = jnp.max(s, axis=1, keepdims=True)
        p = jnp.exp2((buf[0 : count * qrows, :] - m) * factor).astype(BF16)
        oa = nn(p, vaug[k])
        total = oa[:, HD : 2 * HD]
        o = (oa[:, 0:HD] / total).astype(BF16)
        lse = m * factor + jnp.log2(total)
        for c in range(count):
            part = slice(c * qrows, (c + 1) * qrows)
            osend[k * nb + i + c, 0:zn] = o[part].reshape(zn, kr, HD)
            row = jnp.sum(jnp.where(eye, lse[part], 0.0), axis=0, keepdims=True)
            osend[k * nb + i + c, zn] = stat_tile(row)
            if i + c > 0:
                o_copy(k * nb + i + c, i + c).start()

    def o_copy(j, i):
        return rcopy(osend.at[j], orecv.at[j], o_s.at[j], o_r.at[j], minus_dev(i))

    half = nb // 2
    units = [(0, 1, half - 1), (0, half, half), (1, 1, half), (1, half + 1, half - 1)]

    def begin(n):
        k, i, count = units[n]
        for c in range(count):
            q_copy(k, i + c).wait_recv()
        score(*units[n], sbuf[n % 2])

    def z_copies(k):
        return {
            d: rcopy(zsend.at[k, z_plus(d)], zrecv.at[k, d], zr_s.at[k * zn + d], zr_r.at[k * zn + d], z_dev(d))
            for d in ring
        }

    def combine(k):
        for i in range(1, nb):
            o_copy(k * nb + i, i).wait_recv()
        parts = [(osend if i == 0 else orecv).at[k * nb + i] for i in range(nb)]
        stats = [stat_row(part[zn]) for part in parts]
        top = functools.reduce(jnp.maximum, stats)
        weights = [jnp.exp2(st - top) for st in stats]
        weight_sum = functools.reduce(jnp.add, weights)
        inverse = 1.0 / weight_sum
        acc = jnp.zeros((qrows, HD), F32)
        for i in range(nb):
            share = jnp.where(eye, weights[i] * inverse, 0.0)[:, 0:qrows].astype(BF16)
            acc = acc + nn(share, parts[i][0:zn].reshape(qrows, HD))
        zsend[k, :, 0:kr, :] = acc.astype(BF16).reshape(zn, kr, HD)
        tile = stat_tile(top + jnp.log2(weight_sum))
        for d in range(zn):
            zsend[k, d, kr : 2 * kr, :] = tile
        for copy in z_copies(k).values():
            copy.start()

    mine = iota((kr, LANES), 1) == iota((kr, LANES), 0) + z * kr

    def settle(k, copies):
        received(copies)
        parts = [zsend[k, z]] + [zrecv[k, d] for d in range(1, zn)]
        stats = [stat_row(part[kr : 2 * kr, :]) for part in parts]
        top = functools.reduce(jnp.maximum, stats)
        weights = [jnp.exp2(st - top) for st in stats]
        inverse = 1.0 / functools.reduce(jnp.add, weights)
        acc = jnp.zeros((kr, HD), F32)
        for d in range(zn):
            column = jnp.sum(jnp.where(mine, weights[d] * inverse, 0.0), axis=1, keepdims=True)
            acc = acc + column * parts[d][0:kr, :].astype(F32)
        hz[k, pl.ds(z, 1)] = acc.astype(BF16)[None]
        return z_group(
            lambda d: rcopy(hz.at[k, z], hz.at[k, z], hz_s.at[k * zn + d], hz_r.at[k * zn + d], z_dev(d))
        )

    def spread(k, copies):
        received(copies)
        pieces = nn(regroup_h[...], hz[k].reshape(zn * kr, HD)).astype(BF16)
        for h in range(GROUP):
            hall[k, pl.ds(b, 1), :, h * HD : (h + 1) * HD] = pieces[h * tb : (h + 1) * tb, :][None]
        copies = {
            i: rcopy(hall.at[k, b], hall.at[k, b], h2_s.at[k * nb + i], h2_r.at[k * nb + i], plus_dev(i))
            for i in range(1, nb)
        }
        for copy in copies.values():
            copy.start()
        return copies

    def project(k, copies):
        gain = gain_ref[...].astype(F32)
        for i in (0, *range(nb - 1, 0, -1)):
            if i > 0:
                copies[i].wait_recv()
            my, mx = minus(i)
            there = my * xn + mx
            hidden = hall[k, there].astype(F32)
            lines = pl.ds(pl.multiple_of(there * tb, tb), tb)
            partial = jnp.zeros((tb, HD), F32)
            for h in range(GROUP):
                piece = hidden[:, h * HD : (h + 1) * HD]
                partial = partial + piece * piece
                head = k * GROUP + h
                gall[lines, head * HD : (head + 1) * HD] = (piece * gain[head : head + 1, :]).astype(BF16)
            squares[lines, :] = partial if k == 0 else squares[lines, :] + partial
        width = GROUP * HD
        part = nn(gall[:, k * width : (k + 1) * width], ad_t[k * width : (k + 1) * width, :])
        mpre[...] = part if k == 0 else mpre[...] + part

    def turn_adapter(k):
        for h in range(k * GROUP, (k + 1) * GROUP):
            for first in range(0, aw, LANES):
                ad_t[h * HD : (h + 1) * HD, first : first + LANES] = (
                    adp[first : first + LANES, h * HD : (h + 1) * HD].astype(F32).T.astype(BF16)
                )

    score(0, 0, 1, sbuf[0])
    score(1, 0, 1, sbuf[1])
    weigh(0, 0, 1, sbuf[0])
    weigh(1, 0, 1, sbuf[1])
    begin(0)
    for n, unit in enumerate(units):
        if n + 1 < len(units):
            begin(n + 1)
        weigh(*unit, sbuf[n % 2])

    regroup_h[...] = regroup(GROUP, zn)
    received(zc)
    pieces = nn(regroup(groups, zn), cz[...].reshape(zn * groups * 2, LANES))
    cg[...] = pieces.astype(BF16).reshape(groups, tb, LANES)
    my_group = div(ctx, per_group)
    c2 = {}
    for i in range(1, nb):
        py, px = plus(i)
        there = div((py * zn + z) * xn + px, per_group)
        c2[i] = rcopy(cg.at[there], call.at[b], c2_s.at[i], c2_r.at[i], at(py, z, px))
        c2[i].start()
    call[pl.ds(b, 1)] = cg[pl.ds(my_group, 1)]

    combine(0)
    combine(1)
    sent(zq, zc)
    h0 = settle(0, z_copies(0))
    received(za)
    turn_adapter(0)

    sel = iota((rows, rows), 1) == row_of(iota((rows, 1), 0), sizes)
    wanted = jnp.sum(
        jnp.where(sel, jnp.broadcast_to(src_ref[...].astype(F32), (rows, rows)), 0.0),
        axis=1, keepdims=True,
    )
    pick = (wanted == row_of(iota((1, rows), 1), sizes).astype(F32)).astype(F32)
    received(c2)
    cot_rows = nn(pick.T.astype(BF16), call[...].reshape(rows, LANES))
    cot_t[...] = cot_rows.T
    token = iota((nb * 2, 1), 0)
    block = div(token, 2)
    token = 2 * ((div(block, xn) * zn + z) * xn + mod(block, xn)) + mod(token, 2)
    wanted = jnp.sum(
        jnp.where(iota((nb * 2, rows), 1) == token, src_ref[...].astype(F32), 0.0), axis=1, keepdims=True
    )
    pick = (wanted == row_of(iota((1, rows), 1), sizes).astype(F32)).astype(F32)

    h1 = settle(1, z_copies(1))
    g0 = spread(0, h0)
    turn_adapter(1)
    sent(za, z_copies(0), z_copies(1), c2)
    for j in range(kvl * nb):
        if j % nb:
            q_copy(j // nb, j % nb).wait_send()
            o_copy(j, j % nb).wait_send()
    g1 = spread(1, h1)
    project(0, g0)
    sent(h0, h1, g0)
    project(1, g1)

    for first in range(0, aw, LANES):
        mpre_t[first : first + LANES, :] = mpre[:, first : first + LANES].T
    hx[pl.ds(hd, 1), 0:cpd, 0:rows] = mpre_t[own_ad, :][None]
    power = jnp.sum(squares[...].T, axis=0, keepdims=True)
    hx[pl.ds(hd, 1), cpd : cpd + 8, 0:rows] = jnp.broadcast_to(power, (8, rows))[None]
    one_hot = pick.astype(BF16)
    chosen = functools.reduce(jnp.add, [nn(one_hot, term) for term in split3(mpre[...])])
    base = cpd + 8
    for j in range(aw // LANES):
        hx[pl.ds(hd, 1), base + j * 2 * nb : base + (j + 1) * 2 * nb, :] = chosen[
            :, j * LANES : (j + 1) * LANES
        ][None]
    hxc = {}
    for e in range(1, heads):
        hxc[e] = rcopy(hx.at[hd], hx.at[hd], hx_s.at[e], hx_r.at[e], (ctx, mod(hd + e, heads)))
        hxc[e].start()
    sent(g1)
    received(hxc)
    summed = hx[0]
    for e in range(1, heads):
        summed = summed + hx[e]
    scale = lax.rsqrt(summed[cpd : cpd + 1, 0:rows] / eps_div + 1e-05)

    token_scale = jnp.sum(pick * scale, axis=1, keepdims=True)
    for j in range(aw // LANES):
        pre = token_scale * summed[base + j * 2 * nb : base + (j + 1) * 2 * nb, :]
        out = pre / (1.0 + jnp.exp(-pre))
        for d in range(nb):
            st1s[d, 0:2, j * LANES : (j + 1) * LANES] = out[2 * d : 2 * d + 2, :]
    s1 = {}
    for i in range(1, nb):
        py, px = plus(i)
        s1[i] = rcopy(st1s.at[py * xn + px], st1r.at[b], s1_s.at[i], s1_r.at[i], at(py, z, px))
        s1[i].start()
    st1r[pl.ds(b, 1)] = st1s[pl.ds(b, 1)]
    sent(hxc)

    pre = scale * summed[0:cpd, 0:rows]
    sig = 1.0 / (1.0 + jnp.exp(-pre))
    own = pl.multiple_of(mod(ctx, per_group) * cpd, cpd)
    slope = (cot_t[pl.ds(own, cpd), :] * sig * (1.0 + pre * (1.0 - sig)) * scale).astype(BF16)
    grad_ref[...] = nn(slope, gall[...]) * (rows ** -0.5)

    sent(s1)
    received(s1)
    for py in range(yn):
        tile = st1r[py * xn]
        for px in range(1, xn):
            tile = tile + st1r[py * xn + px]
        stu_ref[:, py * aw : (py + 1) * aw] = tile[0:2, :]


def local(sizes, heads, queries, keys, values, norm_gain, adapter, source_row, cotangent):
    yn, zn, xn = sizes
    nb = yn * xn
    tb = 2 * zn
    rows = nb * tb
    positions, kvw = keys.shape
    kvl = kvw // HD
    nh = kvl * GROUP
    nf = nh * HD
    kr = GROUP * 2
    cpd = adapter.shape[0]
    aw = zn * xn * cpd
    groups = cotangent.shape[1] // LANES
    vm = pltpu.VMEM
    dma = pltpu.SemaphoreType.DMA
    scratch = [
        vm(queries.shape, BF16),
        vm((nh, HD), BF16),
        vm((1, rows), jnp.int32),
        vm(cotangent.shape, BF16),
        vm((positions, kvw), BF16),
        vm((kvl, HD, positions), BF16),
        vm((kvl, positions, 2 * HD), BF16),
        vm((kvl, nb, zn, kr, HD), BF16),
        vm((kvl * nb, zn + 1, kr, HD), BF16),
        vm((kvl * nb, zn + 1, kr, HD), BF16),
        vm((kvl, zn, 2 * kr, HD), BF16),
        vm((kvl, zn, 2 * kr, HD), BF16),
        vm((kvl, zn, kr, HD), BF16),
        vm((kvl, nb, tb, GROUP * HD), BF16),
        vm((rows, nf), BF16),
        vm((rows, aw), F32),
        vm((rows, HD), F32),
        vm((heads, cpd + 8 + 2 * nb * (aw // LANES), max(rows, LANES)), F32),
        vm((nb // 2 * zn * kr, positions), F32),
        vm((nb // 2 * zn * kr, positions), F32),
        vm((zn * kr, zn * kr), BF16),
        vm((zn, groups * 2, LANES), BF16),
        vm((groups, tb, LANES), BF16),
        vm((nb, tb, LANES), BF16),
        vm((LANES, rows), F32),
        vm((aw, rows), F32),
        vm((nb, 8, aw), F32),
        vm((nb, 8, aw), F32),
        vm((aw, nf), BF16),
        vm((nf, aw), BF16),
        dma((6 + kvl,)),
        dma((zn,)), dma((zn,)), dma((kvl * nb,)), dma((kvl * nb,)),
        dma((zn,)), dma((zn,)), dma((nb,)), dma((nb,)),
        dma((kvl * nb,)), dma((kvl * nb,)),
        dma((kvl * zn,)), dma((kvl * zn,)), dma((kvl * zn,)), dma((kvl * zn,)),
        dma((kvl * nb,)), dma((kvl * nb,)),
        dma((heads,)), dma((heads,)),
        dma((nb,)), dma((nb,)), dma((zn,)), dma((zn,)),
    ]
    args = (queries, keys, values, norm_gain.reshape(nh, HD), adapter, source_row.reshape(1, -1), cotangent)
    vmem = pl.BlockSpec(memory_space=pltpu.VMEM)
    hbm = pl.BlockSpec(memory_space=pltpu.HBM)
    return pl.pallas_call(
        functools.partial(kernel, sizes, heads, float(heads * nf)),
        out_shape=(
            pltpu.VMEM(cotangent.shape, F32),
            pltpu.VMEM(adapter.shape, F32),
        ),
        in_specs=[hbm] * 7,
        out_specs=(vmem, vmem),
        scratch_shapes=scratch,
        compiler_params=pltpu.CompilerParams(
            collective_id=0, has_side_effects=True, vmem_limit_bytes=48 * 1024 * 1024
        ),
        cost_estimate=pl.CostEstimate(
            flops=4 * rows * nh * HD * positions,
            bytes_accessed=4 * positions * kvw,
            transcendentals=rows * nh * positions,
        ),
        name="distill",
    )(*(pltpu.with_memory_space_constraint(arg, pltpu.HBM) for arg in args))


def solution(mesh, sizes=(YN, ZN, XN)):
    return jax.shard_map(
        functools.partial(local, sizes, mesh.shape["head"]),
        mesh=mesh,
        in_specs=(
            P("ctx", "head"),
            P("ctx", "head"),
            P("ctx", "head"),
            P("head"),
            P("ctx", "head"),
            P(),
            P("ctx", None),
        ),
        out_specs=(P("ctx", None), P("ctx", "head")),
        check_vma=False,
    )
```

```python
import functools

import jax
import jax.numpy as jnp
from jax import lax
from jax.experimental import pallas as pl
from jax.experimental.pallas import tpu as pltpu
from jax.sharding import PartitionSpec as P

H = 64
HD = 128
GROUP = 8
LANES = 128
LOG2E = 1.4426950408889634
YN, ZN, XN = 4, 8, 2

F32 = jnp.float32
BF16 = jnp.bfloat16
MESH = pl.DeviceIdType.MESH


def iota(shape, axis):
    return lax.broadcasted_iota(jnp.int32, shape, axis)


def nn(left, right):
    return lax.dot_general(left, right, (((1,), (0,)), ((), ())), preferred_element_type=F32)


def div(a, n):
    return a // n if isinstance(a, int) else a >> (n.bit_length() - 1)


def mod(a, n):
    return a % n if isinstance(a, int) else a & (n - 1)


def regroup(outer, zn):
    size = outer * zn * 2
    row, col = iota((size, 1), 0), iota((size, size), 1)
    head, rest = div(row, 2 * zn), mod(row, 2 * zn)
    return (col == div(rest, 2) * (2 * outer) + head * 2 + mod(rest, 2)).astype(F32).astype(BF16)


def row_of(position, sizes):
    yn, zn, xn = sizes
    pair, block = div(position, 2), div(position, 2 * zn)
    ctx = (div(block, xn) * zn + mod(pair, zn)) * xn + mod(block, xn)
    return 2 * ctx + mod(position, 2)


def split3(value):
    high = value.astype(BF16)
    rest = value - high.astype(F32)
    middle = rest.astype(BF16)
    return high, middle, (rest - middle.astype(F32)).astype(BF16)


def kernel(sizes, heads, eps_div, q_hbm, k_hbm, v_hbm, gain_hbm, ad_hbm, src_hbm, cot_hbm,
           stu_ref, grad_ref,
           q_ref, gain_ref, src_ref, cot_ref, kbuf, k_t, v_own, qall, osend, orecv, zsend, zrecv,
           hz, hall, gall, mpre, squares, hx, s_even, s_odd, regroup_h, cz, cg, call, cot_t, mpre_t, st1s, st1r,
           adp, ad_t,
           loc_sem, zq_s, zq_r, q2_s, q2_r, zc_s, zc_r, c2_s, c2_r, o_s, o_r,
           zr_s, zr_r, hz_s, hz_r, h2_s, h2_r, hx_s, hx_r, s1_s, s1_r, za_s, za_r):
    sbuf = (s_even, s_odd)
    yn, zn, xn = sizes
    nb = yn * xn
    tb = 2 * zn
    rows = nb * tb
    kvl = k_hbm.shape[1] // HD
    nh = kvl * GROUP
    kr = GROUP * 2
    cpd = ad_hbm.shape[0]
    per_group = LANES // cpd
    aw = zn * xn * cpd
    groups = cot_hbm.shape[1] // LANES

    ctx = lax.axis_index("ctx")
    hd = lax.axis_index("head")
    y = div(ctx, zn * xn)
    z = mod(div(ctx, xn), zn)
    x = mod(ctx, xn)
    b = y * xn + x

    def at(y_, z_, x_):
        return ((y_ * zn + z_) * xn + x_, hd)

    def z_plus(d):
        return mod(z + d, zn)

    ring = sorted(range(1, zn), key=lambda d: -min(d, zn - d))

    def z_dev(d):
        return at(y, z_plus(d), x)

    others = [(dy, dx) for dy in range(yn) for dx in range(xn) if dy or dx]
    steps = [(0, 0)] + sorted(others, key=lambda st: (-min(st[0], yn - st[0]) - st[1], -st[1], st[0]))

    def plus(i):
        dy, dx = steps[i]
        return mod(y + dy, yn), mod(x + dx, xn)

    def minus(i):
        dy, dx = steps[i]
        return mod(y + yn - dy, yn), mod(x + xn - dx, xn)

    def plus_dev(i):
        py, px = plus(i)
        return at(py, z, px)

    def minus_dev(i):
        py, px = minus(i)
        return at(py, z, px)

    def rcopy(src, dst, ssem, rsem, dev):
        return pltpu.make_async_remote_copy(
            src_ref=src, dst_ref=dst, send_sem=ssem, recv_sem=rsem, device_id=dev, device_id_type=MESH
        )

    q_load = pltpu.make_async_copy(q_hbm, q_ref, loc_sem.at[0])
    q_load.start()
    barrier = pltpu.get_barrier_semaphore()
    partners = (
        [z_dev(d) for d in range(1, zn)]
        + [plus_dev(i) for i in range(1, nb)]
        + [(ctx, mod(hd + e, heads)) for e in range(1, heads)]
    )
    for dev in partners:
        pl.semaphore_signal(barrier, inc=1, device_id=dev, device_id_type=MESH)

    cot_load = pltpu.make_async_copy(cot_hbm, cot_ref, loc_sem.at[1])
    k_load = pltpu.make_async_copy(k_hbm, kbuf, loc_sem.at[2])
    own_ad = pl.ds(pl.multiple_of((z * xn + x) * cpd, cpd), cpd)
    ad_load = pltpu.make_async_copy(ad_hbm, adp.at[own_ad], loc_sem.at[3])
    late_loads = [
        pltpu.make_async_copy(gain_hbm, gain_ref, loc_sem.at[4]),
        pltpu.make_async_copy(src_hbm, src_ref, loc_sem.at[5]),
    ]
    for k in range(kvl):
        late_loads.append(
            pltpu.make_async_copy(
                v_hbm.at[:, k * HD : (k + 1) * HD], v_own.at[k], loc_sem.at[6 + k]
            )
        )
    for load in [cot_load, k_load, ad_load] + late_loads:
        load.start()

    q_load.wait()
    qf = q_ref[...].astype(F32)
    for k in range(kvl):
        qall[k, 0, pl.ds(z, 1)] = jnp.concatenate(
            [qf[:, (k * GROUP + h) * HD : (k * GROUP + h + 1) * HD] for h in range(GROUP)], axis=0
        ).astype(BF16)[None]
    cot_load.wait()
    cf = cot_ref[...].astype(F32)
    cz[pl.ds(z, 1)] = jnp.concatenate(
        [cf[:, g * LANES : (g + 1) * LANES] for g in range(groups)], axis=0
    ).astype(BF16)[None]
    pl.semaphore_wait(barrier, len(partners))

    def z_group(make):
        copies = {d: make(d) for d in ring}
        for copy in copies.values():
            copy.start()
        return copies

    def received(copies):
        for copy in copies.values():
            copy.wait_recv()

    def sent(*groups_of_copies):
        for copies in groups_of_copies:
            for copy in copies.values():
                copy.wait_send()

    zq = z_group(lambda d: rcopy(qall.at[:, 0, z], qall.at[:, 0, z], zq_s.at[d], zq_r.at[d], z_dev(d)))
    zc = z_group(lambda d: rcopy(cz.at[z], cz.at[z], zc_s.at[d], zc_r.at[d], z_dev(d)))

    k_load.wait()
    for k in range(kvl):
        k_t[k] = kbuf[:, k * HD : (k + 1) * HD].astype(F32).T.astype(BF16)

    def q_copy(k, i):
        return rcopy(qall.at[k, 0], qall.at[k, i], q2_s.at[k * nb + i], q2_r.at[k * nb + i], plus_dev(i))

    received(zq)
    for k in range(kvl):
        for i in range(1, nb):
            q_copy(k, i).start()

    for d in range(zn):
        for e in range(1, xn):
            other = pl.multiple_of((d * xn + mod(x + e, xn)) * cpd, cpd)
            adp[pl.ds(other, cpd), :] = jnp.zeros((cpd, nh * HD), BF16)
    st1s[...] = jnp.zeros_like(st1s)
    ad_load.wait()
    za = z_group(lambda d: rcopy(adp.at[own_ad], adp.at[own_ad], za_s.at[d], za_r.at[d], z_dev(d)))
    for load in late_loads:
        load.wait()

    factor = (HD ** -0.5) * LOG2E
    qrows = zn * kr
    eye = iota((qrows, LANES), 0) == iota((qrows, LANES), 1)

    def stat_tile(row):
        high, middle, low = split3(row)
        line = iota((kr, LANES), 0)
        tile = jnp.where(line == 0, high.astype(F32), jnp.where(line == 1, middle.astype(F32), low.astype(F32)))
        return jnp.where(line < 3, tile, 0.0).astype(BF16)

    def stat_row(tile):
        wide = tile.astype(F32)
        return wide[0:1, :] + wide[1:2, :] + wide[2:3, :]

    def score(k, i, count, buf):
        q = qall[k, i : i + count].reshape(count * qrows, HD)
        buf[0 : count * qrows, :] = nn(q, k_t[k])

    def weigh(k, i, count, buf):
        s = buf[0 : count * qrows, :]
        m = jnp.max(s, axis=1, keepdims=True)
        p = jnp.exp2((buf[0 : count * qrows, :] - m) * factor)
        total = jnp.sum(p, axis=1, keepdims=True)
        o = (nn(p.astype(BF16), v_own[k]) * (1.0 / total)).astype(BF16)
        lse = m * factor + jnp.log2(total)
        for c in range(count):
            part = slice(c * qrows, (c + 1) * qrows)
            osend[k * nb + i + c, 0:zn] = o[part].reshape(zn, kr, HD)
            row = jnp.sum(jnp.where(eye, lse[part], 0.0), axis=0, keepdims=True)
            osend[k * nb + i + c, zn] = stat_tile(row)
            if i + c > 0:
                o_copy(k * nb + i + c, i + c).start()

    def o_copy(j, i):
        return rcopy(osend.at[j], orecv.at[j], o_s.at[j], o_r.at[j], minus_dev(i))

    units = [(1, nb // 2 - 1), (nb // 2, nb // 2)]

    def queries_here(k, i, count):
        for c in range(count):
            q_copy(k, i + c).wait_recv()

    def attend(k, carry):
        for n, (i, count) in enumerate(units):
            here, there = sbuf[n % 2], sbuf[(n + 1) % 2]
            if n + 1 < len(units):
                queries_here(k, *units[n + 1])
                score(k, *units[n + 1], there)
                weigh(k, i, count, here)
            else:

                later = jnp.minimum(k + 1, kvl - 1)

                @pl.when(k + 1 < kvl)
                def _():
                    queries_here(later, *units[0])

                score(later, *units[0], there)
                weigh(k, i, count, here)
        return carry

    def z_copies(k):
        return {
            d: rcopy(zsend.at[k, z_plus(d)], zrecv.at[k, d], zr_s.at[k * zn + d], zr_r.at[k * zn + d], z_dev(d))
            for d in ring
        }

    def combine(k):
        for i in range(1, nb):
            o_copy(k * nb + i, i).wait_recv()
        parts = [(osend if i == 0 else orecv).at[k * nb + i] for i in range(nb)]
        stats = [stat_row(part[zn]) for part in parts]
        top = functools.reduce(jnp.maximum, stats)
        weights = [jnp.exp2(st - top) for st in stats]
        weight_sum = functools.reduce(jnp.add, weights)
        inverse = 1.0 / weight_sum
        acc = jnp.zeros((qrows, HD), F32)
        for i in range(nb):
            share = jnp.where(eye, weights[i] * inverse, 0.0)[:, 0:qrows].astype(BF16)
            acc = acc + nn(share, parts[i][0:zn].reshape(qrows, HD))
        zsend[k, :, 0:kr, :] = acc.astype(BF16).reshape(zn, kr, HD)
        tile = stat_tile(top + jnp.log2(weight_sum))
        for d in range(zn):
            zsend[k, d, kr : 2 * kr, :] = tile
        for copy in z_copies(k).values():
            copy.start()

    mine = iota((kr, LANES), 1) == iota((kr, LANES), 0) + z * kr

    def settle(k, copies):
        received(copies)
        parts = [zsend[k, z]] + [zrecv[k, d] for d in range(1, zn)]
        stats = [stat_row(part[kr : 2 * kr, :]) for part in parts]
        top = functools.reduce(jnp.maximum, stats)
        weights = [jnp.exp2(st - top) for st in stats]
        inverse = 1.0 / functools.reduce(jnp.add, weights)
        acc = jnp.zeros((kr, HD), F32)
        for d in range(zn):
            column = jnp.sum(jnp.where(mine, weights[d] * inverse, 0.0), axis=1, keepdims=True)
            acc = acc + column * parts[d][0:kr, :].astype(F32)
        hz[k, pl.ds(z, 1)] = acc.astype(BF16)[None]
        return z_group(
            lambda d: rcopy(hz.at[k, z], hz.at[k, z], hz_s.at[k * zn + d], hz_r.at[k * zn + d], z_dev(d))
        )

    def spread(k, copies):
        received(copies)
        pieces = nn(regroup_h[...], hz[k].reshape(zn * kr, HD)).astype(BF16)
        for h in range(GROUP):
            hall[k, pl.ds(b, 1), :, h * HD : (h + 1) * HD] = pieces[h * tb : (h + 1) * tb, :][None]
        copies = {
            i: rcopy(hall.at[k, b], hall.at[k, b], h2_s.at[k * nb + i], h2_r.at[k * nb + i], plus_dev(i))
            for i in range(1, nb)
        }
        for copy in copies.values():
            copy.start()
        return copies

    def project(k, copies):
        gain = gain_ref[...].astype(F32)
        for i in (0, *range(nb - 1, 0, -1)):
            if i > 0:
                copies[i].wait_recv()
            my, mx = minus(i)
            there = my * xn + mx
            hidden = hall[k, there].astype(F32)
            lines = pl.ds(pl.multiple_of(there * tb, tb), tb)
            partial = jnp.zeros((tb, HD), F32)
            for h in range(GROUP):
                piece = hidden[:, h * HD : (h + 1) * HD]
                partial = partial + piece * piece
                head = k * GROUP + h
                gall[lines, head * HD : (head + 1) * HD] = (piece * gain[head : head + 1, :]).astype(BF16)
            squares[lines, :] = partial if k == 0 else squares[lines, :] + partial
        width = GROUP * HD
        part = nn(gall[:, k * width : (k + 1) * width], ad_t[k * width : (k + 1) * width, :])
        mpre[...] = part if k == 0 else mpre[...] + part

    def turn_adapter(k):
        for h in range(k * GROUP, (k + 1) * GROUP):
            for first in range(0, aw, LANES):
                ad_t[h * HD : (h + 1) * HD, first : first + LANES] = (
                    adp[first : first + LANES, h * HD : (h + 1) * HD].astype(F32).T.astype(BF16)
                )

    def attend_own(k, carry):
        score(k, 0, 1, sbuf[0])
        weigh(k, 0, 1, sbuf[0])
        return carry

    lax.fori_loop(0, kvl, attend_own, 0)
    queries_here(0, *units[0])
    score(0, *units[0], sbuf[0])
    lax.fori_loop(0, kvl, attend, 0)

    regroup_h[...] = regroup(GROUP, zn)
    received(zc)
    pieces = nn(regroup(groups, zn), cz[...].reshape(zn * groups * 2, LANES))
    cg[...] = pieces.astype(BF16).reshape(groups, tb, LANES)
    my_group = div(ctx, per_group)
    c2 = {}
    for i in range(1, nb):
        py, px = plus(i)
        there = div((py * zn + z) * xn + px, per_group)
        c2[i] = rcopy(cg.at[there], call.at[b], c2_s.at[i], c2_r.at[i], at(py, z, px))
        c2[i].start()
    call[pl.ds(b, 1)] = cg[pl.ds(my_group, 1)]

    combine(0)
    combine(1)
    sent(zq, zc)
    h0 = settle(0, z_copies(0))
    received(za)
    turn_adapter(0)

    sel = iota((rows, rows), 1) == row_of(iota((rows, 1), 0), sizes)
    wanted = jnp.sum(
        jnp.where(sel, jnp.broadcast_to(src_ref[...].astype(F32), (rows, rows)), 0.0),
        axis=1, keepdims=True,
    )
    pick = (wanted == row_of(iota((1, rows), 1), sizes).astype(F32)).astype(F32)
    received(c2)
    cot_rows = nn(pick.T.astype(BF16), call[...].reshape(rows, LANES))
    cot_t[...] = cot_rows.T
    token = iota((nb * 2, 1), 0)
    block = div(token, 2)
    token = 2 * ((div(block, xn) * zn + z) * xn + mod(block, xn)) + mod(token, 2)
    wanted = jnp.sum(
        jnp.where(iota((nb * 2, rows), 1) == token, src_ref[...].astype(F32), 0.0), axis=1, keepdims=True
    )
    pick = (wanted == row_of(iota((1, rows), 1), sizes).astype(F32)).astype(F32)

    h1 = settle(1, z_copies(1))
    g0 = spread(0, h0)
    turn_adapter(1)
    sent(za, z_copies(0), z_copies(1), c2)
    for j in range(kvl * nb):
        if j % nb:
            q_copy(j // nb, j % nb).wait_send()
            o_copy(j, j % nb).wait_send()
    g1 = spread(1, h1)
    project(0, g0)
    sent(h0, h1, g0)
    project(1, g1)

    for first in range(0, aw, LANES):
        mpre_t[first : first + LANES, :] = mpre[:, first : first + LANES].T
    hx[pl.ds(hd, 1), 0:cpd, 0:rows] = mpre_t[own_ad, :][None]
    power = jnp.sum(squares[...].T, axis=0, keepdims=True)
    hx[pl.ds(hd, 1), cpd : cpd + 8, 0:rows] = jnp.broadcast_to(power, (8, rows))[None]
    one_hot = pick.astype(BF16)
    chosen = functools.reduce(jnp.add, [nn(one_hot, term) for term in split3(mpre[...])])
    base = cpd + 8
    for j in range(aw // LANES):
        hx[pl.ds(hd, 1), base + j * 2 * nb : base + (j + 1) * 2 * nb, :] = chosen[
            :, j * LANES : (j + 1) * LANES
        ][None]
    hxc = {}
    for e in range(1, heads):
        hxc[e] = rcopy(hx.at[hd], hx.at[hd], hx_s.at[e], hx_r.at[e], (ctx, mod(hd + e, heads)))
        hxc[e].start()
    sent(g1)
    received(hxc)
    summed = hx[0]
    for e in range(1, heads):
        summed = summed + hx[e]
    scale = lax.rsqrt(summed[cpd : cpd + 1, 0:rows] / eps_div + 1e-05)

    token_scale = jnp.sum(pick * scale, axis=1, keepdims=True)
    for j in range(aw // LANES):
        pre = token_scale * summed[base + j * 2 * nb : base + (j + 1) * 2 * nb, :]
        out = pre / (1.0 + jnp.exp(-pre))
        for d in range(nb):
            st1s[d, 0:2, j * LANES : (j + 1) * LANES] = out[2 * d : 2 * d + 2, :]
    s1 = {}
    for i in range(1, nb):
        py, px = plus(i)
        s1[i] = rcopy(st1s.at[py * xn + px], st1r.at[b], s1_s.at[i], s1_r.at[i], at(py, z, px))
        s1[i].start()
    st1r[pl.ds(b, 1)] = st1s[pl.ds(b, 1)]
    sent(hxc)

    pre = scale * summed[0:cpd, 0:rows]
    sig = 1.0 / (1.0 + jnp.exp(-pre))
    own = pl.multiple_of(mod(ctx, per_group) * cpd, cpd)
    slope = (cot_t[pl.ds(own, cpd), :] * sig * (1.0 + pre * (1.0 - sig)) * scale).astype(BF16)
    grad_ref[...] = nn(slope, gall[...]) * (rows ** -0.5)

    sent(s1)
    received(s1)
    for py in range(yn):
        tile = st1r[py * xn]
        for px in range(1, xn):
            tile = tile + st1r[py * xn + px]
        stu_ref[:, py * aw : (py + 1) * aw] = tile[0:2, :]


def local(sizes, heads, queries, keys, values, norm_gain, adapter, source_row, cotangent):
    yn, zn, xn = sizes
    nb = yn * xn
    tb = 2 * zn
    rows = nb * tb
    positions, kvw = keys.shape
    kvl = kvw // HD
    nh = kvl * GROUP
    nf = nh * HD
    kr = GROUP * 2
    cpd = adapter.shape[0]
    aw = zn * xn * cpd
    groups = cotangent.shape[1] // LANES
    vm = pltpu.VMEM
    dma = pltpu.SemaphoreType.DMA
    scratch = [
        vm(queries.shape, BF16),
        vm((nh, HD), BF16),
        vm((1, rows), jnp.int32),
        vm(cotangent.shape, BF16),
        vm((positions, kvw), BF16),
        vm((kvl, HD, positions), BF16),
        vm((kvl, positions, HD), BF16),
        vm((kvl, nb, zn, kr, HD), BF16),
        vm((kvl * nb, zn + 1, kr, HD), BF16),
        vm((kvl * nb, zn + 1, kr, HD), BF16),
        vm((kvl, zn, 2 * kr, HD), BF16),
        vm((kvl, zn, 2 * kr, HD), BF16),
        vm((kvl, zn, kr, HD), BF16),
        vm((kvl, nb, tb, GROUP * HD), BF16),
        vm((rows, nf), BF16),
        vm((rows, aw), F32),
        vm((rows, HD), F32),
        vm((heads, cpd + 8 + 2 * nb * (aw // LANES), max(rows, LANES)), F32),
        vm((nb // 2 * zn * kr, positions), F32),
        vm((nb // 2 * zn * kr, positions), F32),
        vm((zn * kr, zn * kr), BF16),
        vm((zn, groups * 2, LANES), BF16),
        vm((groups, tb, LANES), BF16),
        vm((nb, tb, LANES), BF16),
        vm((LANES, rows), F32),
        vm((aw, rows), F32),
        vm((nb, 8, aw), F32),
        vm((nb, 8, aw), F32),
        vm((aw, nf), BF16),
        vm((nf, aw), BF16),
        dma((6 + kvl,)),
        dma((zn,)), dma((zn,)), dma((kvl * nb,)), dma((kvl * nb,)),
        dma((zn,)), dma((zn,)), dma((nb,)), dma((nb,)),
        dma((kvl * nb,)), dma((kvl * nb,)),
        dma((kvl * zn,)), dma((kvl * zn,)), dma((kvl * zn,)), dma((kvl * zn,)),
        dma((kvl * nb,)), dma((kvl * nb,)),
        dma((heads,)), dma((heads,)),
        dma((nb,)), dma((nb,)), dma((zn,)), dma((zn,)),
    ]
    args = (queries, keys, values, norm_gain.reshape(nh, HD), adapter, source_row.reshape(1, -1), cotangent)
    vmem = pl.BlockSpec(memory_space=pltpu.VMEM)
    hbm = pl.BlockSpec(memory_space=pltpu.HBM)
    return pl.pallas_call(
        functools.partial(kernel, sizes, heads, float(heads * nf)),
        out_shape=(
            pltpu.VMEM(cotangent.shape, F32),
            pltpu.VMEM(adapter.shape, F32),
        ),
        in_specs=[hbm] * 7,
        out_specs=(vmem, vmem),
        scratch_shapes=scratch,
        compiler_params=pltpu.CompilerParams(
            collective_id=0, has_side_effects=True, vmem_limit_bytes=48 * 1024 * 1024
        ),
        cost_estimate=pl.CostEstimate(
            flops=4 * rows * nh * HD * positions,
            bytes_accessed=4 * positions * kvw,
            transcendentals=rows * nh * positions,
        ),
        name="distill",
    )(*(pltpu.with_memory_space_constraint(arg, pltpu.HBM) for arg in args))


def solution(mesh, sizes=(YN, ZN, XN)):
    return jax.shard_map(
        functools.partial(local, sizes, mesh.shape["head"]),
        mesh=mesh,
        in_specs=(
            P("ctx", "head"),
            P("ctx", "head"),
            P("ctx", "head"),
            P("head"),
            P("ctx", "head"),
            P(),
            P("ctx", None),
        ),
        out_specs=(P("ctx", None), P("ctx", "head")),
        check_vma=False,
    )
```

```python
import functools

import jax
import jax.numpy as jnp
from jax import lax
from jax.experimental import pallas as pl
from jax.experimental.pallas import tpu as pltpu
from jax.sharding import PartitionSpec as P

H = 64
HD = 128
GROUP = 8
LANES = 128
LOG2E = 1.4426950408889634
YN, ZN, XN = 4, 8, 2

F32 = jnp.float32
BF16 = jnp.bfloat16
MESH = pl.DeviceIdType.MESH


def iota(shape, axis):
    return lax.broadcasted_iota(jnp.int32, shape, axis)


def nn(left, right):
    return lax.dot_general(left, right, (((1,), (0,)), ((), ())), preferred_element_type=F32)


def div(a, n):
    return a // n if isinstance(a, int) else a >> (n.bit_length() - 1)


def mod(a, n):
    return a % n if isinstance(a, int) else a & (n - 1)


def regroup(outer, zn):
    size = outer * zn * 2
    row, col = iota((size, 1), 0), iota((size, size), 1)
    head, rest = div(row, 2 * zn), mod(row, 2 * zn)
    return (col == div(rest, 2) * (2 * outer) + head * 2 + mod(rest, 2)).astype(F32).astype(BF16)


def row_of(position, sizes):
    yn, zn, xn = sizes
    pair, block = div(position, 2), div(position, 2 * zn)
    ctx = (div(block, xn) * zn + mod(pair, zn)) * xn + mod(block, xn)
    return 2 * ctx + mod(position, 2)


def split3(value):
    high = value.astype(BF16)
    rest = value - high.astype(F32)
    middle = rest.astype(BF16)
    return high, middle, (rest - middle.astype(F32)).astype(BF16)


def kernel(sizes, heads, eps_div, q_hbm, k_hbm, v_hbm, gain_hbm, ad_hbm, src_hbm, cot_hbm,
           stu_ref, grad_ref,
           q_ref, gain_ref, src_ref, cot_ref, kbuf, k_t, vaug, qall, osend, orecv, zsend, zrecv,
           hz, hall, gall, mpre, squares, hx, s_even, s_odd, regroup_h, cz, cg, call, cot_t, mpre_t, st1s, st1r,
           adp, ad_t,
           loc_sem, zq_s, zq_r, q2_s, q2_r, zc_s, zc_r, c2_s, c2_r, o_s, o_r,
           zr_s, zr_r, hz_s, hz_r, h2_s, h2_r, hx_s, hx_r, s1_s, s1_r, za_s, za_r):
    sbuf = (s_even, s_odd)
    yn, zn, xn = sizes
    nb = yn * xn
    tb = 2 * zn
    rows = nb * tb
    kvl = k_hbm.shape[1] // HD
    nh = kvl * GROUP
    kr = GROUP * 2
    cpd = ad_hbm.shape[0]
    per_group = LANES // cpd
    aw = zn * xn * cpd
    groups = cot_hbm.shape[1] // LANES

    ctx = lax.axis_index("ctx")
    hd = lax.axis_index("head")
    y = div(ctx, zn * xn)
    z = mod(div(ctx, xn), zn)
    x = mod(ctx, xn)
    b = y * xn + x

    def at(y_, z_, x_):
        return ((y_ * zn + z_) * xn + x_, hd)

    def z_plus(d):
        return mod(z + d, zn)

    ring = sorted(range(1, zn), key=lambda d: -min(d, zn - d))

    def z_dev(d):
        return at(y, z_plus(d), x)

    others = [(dy, dx) for dy in range(yn) for dx in range(xn) if dy or dx]
    steps = [(0, 0)] + sorted(others, key=lambda st: (-min(st[0], yn - st[0]) - st[1], -st[1], st[0]))

    def plus(i):
        dy, dx = steps[i]
        return mod(y + dy, yn), mod(x + dx, xn)

    def minus(i):
        dy, dx = steps[i]
        return mod(y + yn - dy, yn), mod(x + xn - dx, xn)

    def plus_dev(i):
        py, px = plus(i)
        return at(py, z, px)

    def minus_dev(i):
        py, px = minus(i)
        return at(py, z, px)

    def rcopy(src, dst, ssem, rsem, dev):
        return pltpu.make_async_remote_copy(
            src_ref=src, dst_ref=dst, send_sem=ssem, recv_sem=rsem, device_id=dev, device_id_type=MESH
        )

    q_load = pltpu.make_async_copy(q_hbm, q_ref, loc_sem.at[0])
    q_load.start()
    barrier = pltpu.get_barrier_semaphore()
    partners = (
        [z_dev(d) for d in range(1, zn)]
        + [plus_dev(i) for i in range(1, nb)]
        + [(ctx, mod(hd + e, heads)) for e in range(1, heads)]
    )
    for dev in partners:
        pl.semaphore_signal(barrier, inc=1, device_id=dev, device_id_type=MESH)

    cot_load = pltpu.make_async_copy(cot_hbm, cot_ref, loc_sem.at[1])
    k_load = pltpu.make_async_copy(k_hbm, kbuf, loc_sem.at[2])
    own_ad = pl.ds(pl.multiple_of((z * xn + x) * cpd, cpd), cpd)
    ad_load = pltpu.make_async_copy(ad_hbm, adp.at[own_ad], loc_sem.at[3])
    late_loads = [
        pltpu.make_async_copy(gain_hbm, gain_ref, loc_sem.at[4]),
        pltpu.make_async_copy(src_hbm, src_ref, loc_sem.at[5]),
    ]
    for k in range(kvl):
        late_loads.append(
            pltpu.make_async_copy(
                v_hbm.at[:, k * HD : (k + 1) * HD], vaug.at[k, :, 0:HD], loc_sem.at[6 + k]
            )
        )
    for load in [cot_load, k_load, ad_load] + late_loads:
        load.start()

    q_load.wait()
    qf = q_ref[...].astype(F32)
    for k in range(kvl):
        qall[k, 0, pl.ds(z, 1)] = jnp.concatenate(
            [qf[:, (k * GROUP + h) * HD : (k * GROUP + h + 1) * HD] for h in range(GROUP)], axis=0
        ).astype(BF16)[None]
    cot_load.wait()
    cf = cot_ref[...].astype(F32)
    cz[pl.ds(z, 1)] = jnp.concatenate(
        [cf[:, g * LANES : (g + 1) * LANES] for g in range(groups)], axis=0
    ).astype(BF16)[None]
    pl.semaphore_wait(barrier, len(partners))

    def z_group(make):
        copies = {d: make(d) for d in ring}
        for copy in copies.values():
            copy.start()
        return copies

    def received(copies):
        for copy in copies.values():
            copy.wait_recv()

    def sent(*groups_of_copies):
        for copies in groups_of_copies:
            for copy in copies.values():
                copy.wait_send()

    zq = z_group(lambda d: rcopy(qall.at[:, 0, z], qall.at[:, 0, z], zq_s.at[d], zq_r.at[d], z_dev(d)))
    zc = z_group(lambda d: rcopy(cz.at[z], cz.at[z], zc_s.at[d], zc_r.at[d], z_dev(d)))

    k_load.wait()
    for k in range(kvl):
        k_t[k] = kbuf[:, k * HD : (k + 1) * HD].astype(F32).T.astype(BF16)
    for k in range(kvl):
        vaug[k, :, HD : 2 * HD] = jnp.ones((vaug.shape[1], HD), BF16)

    def q_copy(k, i):
        return rcopy(qall.at[k, 0], qall.at[k, i], q2_s.at[k * nb + i], q2_r.at[k * nb + i], plus_dev(i))

    received(zq)
    for k in range(kvl):
        for i in range(1, nb):
            q_copy(k, i).start()

    for d in range(zn):
        for e in range(1, xn):
            other = pl.multiple_of((d * xn + mod(x + e, xn)) * cpd, cpd)
            adp[pl.ds(other, cpd), :] = jnp.zeros((cpd, nh * HD), BF16)
    st1s[...] = jnp.zeros_like(st1s)
    ad_load.wait()
    za = z_group(lambda d: rcopy(adp.at[own_ad], adp.at[own_ad], za_s.at[d], za_r.at[d], z_dev(d)))
    for load in late_loads:
        load.wait()

    factor = (HD ** -0.5) * LOG2E
    qrows = zn * kr
    eye = iota((qrows, LANES), 0) == iota((qrows, LANES), 1)

    def stat_tile(*lines):
        at_line = iota((kr, LANES), 0)
        tile = jnp.zeros((kr, LANES), F32)
        for n, term in enumerate(term for line in lines for term in split3(line)):
            tile = jnp.where(at_line == n, term.astype(F32), tile)
        return tile.astype(BF16)

    def stat_row(tile, n=0):
        wide = tile.astype(F32)
        return wide[3 * n : 3 * n + 1, :] + wide[3 * n + 1 : 3 * n + 2, :] + wide[3 * n + 2 : 3 * n + 3, :]

    def score(k, i, count, buf):
        q = qall[k, i : i + count].reshape(count * qrows, HD)
        buf[0 : count * qrows, :] = nn(q, k_t[k])

    def weigh(k, i, count, buf):
        s = buf[0 : count * qrows, :]
        m = jnp.max(s, axis=1, keepdims=True)
        p = jnp.exp2((buf[0 : count * qrows, :] - m) * factor).astype(BF16)
        oa = nn(p, vaug[k])
        total = oa[:, HD : 2 * HD]
        o = oa[:, 0:HD].astype(BF16)
        for c in range(count):
            part = slice(c * qrows, (c + 1) * qrows)
            osend[k * nb + i + c, 0:zn] = o[part].reshape(zn, kr, HD)
            top, weight = (
                jnp.sum(jnp.where(eye, column[part], 0.0), axis=0, keepdims=True) for column in (m, total)
            )
            osend[k * nb + i + c, zn] = stat_tile(top * factor, weight)
            if i + c > 0:
                o_copy(k * nb + i + c, i + c).start()

    def o_copy(j, i):
        return rcopy(osend.at[j], orecv.at[j], o_s.at[j], o_r.at[j], minus_dev(i))

    units = [(1, nb // 2 - 1), (nb // 2, nb // 2)]

    def queries_here(k, i, count):
        for c in range(count):
            q_copy(k, i + c).wait_recv()

    def attend(k, carry):
        for n, (i, count) in enumerate(units):
            here, there = sbuf[n % 2], sbuf[(n + 1) % 2]
            if n + 1 < len(units):
                queries_here(k, *units[n + 1])
                score(k, *units[n + 1], there)
                weigh(k, i, count, here)
            else:

                later = jnp.minimum(k + 1, kvl - 1)

                @pl.when(k + 1 < kvl)
                def _():
                    queries_here(later, *units[0])

                score(later, *units[0], there)
                weigh(k, i, count, here)
        return carry

    def z_copies(k):
        return {
            d: rcopy(zsend.at[k, z_plus(d)], zrecv.at[k, d], zr_s.at[k * zn + d], zr_r.at[k * zn + d], z_dev(d))
            for d in ring
        }

    def combine(k):
        for i in range(1, nb):
            o_copy(k * nb + i, i).wait_recv()
        parts = [(osend if i == 0 else orecv).at[k * nb + i] for i in range(nb)]
        stats = [stat_row(part[zn]) for part in parts]
        top = functools.reduce(jnp.maximum, stats)
        weights = [jnp.exp2(st - top) for st in stats]
        weight_sum = functools.reduce(
            jnp.add, [weight * stat_row(part[zn], 1) for weight, part in zip(weights, parts)]
        )
        inverse = 1.0 / weight_sum
        acc = jnp.zeros((qrows, HD), F32)
        for i in range(nb):
            share = jnp.where(eye, weights[i] * inverse, 0.0)[:, 0:qrows].astype(BF16)
            acc = acc + nn(share, parts[i][0:zn].reshape(qrows, HD))
        zsend[k, :, 0:kr, :] = acc.astype(BF16).reshape(zn, kr, HD)
        tile = stat_tile(top + jnp.log2(weight_sum))
        for d in range(zn):
            zsend[k, d, kr : 2 * kr, :] = tile
        for copy in z_copies(k).values():
            copy.start()

    mine = iota((kr, LANES), 1) == iota((kr, LANES), 0) + z * kr

    def settle(k, copies):
        received(copies)
        parts = [zsend[k, z]] + [zrecv[k, d] for d in range(1, zn)]
        stats = [stat_row(part[kr : 2 * kr, :]) for part in parts]
        top = functools.reduce(jnp.maximum, stats)
        weights = [jnp.exp2(st - top) for st in stats]
        inverse = 1.0 / functools.reduce(jnp.add, weights)
        acc = jnp.zeros((kr, HD), F32)
        for d in range(zn):
            column = jnp.sum(jnp.where(mine, weights[d] * inverse, 0.0), axis=1, keepdims=True)
            acc = acc + column * parts[d][0:kr, :].astype(F32)
        hz[k, pl.ds(z, 1)] = acc.astype(BF16)[None]
        return z_group(
            lambda d: rcopy(hz.at[k, z], hz.at[k, z], hz_s.at[k * zn + d], hz_r.at[k * zn + d], z_dev(d))
        )

    def spread(k, copies):
        received(copies)
        pieces = nn(regroup_h[...], hz[k].reshape(zn * kr, HD)).astype(BF16)
        for h in range(GROUP):
            hall[k, pl.ds(b, 1), :, h * HD : (h + 1) * HD] = pieces[h * tb : (h + 1) * tb, :][None]
        copies = {
            i: rcopy(hall.at[k, b], hall.at[k, b], h2_s.at[k * nb + i], h2_r.at[k * nb + i], plus_dev(i))
            for i in range(1, nb)
        }
        for copy in copies.values():
            copy.start()
        return copies

    def project(k, copies):
        gain = gain_ref[...].astype(F32)
        for i in (0, *range(nb - 1, 0, -1)):
            if i > 0:
                copies[i].wait_recv()
            my, mx = minus(i)
            there = my * xn + mx
            hidden = hall[k, there].astype(F32)
            lines = pl.ds(pl.multiple_of(there * tb, tb), tb)
            partial = jnp.zeros((tb, HD), F32)
            for h in range(GROUP):
                piece = hidden[:, h * HD : (h + 1) * HD]
                partial = partial + piece * piece
                head = k * GROUP + h
                gall[lines, head * HD : (head + 1) * HD] = (piece * gain[head : head + 1, :]).astype(BF16)
            squares[lines, :] = partial if k == 0 else squares[lines, :] + partial
        width = GROUP * HD
        part = nn(gall[:, k * width : (k + 1) * width], ad_t[k * width : (k + 1) * width, :])
        mpre[...] = part if k == 0 else mpre[...] + part

    def turn_adapter(k):
        for h in range(k * GROUP, (k + 1) * GROUP):
            for first in range(0, aw, LANES):
                ad_t[h * HD : (h + 1) * HD, first : first + LANES] = (
                    adp[first : first + LANES, h * HD : (h + 1) * HD].astype(F32).T.astype(BF16)
                )

    score(0, 0, 1, sbuf[0])
    score(1, 0, 1, sbuf[1])
    weigh(0, 0, 1, sbuf[0])
    weigh(1, 0, 1, sbuf[1])
    queries_here(0, *units[0])
    score(0, *units[0], sbuf[0])
    lax.fori_loop(0, kvl, attend, 0)

    regroup_h[...] = regroup(GROUP, zn)
    received(zc)
    pieces = nn(regroup(groups, zn), cz[...].reshape(zn * groups * 2, LANES))
    cg[...] = pieces.astype(BF16).reshape(groups, tb, LANES)
    my_group = div(ctx, per_group)
    c2 = {}
    for i in range(1, nb):
        py, px = plus(i)
        there = div((py * zn + z) * xn + px, per_group)
        c2[i] = rcopy(cg.at[there], call.at[b], c2_s.at[i], c2_r.at[i], at(py, z, px))
        c2[i].start()
    call[pl.ds(b, 1)] = cg[pl.ds(my_group, 1)]

    combine(0)
    combine(1)
    sent(zq, zc)
    h0 = settle(0, z_copies(0))
    received(za)
    turn_adapter(0)

    sel = iota((rows, rows), 1) == row_of(iota((rows, 1), 0), sizes)
    wanted = jnp.sum(
        jnp.where(sel, jnp.broadcast_to(src_ref[...].astype(F32), (rows, rows)), 0.0),
        axis=1, keepdims=True,
    )
    pick = (wanted == row_of(iota((1, rows), 1), sizes).astype(F32)).astype(F32)
    received(c2)
    cot_rows = nn(pick.T.astype(BF16), call[...].reshape(rows, LANES))
    cot_t[...] = cot_rows.T
    token = iota((nb * 2, 1), 0)
    block = div(token, 2)
    token = 2 * ((div(block, xn) * zn + z) * xn + mod(block, xn)) + mod(token, 2)
    wanted = jnp.sum(
        jnp.where(iota((nb * 2, rows), 1) == token, src_ref[...].astype(F32), 0.0), axis=1, keepdims=True
    )
    pick = (wanted == row_of(iota((1, rows), 1), sizes).astype(F32)).astype(F32)

    h1 = settle(1, z_copies(1))
    g0 = spread(0, h0)
    turn_adapter(1)
    sent(za, z_copies(0), z_copies(1), c2)
    for j in range(kvl * nb):
        if j % nb:
            q_copy(j // nb, j % nb).wait_send()
            o_copy(j, j % nb).wait_send()
    g1 = spread(1, h1)
    project(0, g0)
    sent(h0, h1, g0)
    project(1, g1)

    for first in range(0, aw, LANES):
        mpre_t[first : first + LANES, :] = mpre[:, first : first + LANES].T
    hx[pl.ds(hd, 1), 0:cpd, 0:rows] = mpre_t[own_ad, :][None]
    power = jnp.sum(squares[...].T, axis=0, keepdims=True)
    hx[pl.ds(hd, 1), cpd : cpd + 8, 0:rows] = jnp.broadcast_to(power, (8, rows))[None]
    one_hot = pick.astype(BF16)
    chosen = functools.reduce(jnp.add, [nn(one_hot, term) for term in split3(mpre[...])])
    base = cpd + 8
    for j in range(aw // LANES):
        hx[pl.ds(hd, 1), base + j * 2 * nb : base + (j + 1) * 2 * nb, :] = chosen[
            :, j * LANES : (j + 1) * LANES
        ][None]
    hxc = {}
    for e in range(1, heads):
        hxc[e] = rcopy(hx.at[hd], hx.at[hd], hx_s.at[e], hx_r.at[e], (ctx, mod(hd + e, heads)))
        hxc[e].start()
    sent(g1)
    received(hxc)
    summed = hx[0]
    for e in range(1, heads):
        summed = summed + hx[e]
    scale = lax.rsqrt(summed[cpd : cpd + 1, 0:rows] / eps_div + 1e-05)

    token_scale = jnp.sum(pick * scale, axis=1, keepdims=True)
    for j in range(aw // LANES):
        pre = token_scale * summed[base + j * 2 * nb : base + (j + 1) * 2 * nb, :]
        out = pre / (1.0 + jnp.exp(-pre))
        for d in range(nb):
            st1s[d, 0:2, j * LANES : (j + 1) * LANES] = out[2 * d : 2 * d + 2, :]
    s1 = {}
    for i in range(1, nb):
        py, px = plus(i)
        s1[i] = rcopy(st1s.at[py * xn + px], st1r.at[b], s1_s.at[i], s1_r.at[i], at(py, z, px))
        s1[i].start()
    st1r[pl.ds(b, 1)] = st1s[pl.ds(b, 1)]
    sent(hxc)

    pre = scale * summed[0:cpd, 0:rows]
    sig = 1.0 / (1.0 + jnp.exp(-pre))
    own = pl.multiple_of(mod(ctx, per_group) * cpd, cpd)
    slope = (cot_t[pl.ds(own, cpd), :] * sig * (1.0 + pre * (1.0 - sig)) * scale).astype(BF16)
    grad_ref[...] = nn(slope, gall[...]) * (rows ** -0.5)

    sent(s1)
    received(s1)
    for py in range(yn):
        tile = st1r[py * xn]
        for px in range(1, xn):
            tile = tile + st1r[py * xn + px]
        stu_ref[:, py * aw : (py + 1) * aw] = tile[0:2, :]


def local(sizes, heads, queries, keys, values, norm_gain, adapter, source_row, cotangent):
    yn, zn, xn = sizes
    nb = yn * xn
    tb = 2 * zn
    rows = nb * tb
    positions, kvw = keys.shape
    kvl = kvw // HD
    nh = kvl * GROUP
    nf = nh * HD
    kr = GROUP * 2
    cpd = adapter.shape[0]
    aw = zn * xn * cpd
    groups = cotangent.shape[1] // LANES
    vm = pltpu.VMEM
    dma = pltpu.SemaphoreType.DMA
    scratch = [
        vm(queries.shape, BF16),
        vm((nh, HD), BF16),
        vm((1, rows), jnp.int32),
        vm(cotangent.shape, BF16),
        vm((positions, kvw), BF16),
        vm((kvl, HD, positions), BF16),
        vm((kvl, positions, 2 * HD), BF16),
        vm((kvl, nb, zn, kr, HD), BF16),
        vm((kvl * nb, zn + 1, kr, HD), BF16),
        vm((kvl * nb, zn + 1, kr, HD), BF16),
        vm((kvl, zn, 2 * kr, HD), BF16),
        vm((kvl, zn, 2 * kr, HD), BF16),
        vm((kvl, zn, kr, HD), BF16),
        vm((kvl, nb, tb, GROUP * HD), BF16),
        vm((rows, nf), BF16),
        vm((rows, aw), F32),
        vm((rows, HD), F32),
        vm((heads, cpd + 8 + 2 * nb * (aw // LANES), max(rows, LANES)), F32),
        vm((nb // 2 * zn * kr, positions), F32),
        vm((nb // 2 * zn * kr, positions), F32),
        vm((zn * kr, zn * kr), BF16),
        vm((zn, groups * 2, LANES), BF16),
        vm((groups, tb, LANES), BF16),
        vm((nb, tb, LANES), BF16),
        vm((LANES, rows), F32),
        vm((aw, rows), F32),
        vm((nb, 8, aw), F32),
        vm((nb, 8, aw), F32),
        vm((aw, nf), BF16),
        vm((nf, aw), BF16),
        dma((6 + kvl,)),
        dma((zn,)), dma((zn,)), dma((kvl * nb,)), dma((kvl * nb,)),
        dma((zn,)), dma((zn,)), dma((nb,)), dma((nb,)),
        dma((kvl * nb,)), dma((kvl * nb,)),
        dma((kvl * zn,)), dma((kvl * zn,)), dma((kvl * zn,)), dma((kvl * zn,)),
        dma((kvl * nb,)), dma((kvl * nb,)),
        dma((heads,)), dma((heads,)),
        dma((nb,)), dma((nb,)), dma((zn,)), dma((zn,)),
    ]
    args = (queries, keys, values, norm_gain.reshape(nh, HD), adapter, source_row.reshape(1, -1), cotangent)
    vmem = pl.BlockSpec(memory_space=pltpu.VMEM)
    hbm = pl.BlockSpec(memory_space=pltpu.HBM)
    return pl.pallas_call(
        functools.partial(kernel, sizes, heads, float(heads * nf)),
        out_shape=(
            pltpu.VMEM(cotangent.shape, F32),
            pltpu.VMEM(adapter.shape, F32),
        ),
        in_specs=[hbm] * 7,
        out_specs=(vmem, vmem),
        scratch_shapes=scratch,
        compiler_params=pltpu.CompilerParams(
            collective_id=0, has_side_effects=True, vmem_limit_bytes=48 * 1024 * 1024
        ),
        cost_estimate=pl.CostEstimate(
            flops=4 * rows * nh * HD * positions,
            bytes_accessed=4 * positions * kvw,
            transcendentals=rows * nh * positions,
        ),
        name="distill",
    )(*(pltpu.with_memory_space_constraint(arg, pltpu.HBM) for arg in args))


def solution(mesh, sizes=(YN, ZN, XN)):
    return jax.shard_map(
        functools.partial(local, sizes, mesh.shape["head"]),
        mesh=mesh,
        in_specs=(
            P("ctx", "head"),
            P("ctx", "head"),
            P("ctx", "head"),
            P("head"),
            P("ctx", "head"),
            P(),
            P("ctx", None),
        ),
        out_specs=(P("ctx", None), P("ctx", "head")),
        check_vma=False,
    )
```

```python
import functools

import jax
import jax.numpy as jnp
from jax import lax
from jax.experimental import pallas as pl
from jax.experimental.pallas import tpu as pltpu
from jax.sharding import PartitionSpec as P

H = 64
HD = 128
GROUP = 8
LANES = 128
LOG2E = 1.4426950408889634
YN, ZN, XN = 4, 8, 2

F32 = jnp.float32
BF16 = jnp.bfloat16
MESH = pl.DeviceIdType.MESH


def iota(shape, axis):
    return lax.broadcasted_iota(jnp.int32, shape, axis)


def nn(left, right):
    return lax.dot_general(left, right, (((1,), (0,)), ((), ())), preferred_element_type=F32)


def div(a, n):
    return a // n if isinstance(a, int) else a >> (n.bit_length() - 1)


def mod(a, n):
    return a % n if isinstance(a, int) else a & (n - 1)


def regroup(outer, zn):
    size = outer * zn * 2
    row, col = iota((size, 1), 0), iota((size, size), 1)
    head, rest = div(row, 2 * zn), mod(row, 2 * zn)
    return (col == div(rest, 2) * (2 * outer) + head * 2 + mod(rest, 2)).astype(F32).astype(BF16)


def row_of(position, sizes):
    yn, zn, xn = sizes
    pair, block = div(position, 2), div(position, 2 * zn)
    ctx = (div(block, xn) * zn + mod(pair, zn)) * xn + mod(block, xn)
    return 2 * ctx + mod(position, 2)


def split3(value):
    high = value.astype(BF16)
    rest = value - high.astype(F32)
    middle = rest.astype(BF16)
    return high, middle, (rest - middle.astype(F32)).astype(BF16)


def kernel(sizes, heads, eps_div, q_hbm, k_hbm, v_hbm, gain_hbm, ad_hbm, src_hbm, cot_hbm,
           stu_ref, grad_ref,
           q_ref, gain_ref, src_ref, cot_ref, kbuf, k_t, vaug, qall, osend, orecv, zsend, zrecv,
           hz, hall, gall, mpre, squares, hx, s_even, s_odd, regroup_h, cz, cg, call, cot_t, mpre_t, st1s, st1r,
           adp, ad_t,
           loc_sem, zq_s, zq_r, q2_s, q2_r, zc_s, zc_r, c2_s, c2_r, o_s, o_r,
           zr_s, zr_r, hz_s, hz_r, h2_s, h2_r, hx_s, hx_r, s1_s, s1_r, za_s, za_r):
    sbuf = (s_even, s_odd)
    yn, zn, xn = sizes
    nb = yn * xn
    tb = 2 * zn
    rows = nb * tb
    kvl = k_hbm.shape[1] // HD
    nh = kvl * GROUP
    kr = GROUP * 2
    cpd = ad_hbm.shape[0]
    per_group = LANES // cpd
    aw = zn * xn * cpd
    groups = cot_hbm.shape[1] // LANES

    ctx = lax.axis_index("ctx")
    hd = lax.axis_index("head")
    y = div(ctx, zn * xn)
    z = mod(div(ctx, xn), zn)
    x = mod(ctx, xn)
    b = y * xn + x

    def at(y_, z_, x_):
        return ((y_ * zn + z_) * xn + x_, hd)

    def z_plus(d):
        return mod(z + d, zn)

    ring = sorted(range(1, zn), key=lambda d: -min(d, zn - d))

    def z_dev(d):
        return at(y, z_plus(d), x)

    others = [(dy, dx) for dy in range(yn) for dx in range(xn) if dy or dx]
    steps = [(0, 0)] + sorted(others, key=lambda st: (-min(st[0], yn - st[0]) - st[1], -st[1], st[0]))

    def plus(i):
        dy, dx = steps[i]
        return mod(y + dy, yn), mod(x + dx, xn)

    def minus(i):
        dy, dx = steps[i]
        return mod(y + yn - dy, yn), mod(x + xn - dx, xn)

    def plus_dev(i):
        py, px = plus(i)
        return at(py, z, px)

    def minus_dev(i):
        py, px = minus(i)
        return at(py, z, px)

    def rcopy(src, dst, ssem, rsem, dev):
        return pltpu.make_async_remote_copy(
            src_ref=src, dst_ref=dst, send_sem=ssem, recv_sem=rsem, device_id=dev, device_id_type=MESH
        )

    def loop(first, last, body):
        def step(n, carry):
            body(n)
            return carry

        lax.fori_loop(first, last, step, 0)

    q_load = pltpu.make_async_copy(q_hbm, q_ref, loc_sem.at[0])
    q_load.start()
    barrier = pltpu.get_barrier_semaphore()
    partners = (
        [z_dev(d) for d in range(1, zn)]
        + [plus_dev(i) for i in range(1, nb)]
        + [(ctx, mod(hd + e, heads)) for e in range(1, heads)]
    )
    for dev in partners:
        pl.semaphore_signal(barrier, inc=1, device_id=dev, device_id_type=MESH)

    cot_load = pltpu.make_async_copy(cot_hbm, cot_ref, loc_sem.at[1])
    k_load = pltpu.make_async_copy(k_hbm, kbuf, loc_sem.at[2])
    own_ad = pl.ds(pl.multiple_of((z * xn + x) * cpd, cpd), cpd)
    ad_load = pltpu.make_async_copy(ad_hbm, adp.at[own_ad], loc_sem.at[3])
    late_loads = [
        pltpu.make_async_copy(gain_hbm, gain_ref, loc_sem.at[4]),
        pltpu.make_async_copy(src_hbm, src_ref, loc_sem.at[5]),
    ]
    for k in range(kvl):
        late_loads.append(
            pltpu.make_async_copy(
                v_hbm.at[:, k * HD : (k + 1) * HD], vaug.at[k, :, 0:HD], loc_sem.at[6 + k]
            )
        )
    for load in [cot_load, k_load, ad_load] + late_loads:
        load.start()

    q_load.wait()
    qf = q_ref[...].astype(F32)
    for k in range(kvl):
        qall[k, 0, pl.ds(z, 1)] = jnp.concatenate(
            [qf[:, (k * GROUP + h) * HD : (k * GROUP + h + 1) * HD] for h in range(GROUP)], axis=0
        ).astype(BF16)[None]
    cot_load.wait()
    cf = cot_ref[...].astype(F32)
    cz[pl.ds(z, 1)] = jnp.concatenate(
        [cf[:, g * LANES : (g + 1) * LANES] for g in range(groups)], axis=0
    ).astype(BF16)[None]
    pl.semaphore_wait(barrier, len(partners))

    def z_group(make):
        copies = {d: make(d) for d in ring}
        for copy in copies.values():
            copy.start()
        return copies

    def received(copies):
        for copy in copies.values():
            copy.wait_recv()

    def sent(*groups_of_copies):
        for copies in groups_of_copies:
            for copy in copies.values():
                copy.wait_send()

    zq = z_group(lambda d: rcopy(qall.at[:, 0, z], qall.at[:, 0, z], zq_s.at[d], zq_r.at[d], z_dev(d)))
    zc = z_group(lambda d: rcopy(cz.at[z], cz.at[z], zc_s.at[d], zc_r.at[d], z_dev(d)))

    k_load.wait()

    def turn_keys(c):
        lines = pl.ds(pl.multiple_of(c * LANES, LANES), LANES)
        for k in range(kvl):
            k_t[k, :, lines] = kbuf[lines, k * HD : (k + 1) * HD].astype(F32).T.astype(BF16)

    loop(0, kbuf.shape[0] // LANES, turn_keys)
    for k in range(kvl):
        vaug[k, :, HD : 2 * HD] = jnp.ones((vaug.shape[1], HD), BF16)

    def q_copy(k, i):
        return rcopy(qall.at[k, 0], qall.at[k, i], q2_s.at[k * nb + i], q2_r.at[k * nb + i], plus_dev(i))

    received(zq)
    for k in range(kvl):
        for i in range(1, nb):
            q_copy(k, i).start()

    for d in range(zn):
        for e in range(1, xn):
            other = pl.multiple_of((d * xn + mod(x + e, xn)) * cpd, cpd)
            adp[pl.ds(other, cpd), :] = jnp.zeros((cpd, nh * HD), BF16)
    st1s[...] = jnp.zeros_like(st1s)
    ad_load.wait()
    za = z_group(lambda d: rcopy(adp.at[own_ad], adp.at[own_ad], za_s.at[d], za_r.at[d], z_dev(d)))
    for load in late_loads:
        load.wait()

    factor = (HD ** -0.5) * LOG2E
    qrows = zn * kr
    eye = iota((qrows, LANES), 0) == iota((qrows, LANES), 1)

    def stat_tile(row):
        high, middle, low = split3(row)
        line = iota((kr, LANES), 0)
        tile = jnp.where(line == 0, high.astype(F32), jnp.where(line == 1, middle.astype(F32), low.astype(F32)))
        return jnp.where(line < 3, tile, 0.0).astype(BF16)

    def stat_row(tile):
        wide = tile.astype(F32)
        return wide[0:1, :] + wide[1:2, :] + wide[2:3, :]

    def score(k, i, count, buf):
        q = qall[k, i : i + count].reshape(count * qrows, HD)
        buf[0 : count * qrows, :] = nn(q, k_t[k])

    def weigh(k, i, count, buf):
        s = buf[0 : count * qrows, :]
        m = jnp.max(s, axis=1, keepdims=True)
        p = jnp.exp2((buf[0 : count * qrows, :] - m) * factor).astype(BF16)
        oa = nn(p, vaug[k])
        total = oa[:, HD : 2 * HD]
        o = (oa[:, 0:HD] / total).astype(BF16)
        lse = m * factor + jnp.log2(total)
        for c in range(count):
            part = slice(c * qrows, (c + 1) * qrows)
            osend[k * nb + i + c, 0:zn] = o[part].reshape(zn, kr, HD)
            row = jnp.sum(jnp.where(eye, lse[part], 0.0), axis=0, keepdims=True)
            osend[k * nb + i + c, zn] = stat_tile(row)
            if i + c > 0:
                o_copy(k * nb + i + c, i + c).start()

    def o_copy(j, i):
        return rcopy(osend.at[j], orecv.at[j], o_s.at[j], o_r.at[j], minus_dev(i))

    units = [(1, nb // 2 - 1), (nb // 2, nb // 2)]

    def queries_here(k, i, count):
        for c in range(count):
            q_copy(k, i + c).wait_recv()

    def attend(k, carry):
        for n, (i, count) in enumerate(units):
            here, there = sbuf[n % 2], sbuf[(n + 1) % 2]
            if n + 1 < len(units):
                queries_here(k, *units[n + 1])
                score(k, *units[n + 1], there)
                weigh(k, i, count, here)
            else:

                later = jnp.minimum(k + 1, kvl - 1)

                @pl.when(k + 1 < kvl)
                def _():
                    queries_here(later, *units[0])

                score(later, *units[0], there)
                weigh(k, i, count, here)
        return carry

    def z_copies(k):
        return {
            d: rcopy(zsend.at[k, z_plus(d)], zrecv.at[k, d], zr_s.at[k * zn + d], zr_r.at[k * zn + d], z_dev(d))
            for d in ring
        }

    def combine(k):
        for i in range(1, nb):
            o_copy(k * nb + i, i).wait_recv()
        parts = [(osend if i == 0 else orecv).at[k * nb + i] for i in range(nb)]
        stats = [stat_row(part[zn]) for part in parts]
        top = functools.reduce(jnp.maximum, stats)
        weights = [jnp.exp2(st - top) for st in stats]
        weight_sum = functools.reduce(jnp.add, weights)
        inverse = 1.0 / weight_sum
        acc = jnp.zeros((qrows, HD), F32)
        for i in range(nb):
            share = jnp.where(eye, weights[i] * inverse, 0.0)[:, 0:qrows].astype(BF16)
            acc = acc + nn(share, parts[i][0:zn].reshape(qrows, HD))
        zsend[k, :, 0:kr, :] = acc.astype(BF16).reshape(zn, kr, HD)
        tile = stat_tile(top + jnp.log2(weight_sum))
        for d in range(zn):
            zsend[k, d, kr : 2 * kr, :] = tile
        for copy in z_copies(k).values():
            copy.start()

    mine = iota((kr, LANES), 1) == iota((kr, LANES), 0) + z * kr

    def settle(k, copies):
        received(copies)
        parts = [zsend[k, z]] + [zrecv[k, d] for d in range(1, zn)]
        stats = [stat_row(part[kr : 2 * kr, :]) for part in parts]
        top = functools.reduce(jnp.maximum, stats)
        weights = [jnp.exp2(st - top) for st in stats]
        inverse = 1.0 / functools.reduce(jnp.add, weights)
        acc = jnp.zeros((kr, HD), F32)
        for d in range(zn):
            column = jnp.sum(jnp.where(mine, weights[d] * inverse, 0.0), axis=1, keepdims=True)
            acc = acc + column * parts[d][0:kr, :].astype(F32)
        hz[k, pl.ds(z, 1)] = acc.astype(BF16)[None]
        return z_group(
            lambda d: rcopy(hz.at[k, z], hz.at[k, z], hz_s.at[k * zn + d], hz_r.at[k * zn + d], z_dev(d))
        )

    def spread(k, copies):
        received(copies)
        pieces = nn(regroup_h[...], hz[k].reshape(zn * kr, HD)).astype(BF16)
        for h in range(GROUP):
            hall[k, pl.ds(b, 1), :, h * HD : (h + 1) * HD] = pieces[h * tb : (h + 1) * tb, :][None]
        copies = {
            i: rcopy(hall.at[k, b], hall.at[k, b], h2_s.at[k * nb + i], h2_r.at[k * nb + i], plus_dev(i))
            for i in range(1, nb)
        }
        for copy in copies.values():
            copy.start()
        return copies

    def project(k, copies):
        gain = gain_ref[...].astype(F32)
        for i in (0, *range(nb - 1, 0, -1)):
            if i > 0:
                copies[i].wait_recv()
            my, mx = minus(i)
            there = my * xn + mx
            hidden = hall[k, there].astype(F32)
            lines = pl.ds(pl.multiple_of(there * tb, tb), tb)
            partial = jnp.zeros((tb, HD), F32)
            for h in range(GROUP):
                piece = hidden[:, h * HD : (h + 1) * HD]
                partial = partial + piece * piece
                head = k * GROUP + h
                gall[lines, head * HD : (head + 1) * HD] = (piece * gain[head : head + 1, :]).astype(BF16)
            squares[lines, :] = partial if k == 0 else squares[lines, :] + partial
        width = GROUP * HD
        part = nn(gall[:, k * width : (k + 1) * width], ad_t[k * width : (k + 1) * width, :])
        mpre[...] = part if k == 0 else mpre[...] + part

    def turn_adapter(k):
        def turn(h):
            lanes = pl.ds(pl.multiple_of(h * HD, HD), HD)
            for first in range(0, aw, LANES):
                ad_t[lanes, first : first + LANES] = adp[first : first + LANES, lanes].astype(F32).T.astype(BF16)

        loop(k * GROUP, (k + 1) * GROUP, turn)

    def attend_own(k):
        score(k, 0, 1, sbuf[0])
        weigh(k, 0, 1, sbuf[0])

    loop(0, kvl, attend_own)
    queries_here(0, *units[0])
    score(0, *units[0], sbuf[0])
    lax.fori_loop(0, kvl, attend, 0)

    regroup_h[...] = regroup(GROUP, zn)
    received(zc)
    pieces = nn(regroup(groups, zn), cz[...].reshape(zn * groups * 2, LANES))
    cg[...] = pieces.astype(BF16).reshape(groups, tb, LANES)
    my_group = div(ctx, per_group)
    c2 = {}
    for i in range(1, nb):
        py, px = plus(i)
        there = div((py * zn + z) * xn + px, per_group)
        c2[i] = rcopy(cg.at[there], call.at[b], c2_s.at[i], c2_r.at[i], at(py, z, px))
        c2[i].start()
    call[pl.ds(b, 1)] = cg[pl.ds(my_group, 1)]

    combine(0)
    combine(1)
    sent(zq, zc)
    h0 = settle(0, z_copies(0))
    received(za)
    turn_adapter(0)

    sel = iota((rows, rows), 1) == row_of(iota((rows, 1), 0), sizes)
    wanted = jnp.sum(
        jnp.where(sel, jnp.broadcast_to(src_ref[...].astype(F32), (rows, rows)), 0.0),
        axis=1, keepdims=True,
    )
    pick = (wanted == row_of(iota((1, rows), 1), sizes).astype(F32)).astype(F32)
    received(c2)
    cot_rows = nn(pick.T.astype(BF16), call[...].reshape(rows, LANES))
    cot_t[...] = cot_rows.T
    token = iota((nb * 2, 1), 0)
    block = div(token, 2)
    token = 2 * ((div(block, xn) * zn + z) * xn + mod(block, xn)) + mod(token, 2)
    wanted = jnp.sum(
        jnp.where(iota((nb * 2, rows), 1) == token, src_ref[...].astype(F32), 0.0), axis=1, keepdims=True
    )
    pick = (wanted == row_of(iota((1, rows), 1), sizes).astype(F32)).astype(F32)

    h1 = settle(1, z_copies(1))
    g0 = spread(0, h0)
    turn_adapter(1)
    sent(za, z_copies(0), z_copies(1), c2)
    for j in range(kvl * nb):
        if j % nb:
            q_copy(j // nb, j % nb).wait_send()
            o_copy(j, j % nb).wait_send()
    g1 = spread(1, h1)
    project(0, g0)
    sent(h0, h1, g0)
    project(1, g1)

    for first in range(0, aw, LANES):
        mpre_t[first : first + LANES, :] = mpre[:, first : first + LANES].T
    hx[pl.ds(hd, 1), 0:cpd, 0:rows] = mpre_t[own_ad, :][None]
    power = jnp.sum(squares[...].T, axis=0, keepdims=True)
    hx[pl.ds(hd, 1), cpd : cpd + 8, 0:rows] = jnp.broadcast_to(power, (8, rows))[None]
    one_hot = pick.astype(BF16)
    chosen = functools.reduce(jnp.add, [nn(one_hot, term) for term in split3(mpre[...])])
    base = cpd + 8
    for j in range(aw // LANES):
        hx[pl.ds(hd, 1), base + j * 2 * nb : base + (j + 1) * 2 * nb, :] = chosen[
            :, j * LANES : (j + 1) * LANES
        ][None]
    hxc = {}
    for e in range(1, heads):
        hxc[e] = rcopy(hx.at[hd], hx.at[hd], hx_s.at[e], hx_r.at[e], (ctx, mod(hd + e, heads)))
        hxc[e].start()
    sent(g1)
    received(hxc)
    summed = hx[0]
    for e in range(1, heads):
        summed = summed + hx[e]
    scale = lax.rsqrt(summed[cpd : cpd + 1, 0:rows] / eps_div + 1e-05)

    token_scale = jnp.sum(pick * scale, axis=1, keepdims=True)
    for j in range(aw // LANES):
        pre = token_scale * summed[base + j * 2 * nb : base + (j + 1) * 2 * nb, :]
        out = pre / (1.0 + jnp.exp(-pre))
        for d in range(nb):
            st1s[d, 0:2, j * LANES : (j + 1) * LANES] = out[2 * d : 2 * d + 2, :]
    s1 = {}
    for i in range(1, nb):
        py, px = plus(i)
        s1[i] = rcopy(st1s.at[py * xn + px], st1r.at[b], s1_s.at[i], s1_r.at[i], at(py, z, px))
        s1[i].start()
    st1r[pl.ds(b, 1)] = st1s[pl.ds(b, 1)]
    sent(hxc)

    pre = scale * summed[0:cpd, 0:rows]
    sig = 1.0 / (1.0 + jnp.exp(-pre))
    own = pl.multiple_of(mod(ctx, per_group) * cpd, cpd)
    slope = (cot_t[pl.ds(own, cpd), :] * sig * (1.0 + pre * (1.0 - sig)) * scale).astype(BF16)
    grad_ref[...] = nn(slope, gall[...]) * (rows ** -0.5)

    sent(s1)
    received(s1)
    for py in range(yn):
        tile = st1r[py * xn]
        for px in range(1, xn):
            tile = tile + st1r[py * xn + px]
        stu_ref[:, py * aw : (py + 1) * aw] = tile[0:2, :]


def local(sizes, heads, queries, keys, values, norm_gain, adapter, source_row, cotangent):
    yn, zn, xn = sizes
    nb = yn * xn
    tb = 2 * zn
    rows = nb * tb
    positions, kvw = keys.shape
    kvl = kvw // HD
    nh = kvl * GROUP
    nf = nh * HD
    kr = GROUP * 2
    cpd = adapter.shape[0]
    aw = zn * xn * cpd
    groups = cotangent.shape[1] // LANES
    vm = pltpu.VMEM
    dma = pltpu.SemaphoreType.DMA
    scratch = [
        vm(queries.shape, BF16),
        vm((nh, HD), BF16),
        vm((1, rows), jnp.int32),
        vm(cotangent.shape, BF16),
        vm((positions, kvw), BF16),
        vm((kvl, HD, positions), BF16),
        vm((kvl, positions, 2 * HD), BF16),
        vm((kvl, nb, zn, kr, HD), BF16),
        vm((kvl * nb, zn + 1, kr, HD), BF16),
        vm((kvl * nb, zn + 1, kr, HD), BF16),
        vm((kvl, zn, 2 * kr, HD), BF16),
        vm((kvl, zn, 2 * kr, HD), BF16),
        vm((kvl, zn, kr, HD), BF16),
        vm((kvl, nb, tb, GROUP * HD), BF16),
        vm((rows, nf), BF16),
        vm((rows, aw), F32),
        vm((rows, HD), F32),
        vm((heads, cpd + 8 + 2 * nb * (aw // LANES), max(rows, LANES)), F32),
        vm((nb // 2 * zn * kr, positions), F32),
        vm((nb // 2 * zn * kr, positions), F32),
        vm((zn * kr, zn * kr), BF16),
        vm((zn, groups * 2, LANES), BF16),
        vm((groups, tb, LANES), BF16),
        vm((nb, tb, LANES), BF16),
        vm((LANES, rows), F32),
        vm((aw, rows), F32),
        vm((nb, 8, aw), F32),
        vm((nb, 8, aw), F32),
        vm((aw, nf), BF16),
        vm((nf, aw), BF16),
        dma((6 + kvl,)),
        dma((zn,)), dma((zn,)), dma((kvl * nb,)), dma((kvl * nb,)),
        dma((zn,)), dma((zn,)), dma((nb,)), dma((nb,)),
        dma((kvl * nb,)), dma((kvl * nb,)),
        dma((kvl * zn,)), dma((kvl * zn,)), dma((kvl * zn,)), dma((kvl * zn,)),
        dma((kvl * nb,)), dma((kvl * nb,)),
        dma((heads,)), dma((heads,)),
        dma((nb,)), dma((nb,)), dma((zn,)), dma((zn,)),
    ]
    args = (queries, keys, values, norm_gain.reshape(nh, HD), adapter, source_row.reshape(1, -1), cotangent)
    vmem = pl.BlockSpec(memory_space=pltpu.VMEM)
    hbm = pl.BlockSpec(memory_space=pltpu.HBM)
    return pl.pallas_call(
        functools.partial(kernel, sizes, heads, float(heads * nf)),
        out_shape=(
            pltpu.VMEM(cotangent.shape, F32),
            pltpu.VMEM(adapter.shape, F32),
        ),
        in_specs=[hbm] * 7,
        out_specs=(vmem, vmem),
        scratch_shapes=scratch,
        compiler_params=pltpu.CompilerParams(
            collective_id=0, has_side_effects=True, vmem_limit_bytes=48 * 1024 * 1024
        ),
        cost_estimate=pl.CostEstimate(
            flops=4 * rows * nh * HD * positions,
            bytes_accessed=4 * positions * kvw,
            transcendentals=rows * nh * positions,
        ),
        name="distill",
    )(*(pltpu.with_memory_space_constraint(arg, pltpu.HBM) for arg in args))


def solution(mesh, sizes=(YN, ZN, XN)):
    return jax.shard_map(
        functools.partial(local, sizes, mesh.shape["head"]),
        mesh=mesh,
        in_specs=(
            P("ctx", "head"),
            P("ctx", "head"),
            P("ctx", "head"),
            P("head"),
            P("ctx", "head"),
            P(),
            P("ctx", None),
        ),
        out_specs=(P("ctx", None), P("ctx", "head")),
        check_vma=False,
    )
```
